32 devices in a mesh: phase: 4 (over x, core), dp: 8 (over z, y).
Axes of the slice: x: 2, y: 2, z: 4, core: 2. Of those that a mesh axis runs over, the one named last changes fastest.
Arguments:
- features: bfloat16 [2, 131072], P(None, 'dp'), may hold values from -40 to 40
- site_counts: int32 [2, 8], P(None, 'dp'), may hold values from 16 to 256, as said below
- kernel_map_0: int32 [2, 27, 2048], P(None, None, 'dp'), may hold values from -1 to 255, as said below
- kernel_map_1: int32 [2, 27, 1024], P(None, None, 'dp'), may hold values from -1 to 127, as said below
- kernel_map_2: int32 [2, 27, 512], P(None, None, 'dp'), may hold values from -1 to 63, as said below
- kernel_map_3: int32 [2, 27, 256], P(None, None, 'dp'), may hold values from -1 to 31, as said below
- parent_map_0: int32 [2, 2048], P(None, 'dp'), may hold values from -1 to 127, as said below
- parent_map_1: int32 [2, 1024], P(None, 'dp'), may hold values from -1 to 63, as said below
- parent_map_2: int32 [2, 512], P(None, 'dp'), may hold values from -1 to 31, as said below
- depthwise_0: bfloat16 [27, 64], replicated, may hold values from -1.5 to 1.5
- depthwise_1: bfloat16 [27, 128], replicated, may hold values from -1.5 to 1.5
- depthwise_2: bfloat16 [27, 256], replicated, may hold values from -1.5 to 1.5
- depthwise_3: bfloat16 [27, 512], replicated, may hold values from -1.5 to 1.5
- first_weight_0: bfloat16 [64, 64], replicated, may hold values from -0.75 to 0.75
- first_weight_1: bfloat16 [128, 128], replicated, may hold values from -0.5 to 0.5
- first_weight_2: bfloat16 [256, 256], replicated, may hold values from -0.375 to 0.375
- first_weight_3: bfloat16 [512, 512], replicated, may hold values from -0.25 to 0.25
- second_weight_0: bfloat16 [64, 64], replicated, may hold values from -0.75 to 0.75
- second_weight_1: bfloat16 [128, 128], replicated, may hold values from -0.5 to 0.5
- second_weight_2: bfloat16 [256, 256], replicated, may hold values from -0.375 to 0.375
- second_weight_3: bfloat16 [512, 512], replicated, may hold values from -0.25 to 0.25
- coarsen_0: bfloat16 [64, 128], replicated, may hold values from -0.75 to 0.75
- coarsen_1: bfloat16 [128, 256], replicated, may hold values from -0.5 to 0.5
- coarsen_2: bfloat16 [256, 512], replicated, may hold values from -0.375 to 0.375
- refine_0: bfloat16 [128, 64], replicated, may hold values from -0.5 to 0.5
- refine_1: bfloat16 [256, 128], replicated, may hold values from -0.375 to 0.375
- refine_2: bfloat16 [512, 256], replicated, may hold values from -0.25 to 0.25
- cotangent: bfloat16 [4, 2, 131072], P('phase', None, 'dp'), may hold values from -6 to 6
Outputs:
- decoded: bfloat16 [4, 2, 131072], P('phase', None, 'dp')
- weight_grads: float32 [4, 2, 262144], P('phase', None, 'dp')
The draws below stay inside these ranges and needn't reach their ends.
Inputs may be any that keep to these rules, and one draw needn't show every extreme that they name: `site_counts`: live finest-level sites of a replica in a micro-batch; in every micro-batch some replica has all 256 slots live. `kernel_map_0`: row index within the same replica's block, or -1 for no neighbour; live sites come first in each block, a live site's offset 13 names itself, live sites name only live sites, padded rows hold -1. `kernel_map_1`: as for level 0, at level 1. `kernel_map_2`: as for level 0, at level 2. `kernel_map_3`: as for level 0, at level 3. `parent_map_0`: a live level 1 site of the same replica and micro-batch, -1 for padded rows. `parent_map_1`: a live level 2 site of the same replica and micro-batch, -1 for padded rows. `parent_map_2`: a live level 3 site of the same replica and micro-batch, -1 for padded rows.
All inputs are finite; a program needn't handle non-finite values.
Results may differ from the reference program's by a relative error of at most 0.014.
Values may be sent and summed in bfloat16 or wider, within the bound.
A program may use at most 256 MiB of HBM per device.

```python
import math
import jax
import jax.numpy as jnp
from jax import lax

C0 = 64
C1 = 128
C2 = 256
C3 = 512
ROWS = 256
MICRO = 2
TAPS = 27
REPLICAS = 8
ELEMS = 16384
WSQ = 262144


def level_counts(key):
    base = jax.random.fold_in(key, 101)
    result = []
    for layer_index in range(4):
        height = ROWS // 2 ** layer_index
        subkey = jax.random.fold_in(base, layer_index)
        lowest = max(height // 16, 1)
        counts = jax.random.randint(subkey, (MICRO, REPLICAS), lowest, height + 1)
        filled = jax.random.randint(jax.random.fold_in(subkey, 9), (MICRO,), 0, REPLICAS)
        counts = jnp.where(jnp.arange(REPLICAS)[None, :] == filled[:, None], height, counts)
        result.append(counts)
    return jnp.stack(result, axis=2).astype(jnp.int32)


def neighbour_map(key, layer_index):
    counts = level_counts(key)[:, :, layer_index]
    height = ROWS // 2 ** layer_index
    subkey = jax.random.fold_in(key, 200 + layer_index)
    target = jax.random.randint(subkey, (MICRO, TAPS, REPLICAS, height), 0, 2 ** 30) % counts[:, None, :, None]
    present = jax.random.randint(jax.random.fold_in(subkey, 1), (MICRO, TAPS, REPLICAS, height), 0, 2)
    position = jnp.arange(height)[None, None, None, :]
    live = position < counts[:, None, :, None]
    centre = jnp.arange(TAPS)[None, :, None, None] == 13
    index = jnp.where(centre, position, target)
    index = jnp.where(live & (centre | (present == 1)), index, -1)
    return index.reshape(MICRO, TAPS, REPLICAS * height).astype(jnp.int32)


def parent_map(key, layer_index):
    every = level_counts(key)
    counts = every[:, :, layer_index]
    coarse = every[:, :, layer_index + 1]
    height = ROWS // 2 ** layer_index
    subkey = jax.random.fold_in(key, 300 + layer_index)
    target = jax.random.randint(subkey, (MICRO, REPLICAS, height), 0, 2 ** 30) % coarse[:, :, None]
    live = jnp.arange(height)[None, None, :] < counts[:, :, None]
    return jnp.where(live, target, -1).reshape(MICRO, REPLICAS * height).astype(jnp.int32)


def draw_site_counts(key, part):
    return level_counts(key)[:, :, 0]


def draw_kernel_map_0(key, part):
    return neighbour_map(key, 0)


def draw_kernel_map_1(key, part):
    return neighbour_map(key, 1)


def draw_kernel_map_2(key, part):
    return neighbour_map(key, 2)


def draw_kernel_map_3(key, part):
    return neighbour_map(key, 3)


def draw_parent_map_0(key, part):
    return parent_map(key, 0)


def draw_parent_map_1(key, part):
    return parent_map(key, 1)


def draw_parent_map_2(key, part):
    return parent_map(key, 2)


def draw_features(key, part):
    first_key = jax.random.fold_in(key, 401)
    second_key = jax.random.fold_in(key, 402)
    third_key = jax.random.fold_in(key, 403)
    shape = (MICRO, REPLICAS, ROWS, C0)
    values = jnp.clip(jax.random.normal(first_key, shape, jnp.float32), -4.0, 4.0)
    row_scale = jnp.exp(jax.random.uniform(second_key, (MICRO, REPLICAS, ROWS, 1), jnp.float32, -1.15, 1.15))
    column_scale = jnp.exp(jax.random.uniform(third_key, (1, 1, 1, C0), jnp.float32, -1.15, 1.15))
    return (values * row_scale * column_scale).reshape(MICRO, REPLICAS * ROWS * C0).astype(jnp.bfloat16)


def block_scale(key, dims, cuts, low, high):
    def one(dim, shards_of):
        draws = jax.random.uniform(jax.random.fold_in(jax.random.fold_in(key, 6), dim), (shards_of,), jnp.float32, low / len(cuts), high / len(cuts))
        return jnp.repeat(jnp.exp(draws), dims[dim] // shards_of).reshape((-1,) + (1,) * (len(dims) - dim - 1))

    loudness = one(*cuts[0])
    for cut in cuts[1:]:
        loudness = loudness * one(*cut)
    return loudness


def bell_draw(own_key, shape, spread, limit, cuts=(), kind=jnp.bfloat16):
    factor_of = block_scale(own_key, shape, cuts, -0.22, 0.18) if cuts else 1.0
    drawn = jax.random.normal(own_key, shape, jnp.float32) * spread * factor_of
    return jnp.minimum(jnp.maximum(drawn, -limit), limit).astype(kind)


def setup_inputs(seed: int = 0) -> dict:
    keys = jax.random.split(jax.random.key(seed), 29)
    return {
        "features": draw_features(jax.random.fold_in(keys[28], 71), 0),
        "site_counts": draw_site_counts(jax.random.fold_in(keys[28], 71), 0),
        "kernel_map_0": draw_kernel_map_0(jax.random.fold_in(keys[28], 71), 0),
        "kernel_map_1": draw_kernel_map_1(jax.random.fold_in(keys[28], 71), 0),
        "kernel_map_2": draw_kernel_map_2(jax.random.fold_in(keys[28], 71), 0),
        "kernel_map_3": draw_kernel_map_3(jax.random.fold_in(keys[28], 71), 0),
        "parent_map_0": draw_parent_map_0(jax.random.fold_in(keys[28], 71), 0),
        "parent_map_1": draw_parent_map_1(jax.random.fold_in(keys[28], 71), 0),
        "parent_map_2": draw_parent_map_2(jax.random.fold_in(keys[28], 71), 0),
        "depthwise_0": bell_draw(keys[9], (TAPS, C0), 0.25, 1.5),
        "depthwise_1": bell_draw(keys[10], (TAPS, C1), 0.25, 1.5),
        "depthwise_2": bell_draw(keys[11], (TAPS, C2), 0.25, 1.5),
        "depthwise_3": bell_draw(keys[12], (TAPS, C3), 0.25, 1.5),
        "first_weight_0": bell_draw(keys[13], (C0, C0), C0 ** -0.5, 0.75),
        "first_weight_1": bell_draw(keys[14], (C1, C1), C1 ** -0.5, 0.5),
        "first_weight_2": bell_draw(keys[15], (C2, C2), C2 ** -0.5, 0.375),
        "first_weight_3": bell_draw(keys[16], (C3, C3), C3 ** -0.5, 0.25),
        "second_weight_0": bell_draw(keys[17], (C0, C0), C0 ** -0.5, 0.75),
        "second_weight_1": bell_draw(keys[18], (C1, C1), C1 ** -0.5, 0.5),
        "second_weight_2": bell_draw(keys[19], (C2, C2), C2 ** -0.5, 0.375),
        "second_weight_3": bell_draw(keys[20], (C3, C3), C3 ** -0.5, 0.25),
        "coarsen_0": bell_draw(keys[21], (C0, C1), C0 ** -0.5, 0.75),
        "coarsen_1": bell_draw(keys[22], (C1, C2), C1 ** -0.5, 0.5),
        "coarsen_2": bell_draw(keys[23], (C2, C3), C2 ** -0.5, 0.375),
        "refine_0": bell_draw(keys[24], (C1, C0), C1 ** -0.5, 0.5),
        "refine_1": bell_draw(keys[25], (C2, C1), C2 ** -0.5, 0.375),
        "refine_2": bell_draw(keys[26], (C3, C2), C3 ** -0.5, 0.25),
        "cotangent": bell_draw(keys[27], (4, MICRO, REPLICAS * ELEMS), 1.0, 6.0, ((0, 4), (2, 8))),
    }


def gathered_mix(block, taps, kernel):
    rows = block.shape[0]
    padded = jnp.concatenate([block, jnp.zeros((1, block.shape[1]), block.dtype)], axis=0)
    index = jnp.where(kernel < 0, rows, kernel).astype(jnp.int32)
    gathered = jnp.take(padded, index, axis=0)
    return jnp.einsum('krc,kc->rc', gathered.astype(jnp.float32), taps.astype(jnp.float32))

def level_forward(block, taps, first, second, kernel, target):
    mixed = gathered_mix(block, taps, kernel)
    normed = (mixed * lax.rsqrt(lax.optimization_barrier(jnp.mean(mixed * mixed, axis=1, keepdims=True)) + 1e-05)).astype(jnp.bfloat16)
    inner = jnp.dot(normed, first, preferred_element_type=jnp.float32)
    active = jax.nn.gelu(inner).astype(jnp.bfloat16)
    update = jnp.dot(active, second, preferred_element_type=jnp.float32)
    encoded = (block.astype(jnp.float32) + update).astype(jnp.bfloat16)
    backward = jnp.dot(target, second.T, preferred_element_type=jnp.float32)
    slope = jax.vjp(jax.nn.gelu, inner)[1](backward)[0].astype(jnp.bfloat16)
    grad_first = jnp.dot(normed.T, slope, preferred_element_type=jnp.float32)
    grad_second = jnp.dot(active.T, target, preferred_element_type=jnp.float32)
    return (encoded, grad_first, grad_second)

def pool_rows(encoded, parent, coarse_rows):
    index = jnp.where(parent < 0, coarse_rows, parent).astype(jnp.int32)
    sums = jax.ops.segment_sum(encoded.astype(jnp.float32), index, num_segments=coarse_rows + 1)[:coarse_rows]
    number = jax.ops.segment_sum((parent >= 0).astype(jnp.float32), index, num_segments=coarse_rows + 1)[:coarse_rows]
    return (sums / jnp.maximum(number, 1.0)[:, None]).astype(jnp.bfloat16)

def unpool_rows(encoded, lifted, parent):
    coarse_rows = lifted.shape[0]
    padded = jnp.concatenate([lifted, jnp.zeros((1, lifted.shape[1]), lifted.dtype)], axis=0)
    index = jnp.where(parent < 0, coarse_rows, parent).astype(jnp.int32)
    return (encoded.astype(jnp.float32) + jnp.take(padded, index, axis=0).astype(jnp.float32)).astype(jnp.bfloat16)

def replica_pass(block, count, kernels, parents, targets, taps, firsts, seconds, coarsens, refines):
    live = jnp.arange(block.shape[0]) < count
    block = jnp.where(live[:, None], block, jnp.zeros_like(block))
    encodes = []
    grads = []
    for layer_index in range(4):
        encoded, grad_first, grad_second = level_forward(block, taps[layer_index], firsts[layer_index], seconds[layer_index], kernels[layer_index], targets[layer_index])
        encodes.append(encoded)
        grads.append((grad_first, grad_second))
        if layer_index < 3:
            pooled = pool_rows(encoded, parents[layer_index], kernels[layer_index + 1].shape[1])
            block = jnp.dot(pooled, coarsens[layer_index], preferred_element_type=jnp.float32).astype(jnp.bfloat16)
    decodes = [None, None, None, encodes[3]]
    for layer_index in (2, 1, 0):
        lifted = jnp.dot(decodes[layer_index + 1], refines[layer_index], preferred_element_type=jnp.float32).astype(jnp.bfloat16)
        decodes[layer_index] = unpool_rows(encodes[layer_index], lifted, parents[layer_index])
    return (decodes, grads)

def reference(features, site_counts, kernel_map_0, kernel_map_1, kernel_map_2, kernel_map_3, parent_map_0, parent_map_1, parent_map_2, depthwise_0, depthwise_1, depthwise_2, depthwise_3, first_weight_0, first_weight_1, first_weight_2, first_weight_3, second_weight_0, second_weight_1, second_weight_2, second_weight_3, coarsen_0, coarsen_1, coarsen_2, refine_0, refine_1, refine_2, cotangent):
    heights = [ROWS // 2 ** layer_index for layer_index in range(4)]
    widths = [C0 * 2 ** layer_index for layer_index in range(4)]
    taps = (depthwise_0, depthwise_1, depthwise_2, depthwise_3)
    firsts = (first_weight_0, first_weight_1, first_weight_2, first_weight_3)
    seconds = (second_weight_0, second_weight_1, second_weight_2, second_weight_3)
    coarsens = (coarsen_0, coarsen_1, coarsen_2)
    refines = (refine_0, refine_1, refine_2)
    kernel_maps = (kernel_map_0, kernel_map_1, kernel_map_2, kernel_map_3)
    parent_maps = (parent_map_0, parent_map_1, parent_map_2)
    feats_rep = features.reshape(MICRO, REPLICAS, ROWS, C0).transpose(1, 0, 2, 3)
    counts_rep = site_counts.T
    kernels_rep = tuple((kernel_maps[layer_index].reshape(MICRO, TAPS, REPLICAS, heights[layer_index]).transpose(2, 0, 1, 3) for layer_index in range(4)))
    parents_rep = tuple((parent_maps[layer_index].reshape(MICRO, REPLICAS, heights[layer_index]).transpose(1, 0, 2) for layer_index in range(3)))
    targets_rep = tuple((cotangent[layer_index].reshape(MICRO, REPLICAS, heights[layer_index], widths[layer_index]).transpose(1, 0, 2, 3) for layer_index in range(4)))

    def one_replica(carry, slices):
        feats_one, counts_one, kernels_one, parents_one, targets_one = slices
        carry = list(carry)
        outputs = [[], [], [], []]
        for micro_index in range(MICRO):
            decodes, grads = replica_pass(feats_one[micro_index], counts_one[micro_index], [kernel[micro_index] for kernel in kernels_one], [parent[micro_index] for parent in parents_one], [target[micro_index] for target in targets_one], taps, firsts, seconds, coarsens, refines)
            for layer_index in range(4):
                carry[2 * layer_index] = carry[2 * layer_index] + grads[layer_index][0]
                carry[2 * layer_index + 1] = carry[2 * layer_index + 1] + grads[layer_index][1]
                outputs[layer_index].append(decodes[layer_index].reshape(-1))
        return (tuple(carry), tuple((jnp.stack(outputs[layer_index]) for layer_index in range(4))))
    initial = []
    for layer_index in range(4):
        initial.append(jnp.zeros((widths[layer_index], widths[layer_index]), jnp.float32))
        initial.append(jnp.zeros((widths[layer_index], widths[layer_index]), jnp.float32))
    totals, levels = lax.scan(one_replica, tuple(initial), (feats_rep, counts_rep, kernels_rep, parents_rep, targets_rep))
    decoded = jnp.stack([levels[layer_index].transpose(1, 0, 2).reshape(MICRO, REPLICAS * ELEMS) for layer_index in range(4)])
    stacked = []
    for layer_index in range(4):
        factor = 1.0 / math.sqrt(MICRO * REPLICAS * heights[layer_index])
        spare = WSQ - widths[layer_index] * widths[layer_index]
        pair = [jnp.pad(totals[2 * layer_index + which].reshape(-1) * factor, (0, spare)) for which in range(2)]
        stacked.append(jnp.stack(pair))
    return (decoded, jnp.stack(stacked))
```

```python
import functools
import math

import jax
import jax.numpy as jnp
from jax import lax
from jax.experimental import pallas as pl
from jax.experimental.pallas import tpu as pltpu
from jax.sharding import PartitionSpec as P

LANES = 128
TAPS = 27
IDX_ROWS = 32
BATCH = 9
F32 = jnp.float32
BF16 = jnp.bfloat16
MESH = pl.DeviceIdType.MESH
GELU_A = math.sqrt(2.0 / math.pi)
GELU_B = 0.044715


def dot(a, b):
    return lax.dot_general(a, b, (((1,), (0,)), ((), ())), preferred_element_type=F32)


def dot_nt(a, b):
    return lax.dot_general(a, b, (((1,), (1,)), ((), ())), preferred_element_type=F32)


def dot_tn(a, b):
    return lax.dot_general(a, b, (((0,), (0,)), ((), ())), preferred_element_type=F32)


def one_hot(column, width):
    lanes = lax.broadcasted_iota(jnp.int32, (column.shape[0], width), 1).astype(F32)
    return jnp.where(column == lanes, 1.0, 0.0).astype(BF16)


def pool_matrix(parent_row, coarse):
    rows = lax.broadcasted_iota(jnp.int32, (coarse, parent_row.shape[1]), 0)
    return jnp.where(rows == parent_row, 1.0, 0.0).astype(F32)


def kernel(replicas, heights, widths, micro, count, *refs):
    sources, (dec_out, grad_out) = refs[:count], refs[count : count + 2]
    held, refs = refs[count + 2 : 2 * count + 2], refs[2 * count + 2 :]
    (
        load_sem,
        pack_f,
        pack_c,
        pack_d,
        pack_g,
        small,
        idx_raw,
        idx,
        idx_t,
        part0,
        part1,
        part2,
        got0,
        got1,
        got2,
        near0,
        near1,
        near2,
        sum0,
        sum1,
        sum2,
        cot_all,
        slope_all,
        cols_send,
        cols_all,
        send_part,
        recv_part,
        send_cot,
        recv_cot,
        send_slope,
        recv_slope,
        send_cols,
        recv_cols,
        send_near,
        recv_near,
    ) = refs
    nears, sums_of = (near0, near1, near2), (sum0, sum1, sum2)
    features, counts, cot = held[0], held[1], held[27]
    kms, pms, dws = held[2:6], held[6:9], held[9:13]
    fws, sws = held[13:17], held[17:21]
    cos, res = held[21:24], held[24:27]
    parts, gots = (part0, part1, part2), (got0, got1, got2)
    phase = lax.axis_index("phase")
    me = lax.axis_index("dp")
    chunks = features.shape[1] // LANES

    def peer(offset):
        return {"phase": phase, "dp": lax.rem(me + offset, replicas)}

    def load(i):
        return pltpu.make_async_copy(sources[i], held[i], load_sem.at[i])

    order = [0, 27, 2, 3, 4, 5, 6, 7, 8, 1, 9, 13, 17, 21, 10, 14, 18, 22, 11, 15, 19, 23, 12, 16, 20]
    for i in order + [26, 25, 24]:
        load(i).start()

    barrier = pltpu.get_barrier_semaphore()

    @pl.loop(1, replicas)
    def _(offset):
        pl.semaphore_signal(barrier, inc=1, device_id=peer(offset), device_id_type=MESH)

    for i in (0, 27):
        load(i).wait()

    for j in range(chunks):
        lanes = slice(j * LANES, (j + 1) * LANES)
        pack_f[2 * j : 2 * j + 2, :] = features[:, lanes].astype(F32)
        pack_c[2 * j : 2 * j + 2, :] = cot[0, :, lanes].astype(F32)

    def unpack(pack, layer, m):
        rows, width = heights[layer], widths[layer]
        if width < LANES:
            both = pack[pl.ds(m, rows // 2, stride=2), :]
            small[pl.ds(0, rows // 2, stride=2), :] = both[:, :width]
            small[pl.ds(1, rows // 2, stride=2), :] = both[:, width:]
            return small[...]
        split = width // LANES
        return jnp.concatenate(
            [pack[pl.ds(2 * h + m, rows, stride=2 * split), :] for h in range(split)], axis=1
        )

    def target(layer):
        return jnp.concatenate([unpack(pack_c, layer, m) for m in range(micro)], axis=0).astype(BF16)

    top = 3

    pl.semaphore_wait(barrier, replicas - 1)

    def all_send(source, gathered, send_sem, recv_sem, indexed):
        def copy(offset):
            to = peer(offset)
            return pltpu.make_async_remote_copy(
                src_ref=source.at[to["dp"]] if indexed else source.at[0],
                dst_ref=gathered.at[offset],
                send_sem=send_sem.at[offset],
                recv_sem=recv_sem.at[offset],
                device_id=to,
                device_id_type=MESH,
            )

        return copy

    copy_cot = all_send(cot_all, cot_all, send_cot, recv_cot, False)
    copy_slope = all_send(slope_all, slope_all, send_slope, recv_slope, False)
    copy_cols = all_send(cols_send, cols_all, send_cols, recv_cols, True)

    def start_all(copy):
        @pl.loop(1, replicas)
        def _(offset):
            copy(offset).start()

    def wait_all(copy):
        @pl.loop(1, replicas)
        def _(offset):
            copy(offset).wait()

    def group_of(layer):
        owners = parts[layer].shape[0]
        return owners, lax.div(me, owners), lax.rem(me, owners)

    def near_copy(layer, w, sender):
        owners, group, _ = group_of(layer)
        return pltpu.make_async_remote_copy(
            src_ref=parts[layer].at[w],
            dst_ref=nears[layer].at[sender],
            send_sem=send_near.at[w],
            recv_sem=recv_near.at[sender],
            device_id={"phase": phase, "dp": group * owners + w},
            device_id_type=MESH,
        )

    def far_copy(layer, group):
        return pltpu.make_async_remote_copy(
            src_ref=sums_of[layer].at[0],
            dst_ref=gots[layer].at[group],
            send_sem=send_part.at[0],
            recv_sem=recv_part.at[group],
            device_id={"phase": phase, "dp": group_of(layer)[2]},
            device_id_type=MESH,
        )

    @pl.when(phase == top)
    def _():
        cot_all[0] = target(top)
        start_all(copy_cot)

    for i in (2, 3, 4, 5, 6, 7, 8, 1):
        load(i).wait()
    idx[...] = jnp.full(idx.shape, -1.0, F32)
    base = []
    position = 0
    for layer in range(4):
        rows = heights[layer]
        base.append(position)
        pieces = [(at, min(LANES, rows - at)) for at in range(0, rows, LANES)]
        for k in range(TAPS):
            for piece, (at, span) in enumerate(pieces):
                idx_raw[piece, 2 * k : 2 * k + 2, 0:span] = kms[layer][k, :, at : at + span].astype(F32)
        for m in range(micro):
            at = position + m * rows
            values = jnp.concatenate(
                [
                    idx_raw.at[piece][pl.ds(m, TAPS, stride=2), :][:, :span]
                    for piece, (_, span) in enumerate(pieces)
                ],
                axis=1,
            )
            shift = m * rows if layer >= 2 else 0
            if shift:
                values = jnp.where(values < 0.0, values, values + float(shift))
            idx[0:TAPS, at : at + rows] = values
            if layer < 3:
                idx[TAPS : TAPS + 1, at : at + rows] = pms[layer][m : m + 1, :].astype(F32)
        position += micro * rows
    for j in range(idx.shape[1] // LANES):
        lanes = slice(j * LANES, (j + 1) * LANES)
        idx_t[lanes, :] = idx[:, lanes].T

    live = []
    for m in range(micro):
        block = unpack(pack_f, 0, m)
        site = lax.broadcasted_iota(jnp.int32, block.shape, 0)
        live.append(jnp.where(site < counts[:, m : m + 1], block, 0.0))
    x = jnp.concatenate(live, axis=0).astype(BF16)

    encodes = []
    for layer in range(4):
        for i in (9 + layer, 13 + layer, 17 + layer) + ((21 + layer,) if layer < 3 else ()):
            load(i).wait()
        rows, width = heights[layer], widths[layer]
        group = rows if layer < 2 else micro * rows
        mixes = []
        for start in range(0, micro * rows, group):
            block = x[start : start + group]
            index = idx_t[base[layer] + start : base[layer] + start + group, :]
            mixed = jnp.zeros((group, width), F32)
            for first in range(0, TAPS, BATCH):
                hots = [one_hot(index[:, k : k + 1], group) for k in range(first, first + BATCH)]
                gathered = dot(jnp.concatenate(hots, axis=0), block)
                for k in range(BATCH):
                    tap = dws[layer][first + k : first + k + 1, :].astype(F32)
                    mixed = mixed + gathered[k * group : (k + 1) * group] * tap
            mixes.append(mixed)
        mixed = mixes[0] if len(mixes) == 1 else jnp.concatenate(mixes, axis=0)
        normed_f = mixed * lax.rsqrt(jnp.mean(mixed * mixed, axis=1, keepdims=True) + 1e-05)
        normed = normed_f.astype(BF16)
        inner = dot(normed, fws[layer][...])
        squared = inner * inner
        bend = jnp.tanh(GELU_A * inner * (1.0 + GELU_B * squared))
        active = (0.5 * inner * (1.0 + bend)).astype(BF16)
        encoded = (x.astype(F32) + dot(active, sws[layer][...])).astype(BF16)
        encodes.append(encoded)

        @pl.when(phase == layer)
        def _():
            aim = target(layer) if layer < top else cot_all[0]
            backward = dot_nt(aim, sws[layer][...])
            grad = 0.5 * (1.0 + bend) + 0.5 * inner * (1.0 - bend * bend) * GELU_A * (
                1.0 + 3.0 * GELU_B * squared
            )
            slope = (grad * backward).astype(BF16)
            if layer == top:
                slope_all[0] = slope
                both = jnp.concatenate(
                    [normed.astype(F32).T, active.astype(F32).T], axis=1
                ).astype(cols_send.dtype)
                rows_here = cols_send.shape[1]
                for d in range(replicas):
                    cols_send[d] = both[d * rows_here : (d + 1) * rows_here]
                start_all(copy_slope)
                start_all(copy_cols)
            else:
                part = parts[layer]
                owners, _, rows_here, _ = part.shape
                for i, term in enumerate((dot_tn(normed, slope), dot_tn(active, aim))):
                    for w in range(owners):
                        part[w, i] = term[w * rows_here : (w + 1) * rows_here].astype(part.dtype)
                for w in range(owners):

                    @pl.when(group_of(layer)[2] != w)
                    def _():
                        near_copy(layer, w, group_of(layer)[2]).start()

        if layer < 3:
            coarse = heights[layer + 1]
            pooled = []
            for m in range(micro):
                matrix = pool_matrix(pms[layer][m : m + 1, :], coarse)
                number = jnp.sum(matrix, axis=1, keepdims=True)
                sums = dot(matrix.astype(BF16), encoded[m * rows : (m + 1) * rows])
                pooled.append(sums / jnp.maximum(number, 1.0))
            x = dot(jnp.concatenate(pooled, axis=0).astype(BF16), cos[layer][...]).astype(BF16)

    for layer in range(3):
        part, near = parts[layer], nears[layer]

        @pl.when(phase == layer)
        def _():
            owners, group, member = group_of(layer)
            near[member] = part[member]
            for w in range(owners):

                @pl.when(member != w)
                def _():
                    near_copy(layer, w, member).wait_send()
                    near_copy(layer, w, w).wait_recv()

            for i in range(2):
                term = near[0, i].astype(F32)
                for w in range(1, owners):
                    term = term + near[w, i].astype(F32)
                sums_of[layer][0, i] = term.astype(near.dtype)

            @pl.when(group != 0)
            def _():
                far_copy(layer, group).start()

    decoded = encodes[3]
    for layer in range(3, -1, -1):
        rows, width = heights[layer], widths[layer]
        if layer < 3:
            coarse = heights[layer + 1]
            load(24 + layer).wait()
            mix = dot_nt if layer == 0 else dot
            lifted = mix(decoded, res[layer][...]).astype(BF16)
            ups = []
            for m in range(micro):
                at = base[layer] + m * rows
                matrix = one_hot(idx_t[at : at + rows, TAPS : TAPS + 1], coarse)
                ups.append(dot(matrix, lifted[m * coarse : (m + 1) * coarse]))
            decoded = (encodes[layer].astype(F32) + jnp.concatenate(ups, axis=0)).astype(BF16)

        @pl.when(phase == layer)
        def _():
            wide = decoded.astype(F32)
            for m in range(micro):
                own = wide[m * rows : (m + 1) * rows]
                if width < LANES:
                    small[...] = own
                    pack_d[pl.ds(m, rows // 2, stride=2), :] = jnp.concatenate(
                        [
                            small[pl.ds(0, rows // 2, stride=2), :],
                            small[pl.ds(1, rows // 2, stride=2), :],
                        ],
                        axis=1,
                    )
                else:
                    split = width // LANES
                    for h in range(split):
                        pack_d[pl.ds(2 * h + m, rows, stride=2 * split), :] = own[
                            :, h * LANES : (h + 1) * LANES
                        ]

    for j in range(chunks):
        dec_out[0, :, j * LANES : (j + 1) * LANES] = pack_d[2 * j : 2 * j + 2, :].astype(BF16)

    pack_g[...] = jnp.zeros(pack_g.shape, F32)

    def put_grad(layer, i, term):
        rows_here, width = term.shape
        term = term * (micro * replicas * heights[layer]) ** -0.5
        if width < LANES:
            small[0:rows_here, :] = term
            pack_g[pl.ds(i, rows_here // 2, stride=2), :] = jnp.concatenate(
                [
                    small[pl.ds(0, rows_here // 2, stride=2), :],
                    small[pl.ds(1, rows_here // 2, stride=2), :],
                ],
                axis=1,
            )
        else:
            split = width // LANES
            for h in range(split):
                pack_g[pl.ds(2 * h + i, rows_here, stride=2 * split), :] = term[
                    :, h * LANES : (h + 1) * LANES
                ]

    for layer in range(3):
        got = gots[layer]

        @pl.when(phase == layer)
        def _():
            owners, group, _ = group_of(layer)
            groups = replicas // owners

            @pl.when(group != 0)
            def _():
                far_copy(layer, group).wait_send()

            @pl.when(group == 0)
            def _():
                got[0] = sums_of[layer][0]
                for sender in range(1, groups):
                    far_copy(layer, sender).wait_recv()
                for i in range(2):
                    term = got[0, i].astype(F32)
                    for sender in range(1, groups):
                        term = term + got[sender, i].astype(F32)
                    put_grad(layer, i, term)

    @pl.when(phase == top)
    def _():
        wait_all(copy_cot)
        cols_all[0] = cols_send[me]
        wait_all(copy_cols)
        wait_all(copy_slope)
        span = micro * heights[top]

        def terms(slot):
            cols = cols_all[slot].astype(BF16)
            return (
                dot(cols[:, :span], slope_all[slot]),
                dot(cols[:, span:], cot_all[slot]),
            )

        total = terms(0)
        if replicas <= 16:
            for slot in range(1, replicas):
                total = jax.tree.map(jnp.add, total, terms(slot))
        else:
            total = lax.fori_loop(
                1, replicas, lambda s, t: jax.tree.map(jnp.add, t, terms(s)), total
            )
        for i in range(2):
            put_grad(top, i, total[i])

    for q in range(grad_out.shape[2] // LANES):
        grad_out[0, :, q * LANES : (q + 1) * LANES] = pack_g[2 * q : 2 * q + 2, :]


def deliver(dec_in, grad_in, dec_out, grad_out, sem):
    copies = [
        pltpu.make_async_copy(grad_in, grad_out, sem.at[0]),
        pltpu.make_async_copy(dec_in, dec_out, sem.at[1]),
    ]
    for copy in copies:
        copy.start()
    for copy in copies:
        copy.wait()


def on_device(*arrays):
    features, kms, dws = arrays[0], arrays[2:6], arrays[9:13]
    arrays = list(arrays)
    arrays[1] = arrays[1].T
    arrays[2:6] = [jnp.transpose(km, (1, 0, 2)) for km in kms]
    arrays[24] = arrays[24].T
    widths = [taps.shape[1] for taps in dws]
    heights = [km.shape[2] for km in kms]
    micro, elements = features.shape
    replicas = lax.axis_size("dp")
    owned = widths[3] * widths[3] // replicas

    def narrow(rows):
        return BF16 if rows % 16 == 0 else F32

    parts, gots, nears, sums_of = [], [], [], []
    for layer in range(3):
        rows_here = min(widths[layer], owned // widths[layer])
        owners = widths[layer] // rows_here
        kind = narrow(rows_here)
        parts.append(pltpu.VMEM((owners, 2, rows_here, widths[layer]), kind))
        gots.append(pltpu.VMEM((replicas // owners, 2, rows_here, widths[layer]), kind))
        nears.append(pltpu.VMEM((owners, 2, rows_here, widths[layer]), kind))
        sums_of.append(pltpu.VMEM((1, 2, rows_here, widths[layer]), kind))
    top_rows = owned // widths[3]
    span = micro * heights[3]
    idx_lanes = -(-micro * sum(heights) // LANES) * LANES
    sem = pltpu.SemaphoreType.DMA((replicas,))
    scratch = [
        *[pltpu.VMEM(a.shape, a.dtype) for a in arrays],
        pltpu.SemaphoreType.DMA((len(arrays),)),
        pltpu.VMEM((2 * elements // LANES, LANES), F32),
        pltpu.VMEM((2 * elements // LANES, LANES), F32),
        pltpu.VMEM((2 * elements // LANES, LANES), F32),
        pltpu.VMEM((2 * owned // LANES, LANES), F32),
        pltpu.VMEM((heights[0], widths[0]), F32),
        pltpu.VMEM((-(-heights[0] // LANES), 2 * IDX_ROWS, LANES), F32),
        pltpu.VMEM((IDX_ROWS, idx_lanes), F32),
        pltpu.VMEM((idx_lanes, IDX_ROWS), F32),
        *parts,
        *gots,
        *nears,
        *sums_of,
        pltpu.VMEM((replicas, span, widths[3]), BF16),
        pltpu.VMEM((replicas, span, widths[3]), BF16),
        pltpu.VMEM((replicas, top_rows, 2 * span), narrow(top_rows)),
        pltpu.VMEM((replicas, top_rows, 2 * span), narrow(top_rows)),
        *[sem] * 10,
    ]
    held = pl.pallas_call(
        functools.partial(kernel, replicas, heights, widths, micro, len(arrays)),
        out_shape=(
            pltpu.VMEM((1, micro, elements), BF16),
            pltpu.VMEM((1, 2, owned), F32),
        ),
        in_specs=[pl.BlockSpec(memory_space=pltpu.HBM)] * len(arrays),
        out_specs=[pl.BlockSpec(memory_space=pltpu.VMEM)] * 2,
        scratch_shapes=scratch,
        compiler_params=pltpu.CompilerParams(
            collective_id=0, has_side_effects=True, vmem_limit_bytes=64 * 1024 * 1024 - 512 * 1024
        ),
    )(*arrays)
    return pl.pallas_call(
        deliver,
        out_shape=(
            jax.ShapeDtypeStruct((1, micro, elements), BF16),
            jax.ShapeDtypeStruct((1, 2, owned), F32),
        ),
        in_specs=[pl.BlockSpec(memory_space=pltpu.VMEM)] * 2,
        out_specs=[pl.BlockSpec(memory_space=pltpu.HBM)] * 2,
        scratch_shapes=[pltpu.SemaphoreType.DMA((2,))],
        compiler_params=pltpu.CompilerParams(vmem_limit_bytes=1024 * 1024),
    )(*[pltpu.with_memory_space_constraint(a, pltpu.VMEM) for a in held])


def solution(mesh):
    placed = (
        (P(None, "dp"), P(None, "dp"))
        + (P(None, None, "dp"),) * 4
        + (P(None, "dp"),) * 3
        + (P(),) * 18
        + (P("phase", None, "dp"),)
    )
    return jax.shard_map(
        on_device,
        mesh=mesh,
        in_specs=placed,
        out_specs=(P("phase", None, "dp"), P("phase", None, "dp")),
        check_vma=False,
    )
```

```python
import functools
import math

import jax
import jax.numpy as jnp
from jax import lax
from jax.experimental import pallas as pl
from jax.experimental.pallas import tpu as pltpu
from jax.sharding import PartitionSpec as P

LANES = 128
TAPS = 27
IDX_ROWS = 32
BATCH = 9
F32 = jnp.float32
BF16 = jnp.bfloat16
MESH = pl.DeviceIdType.MESH
GELU_A = math.sqrt(2.0 / math.pi)
GELU_B = 0.044715


def dot(a, b):
    return lax.dot_general(a, b, (((1,), (0,)), ((), ())), preferred_element_type=F32)


def dot_nt(a, b):
    return lax.dot_general(a, b, (((1,), (1,)), ((), ())), preferred_element_type=F32)


def dot_tn(a, b):
    return lax.dot_general(a, b, (((0,), (0,)), ((), ())), preferred_element_type=F32)


def one_hot(column, width):
    lanes = lax.broadcasted_iota(jnp.int32, (column.shape[0], width), 1).astype(F32)
    return jnp.where(column == lanes, 1.0, 0.0).astype(BF16)


def pool_matrix(parent_row, coarse):
    rows = lax.broadcasted_iota(jnp.int32, (coarse, parent_row.shape[1]), 0)
    return jnp.where(rows == parent_row, 1.0, 0.0).astype(F32)


def kernel(replicas, heights, widths, micro, count, *refs):
    sources, (dec_out, grad_out) = refs[:count], refs[count : count + 2]
    held, refs = refs[count + 2 : 2 * count + 2], refs[2 * count + 2 :]
    (
        load_sem,
        pack_f,
        pack_c,
        pack_d,
        pack_g,
        small,
        idx_raw,
        idx,
        idx_t,
        part0,
        part1,
        part2,
        got0,
        got1,
        got2,
        near0,
        near1,
        near2,
        sum0,
        sum1,
        sum2,
        cot_all,
        slope_all,
        cols_send,
        cols_all,
        send_part,
        recv_part,
        send_cot,
        recv_cot,
        send_slope,
        recv_slope,
        send_cols,
        recv_cols,
        send_near,
        recv_near,
    ) = refs
    nears, sums_of = (near0, near1, near2), (sum0, sum1, sum2)
    features, counts, cot = held[0], held[1], held[27]
    kms, pms, dws = held[2:6], held[6:9], held[9:13]
    fws, sws = held[13:17], held[17:21]
    cos, res = held[21:24], held[24:27]
    parts, gots = (part0, part1, part2), (got0, got1, got2)
    phase = lax.axis_index("phase")
    me = lax.axis_index("dp")
    chunks = features.shape[1] // LANES

    def peer(offset):
        return {"phase": phase, "dp": lax.rem(me + offset, replicas)}

    def load(i):
        return pltpu.make_async_copy(sources[i], held[i], load_sem.at[i])

    order = [0, 27, 2, 3, 4, 5, 6, 7, 8, 1, 9, 13, 17, 21, 10, 14, 18, 22, 11, 15, 19, 23, 12, 16, 20]
    for i in order + [26, 25, 24]:
        load(i).start()

    barrier = pltpu.get_barrier_semaphore()

    @pl.loop(1, replicas)
    def _(offset):
        pl.semaphore_signal(barrier, inc=1, device_id=peer(offset), device_id_type=MESH)

    for i in (0, 27):
        load(i).wait()

    for j in range(chunks):
        lanes = slice(j * LANES, (j + 1) * LANES)
        pack_f[2 * j : 2 * j + 2, :] = features[:, lanes].astype(F32)
        pack_c[2 * j : 2 * j + 2, :] = cot[0, :, lanes].astype(F32)

    def unpack(pack, layer, m):
        rows, width = heights[layer], widths[layer]
        if width < LANES:
            both = pack[pl.ds(m, rows // 2, stride=2), :]
            small[pl.ds(0, rows // 2, stride=2), :] = both[:, :width]
            small[pl.ds(1, rows // 2, stride=2), :] = both[:, width:]
            return small[...]
        split = width // LANES
        return jnp.concatenate(
            [pack[pl.ds(2 * h + m, rows, stride=2 * split), :] for h in range(split)], axis=1
        )

    def target(layer):
        return jnp.concatenate([unpack(pack_c, layer, m) for m in range(micro)], axis=0).astype(BF16)

    top = 3

    def all_send(source, gathered, send_sem, recv_sem, indexed):
        def copy(to, sender):
            return pltpu.make_async_remote_copy(
                src_ref=source.at[to] if indexed else source.at[sender],
                dst_ref=gathered.at[sender],
                send_sem=send_sem.at[to],
                recv_sem=recv_sem.at[sender],
                device_id={"phase": phase, "dp": to},
                device_id_type=MESH,
            )

        return copy

    copy_cot = all_send(cot_all, cot_all, send_cot, recv_cot, False)
    copy_slope = all_send(slope_all, slope_all, send_slope, recv_slope, False)
    copy_cols = all_send(cols_send, cols_all, send_cols, recv_cols, True)

    def others(body):
        @pl.loop(0, replicas)
        def _(other):
            @pl.when(other != me)
            def _():
                body(other)

    def group_of(layer):
        owners = parts[layer].shape[0]
        return owners, lax.div(me, owners), lax.rem(me, owners)

    def near_copy(layer, w, sender):
        owners, group, _ = group_of(layer)
        return pltpu.make_async_remote_copy(
            src_ref=parts[layer].at[w],
            dst_ref=nears[layer].at[sender],
            send_sem=send_near.at[w],
            recv_sem=recv_near.at[sender],
            device_id={"phase": phase, "dp": group * owners + w},
            device_id_type=MESH,
        )

    def far_copy(layer, group):
        return pltpu.make_async_remote_copy(
            src_ref=sums_of[layer].at[0],
            dst_ref=gots[layer].at[group],
            send_sem=send_part.at[0],
            recv_sem=recv_part.at[group],
            device_id={"phase": phase, "dp": group_of(layer)[2]},
            device_id_type=MESH,
        )

    @pl.when(phase == top)
    def _():
        cot_all[me] = target(top)

    for i in (2, 3, 4, 5, 6, 7, 8, 1):
        load(i).wait()
    idx[...] = jnp.full(idx.shape, -1.0, F32)
    base = []
    position = 0
    for layer in range(4):
        rows = heights[layer]
        base.append(position)
        pieces = [(at, min(LANES, rows - at)) for at in range(0, rows, LANES)]
        for k in range(TAPS):
            for piece, (at, span) in enumerate(pieces):
                idx_raw[piece, 2 * k : 2 * k + 2, 0:span] = kms[layer][k, :, at : at + span].astype(F32)
        for m in range(micro):
            at = position + m * rows
            values = jnp.concatenate(
                [
                    idx_raw.at[piece][pl.ds(m, TAPS, stride=2), :][:, :span]
                    for piece, (_, span) in enumerate(pieces)
                ],
                axis=1,
            )
            shift = m * rows if layer >= 2 else 0
            if shift:
                values = jnp.where(values < 0.0, values, values + float(shift))
            idx[0:TAPS, at : at + rows] = values
            if layer < 3:
                idx[TAPS : TAPS + 1, at : at + rows] = pms[layer][m : m + 1, :].astype(F32)
        position += micro * rows
    for j in range(idx.shape[1] // LANES):
        lanes = slice(j * LANES, (j + 1) * LANES)
        idx_t[lanes, :] = idx[:, lanes].T

    live = []
    for m in range(micro):
        block = unpack(pack_f, 0, m)
        site = lax.broadcasted_iota(jnp.int32, block.shape, 0)
        live.append(jnp.where(site < counts[:, m : m + 1], block, 0.0))
    x = jnp.concatenate(live, axis=0).astype(BF16)

    def pass_on(layer):
        part, near = parts[layer], nears[layer]

        @pl.when(phase == layer)
        def _():
            owners, group, member = group_of(layer)
            near[member] = part[member]
            for w in range(owners):

                @pl.when(member != w)
                def _():
                    near_copy(layer, w, member).wait_send()
                    near_copy(layer, w, w).wait_recv()

            for i in range(2):
                term = near[0, i].astype(F32)
                for w in range(1, owners):
                    term = term + near[w, i].astype(F32)
                sums_of[layer][0, i] = term.astype(near.dtype)

            @pl.when(group != 0)
            def _():
                far_copy(layer, group).start()

    encodes = []
    for layer in range(4):
        for i in (9 + layer, 13 + layer, 17 + layer) + ((21 + layer,) if layer < 3 else ()):
            load(i).wait()
        rows, width = heights[layer], widths[layer]
        group = rows if layer < 2 else micro * rows
        mixes = []
        for start in range(0, micro * rows, group):
            block = x[start : start + group]
            index = idx_t[base[layer] + start : base[layer] + start + group, :]
            mixed = jnp.zeros((group, width), F32)
            for first in range(0, TAPS, BATCH):
                hots = [one_hot(index[:, k : k + 1], group) for k in range(first, first + BATCH)]
                gathered = dot(jnp.concatenate(hots, axis=0), block)
                for k in range(BATCH):
                    tap = dws[layer][first + k : first + k + 1, :].astype(F32)
                    mixed = mixed + gathered[k * group : (k + 1) * group] * tap
            mixes.append(mixed)
        mixed = mixes[0] if len(mixes) == 1 else jnp.concatenate(mixes, axis=0)
        normed_f = mixed * lax.rsqrt(jnp.mean(mixed * mixed, axis=1, keepdims=True) + 1e-05)
        normed = normed_f.astype(BF16)
        inner = dot(normed, fws[layer][...])
        squared = inner * inner
        bend = jnp.tanh(GELU_A * inner * (1.0 + GELU_B * squared))
        active = (0.5 * inner * (1.0 + bend)).astype(BF16)
        encoded = (x.astype(F32) + dot(active, sws[layer][...])).astype(BF16)
        encodes.append(encoded)
        if layer == 0:
            pl.semaphore_wait(barrier, replicas - 1)

            @pl.when(phase == top)
            def _():
                others(lambda to: copy_cot(to, me).start())

        @pl.when(phase == layer)
        def _():
            aim = target(layer) if layer < top else cot_all[me]
            backward = dot_nt(aim, sws[layer][...])
            grad = 0.5 * (1.0 + bend) + 0.5 * inner * (1.0 - bend * bend) * GELU_A * (
                1.0 + 3.0 * GELU_B * squared
            )
            slope = (grad * backward).astype(BF16)
            if layer == top:
                slope_all[me] = slope
                both = jnp.concatenate(
                    [normed.astype(F32).T, active.astype(F32).T], axis=1
                ).astype(cols_send.dtype)
                rows_here = cols_send.shape[1]
                for d in range(replicas):
                    cols_send[d] = both[d * rows_here : (d + 1) * rows_here]
                cols_all[me] = cols_send[me]

                @others
                def _(to):
                    copy_cols(to, me).start()
                    copy_slope(to, me).start()

            else:
                part = parts[layer]
                owners, _, rows_here, _ = part.shape
                for i, term in enumerate((dot_tn(normed, slope), dot_tn(active, aim))):
                    for w in range(owners):
                        part[w, i] = term[w * rows_here : (w + 1) * rows_here].astype(part.dtype)
                for w in range(owners):

                    @pl.when(group_of(layer)[2] != w)
                    def _():
                        near_copy(layer, w, group_of(layer)[2]).start()

        if layer > 0:
            pass_on(layer - 1)

        if layer < 3:
            coarse = heights[layer + 1]
            pooled = []
            for m in range(micro):
                matrix = pool_matrix(pms[layer][m : m + 1, :], coarse)
                number = jnp.sum(matrix, axis=1, keepdims=True)
                sums = dot(matrix.astype(BF16), encoded[m * rows : (m + 1) * rows])
                pooled.append(sums / jnp.maximum(number, 1.0))
            x = dot(jnp.concatenate(pooled, axis=0).astype(BF16), cos[layer][...]).astype(BF16)

    decoded = encodes[3]
    for layer in range(3, -1, -1):
        rows, width = heights[layer], widths[layer]
        if layer < 3:
            coarse = heights[layer + 1]
            load(24 + layer).wait()
            mix = dot_nt if layer == 0 else dot
            lifted = mix(decoded, res[layer][...]).astype(BF16)
            ups = []
            for m in range(micro):
                at = base[layer] + m * rows
                matrix = one_hot(idx_t[at : at + rows, TAPS : TAPS + 1], coarse)
                ups.append(dot(matrix, lifted[m * coarse : (m + 1) * coarse]))
            decoded = (encodes[layer].astype(F32) + jnp.concatenate(ups, axis=0)).astype(BF16)

        @pl.when(phase == layer)
        def _():
            wide = decoded.astype(F32)
            for m in range(micro):
                own = wide[m * rows : (m + 1) * rows]
                if width < LANES:
                    small[...] = own
                    pack_d[pl.ds(m, rows // 2, stride=2), :] = jnp.concatenate(
                        [
                            small[pl.ds(0, rows // 2, stride=2), :],
                            small[pl.ds(1, rows // 2, stride=2), :],
                        ],
                        axis=1,
                    )
                else:
                    split = width // LANES
                    for h in range(split):
                        pack_d[pl.ds(2 * h + m, rows, stride=2 * split), :] = own[
                            :, h * LANES : (h + 1) * LANES
                        ]

    for j in range(chunks):
        dec_out[0, :, j * LANES : (j + 1) * LANES] = pack_d[2 * j : 2 * j + 2, :].astype(BF16)

    pack_g[...] = jnp.zeros(pack_g.shape, F32)

    def put_grad(layer, i, term):
        rows_here, width = term.shape
        term = term * (micro * replicas * heights[layer]) ** -0.5
        if width < LANES:
            small[0:rows_here, :] = term
            pack_g[pl.ds(i, rows_here // 2, stride=2), :] = jnp.concatenate(
                [
                    small[pl.ds(0, rows_here // 2, stride=2), :],
                    small[pl.ds(1, rows_here // 2, stride=2), :],
                ],
                axis=1,
            )
        else:
            split = width // LANES
            for h in range(split):
                pack_g[pl.ds(2 * h + i, rows_here, stride=2 * split), :] = term[
                    :, h * LANES : (h + 1) * LANES
                ]

    for layer in range(3):
        got = gots[layer]

        @pl.when(phase == layer)
        def _():
            owners, group, _ = group_of(layer)
            groups = replicas // owners

            @pl.when(group != 0)
            def _():
                far_copy(layer, group).wait_send()

            @pl.when(group == 0)
            def _():
                got[0] = sums_of[layer][0]
                for sender in range(1, groups):
                    far_copy(layer, sender).wait_recv()
                for i in range(2):
                    term = got[0, i].astype(F32)
                    for sender in range(1, groups):
                        term = term + got[sender, i].astype(F32)
                    put_grad(layer, i, term)

    @pl.when(phase == top)
    def _():
        span = micro * heights[top]

        def terms(sender):
            @pl.when(sender != me)
            def _():
                copy_cot(me, sender).wait_recv()
                copy_cols(me, sender).wait_recv()
                copy_slope(me, sender).wait_recv()

            cols = cols_all[sender].astype(BF16)
            return (
                dot(cols[:, :span], slope_all[sender]),
                dot(cols[:, span:], cot_all[sender]),
            )

        total = terms(0)
        if replicas <= 16:
            for sender in range(1, replicas):
                total = jax.tree.map(jnp.add, total, terms(sender))
        else:
            total = lax.fori_loop(
                1, replicas, lambda s, t: jax.tree.map(jnp.add, t, terms(s)), total
            )
        for i in range(2):
            put_grad(top, i, total[i])

        @others
        def _(to):
            copy_cot(to, me).wait_send()
            copy_cols(to, me).wait_send()
            copy_slope(to, me).wait_send()


    for q in range(grad_out.shape[2] // LANES):
        grad_out[0, :, q * LANES : (q + 1) * LANES] = pack_g[2 * q : 2 * q + 2, :]


def deliver(dec_in, grad_in, dec_out, grad_out, sem):
    copies = [
        pltpu.make_async_copy(grad_in, grad_out, sem.at[0]),
        pltpu.make_async_copy(dec_in, dec_out, sem.at[1]),
    ]
    for copy in copies:
        copy.start()
    for copy in copies:
        copy.wait()


def on_device(*arrays):
    features, kms, dws = arrays[0], arrays[2:6], arrays[9:13]
    arrays = list(arrays)
    arrays[1] = arrays[1].T
    arrays[2:6] = [jnp.transpose(km, (1, 0, 2)) for km in kms]
    arrays[24] = arrays[24].T
    widths = [taps.shape[1] for taps in dws]
    heights = [km.shape[2] for km in kms]
    micro, elements = features.shape
    replicas = lax.axis_size("dp")
    owned = widths[3] * widths[3] // replicas

    def narrow(rows):
        return BF16 if rows % 16 == 0 else F32

    parts, gots, nears, sums_of = [], [], [], []
    for layer in range(3):
        rows_here = min(widths[layer], owned // widths[layer])
        owners = widths[layer] // rows_here
        kind = narrow(rows_here)
        parts.append(pltpu.VMEM((owners, 2, rows_here, widths[layer]), kind))
        gots.append(pltpu.VMEM((replicas // owners, 2, rows_here, widths[layer]), kind))
        nears.append(pltpu.VMEM((owners, 2, rows_here, widths[layer]), kind))
        sums_of.append(pltpu.VMEM((1, 2, rows_here, widths[layer]), kind))
    top_rows = owned // widths[3]
    span = micro * heights[3]
    idx_lanes = -(-micro * sum(heights) // LANES) * LANES
    sem = pltpu.SemaphoreType.DMA((replicas,))
    scratch = [
        *[pltpu.VMEM(a.shape, a.dtype) for a in arrays],
        pltpu.SemaphoreType.DMA((len(arrays),)),
        pltpu.VMEM((2 * elements // LANES, LANES), F32),
        pltpu.VMEM((2 * elements // LANES, LANES), F32),
        pltpu.VMEM((2 * elements // LANES, LANES), F32),
        pltpu.VMEM((2 * owned // LANES, LANES), F32),
        pltpu.VMEM((heights[0], widths[0]), F32),
        pltpu.VMEM((-(-heights[0] // LANES), 2 * IDX_ROWS, LANES), F32),
        pltpu.VMEM((IDX_ROWS, idx_lanes), F32),
        pltpu.VMEM((idx_lanes, IDX_ROWS), F32),
        *parts,
        *gots,
        *nears,
        *sums_of,
        pltpu.VMEM((replicas, span, widths[3]), BF16),
        pltpu.VMEM((replicas, span, widths[3]), BF16),
        pltpu.VMEM((replicas, top_rows, 2 * span), narrow(top_rows)),
        pltpu.VMEM((replicas, top_rows, 2 * span), narrow(top_rows)),
        *[sem] * 10,
    ]
    held = pl.pallas_call(
        functools.partial(kernel, replicas, heights, widths, micro, len(arrays)),
        out_shape=(
            pltpu.VMEM((1, micro, elements), BF16),
            pltpu.VMEM((1, 2, owned), F32),
        ),
        in_specs=[pl.BlockSpec(memory_space=pltpu.HBM)] * len(arrays),
        out_specs=[pl.BlockSpec(memory_space=pltpu.VMEM)] * 2,
        scratch_shapes=scratch,
        compiler_params=pltpu.CompilerParams(
            collective_id=0, has_side_effects=True, vmem_limit_bytes=64 * 1024 * 1024 - 512 * 1024
        ),
    )(*arrays)
    return pl.pallas_call(
        deliver,
        out_shape=(
            jax.ShapeDtypeStruct((1, micro, elements), BF16),
            jax.ShapeDtypeStruct((1, 2, owned), F32),
        ),
        in_specs=[pl.BlockSpec(memory_space=pltpu.VMEM)] * 2,
        out_specs=[pl.BlockSpec(memory_space=pltpu.HBM)] * 2,
        scratch_shapes=[pltpu.SemaphoreType.DMA((2,))],
        compiler_params=pltpu.CompilerParams(vmem_limit_bytes=1024 * 1024),
    )(*[pltpu.with_memory_space_constraint(a, pltpu.VMEM) for a in held])


def solution(mesh):
    placed = (
        (P(None, "dp"), P(None, "dp"))
        + (P(None, None, "dp"),) * 4
        + (P(None, "dp"),) * 3
        + (P(),) * 18
        + (P("phase", None, "dp"),)
    )
    return jax.shard_map(
        on_device,
        mesh=mesh,
        in_specs=placed,
        out_specs=(P("phase", None, "dp"), P("phase", None, "dp")),
        check_vma=False,
    )
```

```python
import functools
import math

import jax
import jax.numpy as jnp
from jax import lax
from jax.experimental import pallas as pl
from jax.experimental.pallas import tpu as pltpu
from jax.sharding import PartitionSpec as P

LANES = 128
TAPS = 27
IDX_ROWS = 32
BATCH = 9
F32 = jnp.float32
BF16 = jnp.bfloat16
MESH = pl.DeviceIdType.MESH
GELU_A = math.sqrt(2.0 / math.pi)
GELU_B = 0.044715


def dot(a, b):
    return lax.dot_general(a, b, (((1,), (0,)), ((), ())), preferred_element_type=F32)


def dot_nt(a, b):
    return lax.dot_general(a, b, (((1,), (1,)), ((), ())), preferred_element_type=F32)


def dot_tn(a, b):
    return lax.dot_general(a, b, (((0,), (0,)), ((), ())), preferred_element_type=F32)


def one_hot(column, width):
    lanes = lax.broadcasted_iota(jnp.int32, (column.shape[0], width), 1).astype(F32)
    return jnp.where(column == lanes, 1.0, 0.0).astype(BF16)


def pool_matrix(parent_row, coarse):
    rows = lax.broadcasted_iota(jnp.int32, (coarse, parent_row.shape[1]), 0)
    return jnp.where(rows == parent_row, 1.0, 0.0).astype(F32)


def kernel(replicas, heights, widths, micro, count, *refs):
    sources, (dec_out, grad_out) = refs[:count], refs[count : count + 2]
    held, refs = refs[count + 2 : 2 * count + 2], refs[2 * count + 2 :]
    (
        load_sem,
        pack_f,
        pack_c,
        pack_d,
        pack_g,
        small,
        idx_raw,
        idx,
        idx_t,
        part0,
        part1,
        part2,
        got0,
        got1,
        got2,
        near0,
        near1,
        near2,
        sum0,
        sum1,
        sum2,
        cot_all,
        slope_all,
        cols_send,
        cols_all,
        send_part,
        recv_part,
        send_cot,
        recv_cot,
        send_slope,
        recv_slope,
        send_cols,
        recv_cols,
        send_near,
        recv_near,
        aim_mid,
        got_help,
        send_aim,
        recv_aim,
        send_mid,
        recv_mid,
        send_far,
        recv_far,
        recv_help,
    ) = refs
    nears, sums_of = (near0, near1, near2), (sum0, sum1, sum2)
    features, counts, cot = held[0], held[1], held[27]
    kms, pms, dws = held[2:6], held[6:9], held[9:13]
    fws, sws = held[13:17], held[17:21]
    cos, res = held[21:24], held[24:27]
    parts, gots = (part0, part1, part2), (got0, got1, got2)
    phase = lax.axis_index("phase")
    me = lax.axis_index("dp")
    chunks = features.shape[1] // LANES

    def peer(offset):
        return {"phase": phase, "dp": lax.rem(me + offset, replicas)}

    def load(i):
        return pltpu.make_async_copy(sources[i], held[i], load_sem.at[i])

    order = [0, 27, 2, 3, 4, 5, 6, 7, 8, 1, 9, 13, 17, 21, 10, 14, 18, 22, 11, 15, 19, 23, 12, 16, 20]
    for i in order + [26, 25, 24]:
        load(i).start()

    mid, helper = 2, 0
    barrier = pltpu.get_barrier_semaphore()

    @pl.loop(1, replicas)
    def _(offset):
        pl.semaphore_signal(barrier, inc=1, device_id=peer(offset), device_id_type=MESH)

    mid_owners = part2.shape[0]
    mid_groups = replicas // mid_owners

    @pl.when(phase == helper)
    def _():
        pl.semaphore_signal(barrier, inc=1, device_id={"phase": mid, "dp": me}, device_id_type=MESH)

    @pl.when((phase == mid) & (me < mid_owners))
    def _():
        @pl.loop(0, mid_groups)
        def _(group):
            pl.semaphore_signal(
                barrier,
                inc=1,
                device_id={"phase": helper, "dp": group * mid_owners + me},
                device_id_type=MESH,
            )

    for i in (0, 27):
        load(i).wait()

    for j in range(chunks):
        lanes = slice(j * LANES, (j + 1) * LANES)
        pack_f[2 * j : 2 * j + 2, :] = features[:, lanes].astype(F32)
        pack_c[2 * j : 2 * j + 2, :] = cot[0, :, lanes].astype(F32)

    def unpack(pack, layer, m):
        rows, width = heights[layer], widths[layer]
        if width < LANES:
            both = pack[pl.ds(m, rows // 2, stride=2), :]
            small[pl.ds(0, rows // 2, stride=2), :] = both[:, :width]
            small[pl.ds(1, rows // 2, stride=2), :] = both[:, width:]
            return small[...]
        split = width // LANES
        return jnp.concatenate(
            [pack[pl.ds(2 * h + m, rows, stride=2 * split), :] for h in range(split)], axis=1
        )

    def target(layer):
        return jnp.concatenate([unpack(pack_c, layer, m) for m in range(micro)], axis=0).astype(BF16)

    top = 3

    def all_send(source, gathered, send_sem, recv_sem, indexed):
        def copy(to, sender):
            return pltpu.make_async_remote_copy(
                src_ref=source.at[to] if indexed else source.at[sender],
                dst_ref=gathered.at[sender],
                send_sem=send_sem.at[to],
                recv_sem=recv_sem.at[sender],
                device_id={"phase": phase, "dp": to},
                device_id_type=MESH,
            )

        return copy

    copy_cot = all_send(cot_all, cot_all, send_cot, recv_cot, False)
    copy_slope = all_send(slope_all, slope_all, send_slope, recv_slope, False)
    copy_cols = all_send(cols_send, cols_all, send_cols, recv_cols, True)

    def others(body):
        @pl.loop(0, replicas)
        def _(other):
            @pl.when(other != me)
            def _():
                body(other)

    def group_of(layer):
        owners = parts[layer].shape[0]
        return owners, lax.div(me, owners), lax.rem(me, owners)

    def near_copy(layer, w, sender):
        owners, group, _ = group_of(layer)
        return pltpu.make_async_remote_copy(
            src_ref=parts[layer].at[w],
            dst_ref=nears[layer].at[sender],
            send_sem=send_near.at[w],
            recv_sem=recv_near.at[sender],
            device_id={"phase": phase, "dp": group * owners + w},
            device_id_type=MESH,
        )

    def far_copy(layer, group):
        return pltpu.make_async_remote_copy(
            src_ref=sums_of[layer].at[0],
            dst_ref=gots[layer].at[group],
            send_sem=send_part.at[0],
            recv_sem=recv_part.at[group],
            device_id={"phase": phase, "dp": group_of(layer)[2]},
            device_id_type=MESH,
        )

    @pl.when(phase == top)
    def _():
        cot_all[me] = target(top)

    @pl.when(phase == mid)
    def _():
        aim_mid[0] = target(mid)

    aim_copy = pltpu.make_async_remote_copy(
        src_ref=aim_mid.at[0],
        dst_ref=aim_mid.at[1],
        send_sem=send_aim.at[0],
        recv_sem=recv_aim.at[0],
        device_id={"phase": helper, "dp": me},
        device_id_type=MESH,
    )

    def mid_near(w, sender):
        _, group, _ = group_of(mid)
        return pltpu.make_async_remote_copy(
            src_ref=part2.at[w],
            dst_ref=near2.at[sender],
            send_sem=send_mid.at[w],
            recv_sem=recv_mid.at[sender],
            device_id={"phase": phase, "dp": group * mid_owners + w},
            device_id_type=MESH,
        )

    def mid_far(got, recv_sem, group):
        return pltpu.make_async_remote_copy(
            src_ref=sum2.at[0],
            dst_ref=got.at[group],
            send_sem=send_far.at[0],
            recv_sem=recv_sem.at[group],
            device_id={"phase": mid, "dp": group_of(mid)[2]},
            device_id_type=MESH,
        )

    def mid_start(term):
        rows_here = part2.shape[1]
        member = group_of(mid)[2]
        for w in range(mid_owners):
            part2[w] = term[w * rows_here : (w + 1) * rows_here].astype(part2.dtype)
        for w in range(mid_owners):

            @pl.when(member != w)
            def _():
                mid_near(w, member).start()

    def mid_pass():
        @pl.when((phase == mid) | (phase == helper))
        def _():
            _, group, member = group_of(mid)
            near2[member] = part2[member]
            for w in range(mid_owners):

                @pl.when(member != w)
                def _():
                    mid_near(w, member).wait_send()
                    mid_near(w, w).wait_recv()

            term = near2[0].astype(F32)
            for w in range(1, mid_owners):
                term = term + near2[w].astype(F32)
            sum2[0] = term.astype(near2.dtype)

            @pl.when(phase == helper)
            def _():
                mid_far(got_help, recv_help, group).start()

            @pl.when((phase == mid) & (group != 0))
            def _():
                mid_far(got2, recv_far, group).start()

    for i in (2, 3, 4, 5, 6, 7, 8, 1):
        load(i).wait()
    idx[...] = jnp.full(idx.shape, -1.0, F32)
    base = []
    position = 0
    for layer in range(4):
        rows = heights[layer]
        base.append(position)
        pieces = [(at, min(LANES, rows - at)) for at in range(0, rows, LANES)]
        for k in range(TAPS):
            for piece, (at, span) in enumerate(pieces):
                idx_raw[piece, 2 * k : 2 * k + 2, 0:span] = kms[layer][k, :, at : at + span].astype(F32)
        for m in range(micro):
            at = position + m * rows
            values = jnp.concatenate(
                [
                    idx_raw.at[piece][pl.ds(m, TAPS, stride=2), :][:, :span]
                    for piece, (_, span) in enumerate(pieces)
                ],
                axis=1,
            )
            shift = m * rows if layer >= 2 else 0
            if shift:
                values = jnp.where(values < 0.0, values, values + float(shift))
            idx[0:TAPS, at : at + rows] = values
            if layer < 3:
                idx[TAPS : TAPS + 1, at : at + rows] = pms[layer][m : m + 1, :].astype(F32)
        position += micro * rows
    for j in range(idx.shape[1] // LANES):
        lanes = slice(j * LANES, (j + 1) * LANES)
        idx_t[lanes, :] = idx[:, lanes].T

    live = []
    for m in range(micro):
        block = unpack(pack_f, 0, m)
        site = lax.broadcasted_iota(jnp.int32, block.shape, 0)
        live.append(jnp.where(site < counts[:, m : m + 1], block, 0.0))
    x = jnp.concatenate(live, axis=0).astype(BF16)

    def pass_on(layer):
        part, near = parts[layer], nears[layer]

        @pl.when(phase == layer)
        def _():
            owners, group, member = group_of(layer)
            near[member] = part[member]
            for w in range(owners):

                @pl.when(member != w)
                def _():
                    near_copy(layer, w, member).wait_send()
                    near_copy(layer, w, w).wait_recv()

            for i in range(2):
                term = near[0, i].astype(F32)
                for w in range(1, owners):
                    term = term + near[w, i].astype(F32)
                sums_of[layer][0, i] = term.astype(near.dtype)

            @pl.when(group != 0)
            def _():
                far_copy(layer, group).start()

    encodes = []
    for layer in range(4):
        for i in (9 + layer, 13 + layer, 17 + layer) + ((21 + layer,) if layer < 3 else ()):
            load(i).wait()
        rows, width = heights[layer], widths[layer]
        group = rows if layer < 2 else micro * rows
        mixes = []
        for start in range(0, micro * rows, group):
            block = x[start : start + group]
            index = idx_t[base[layer] + start : base[layer] + start + group, :]
            mixed = jnp.zeros((group, width), F32)
            for first in range(0, TAPS, BATCH):
                hots = [one_hot(index[:, k : k + 1], group) for k in range(first, first + BATCH)]
                gathered = dot(jnp.concatenate(hots, axis=0), block)
                for k in range(BATCH):
                    tap = dws[layer][first + k : first + k + 1, :].astype(F32)
                    mixed = mixed + gathered[k * group : (k + 1) * group] * tap
            mixes.append(mixed)
        mixed = mixes[0] if len(mixes) == 1 else jnp.concatenate(mixes, axis=0)
        normed_f = mixed * lax.rsqrt(jnp.mean(mixed * mixed, axis=1, keepdims=True) + 1e-05)
        normed = normed_f.astype(BF16)
        inner = dot(normed, fws[layer][...])
        squared = inner * inner
        bend = jnp.tanh(GELU_A * inner * (1.0 + GELU_B * squared))
        active = (0.5 * inner * (1.0 + bend)).astype(BF16)
        encoded = (x.astype(F32) + dot(active, sws[layer][...])).astype(BF16)
        encodes.append(encoded)
        if layer == 0:
            paired = (phase == helper) | (phase == mid)

            @pl.when(paired)
            def _():
                pl.semaphore_wait(barrier, replicas)

            @pl.when(jnp.logical_not(paired))
            def _():
                pl.semaphore_wait(barrier, replicas - 1)

            @pl.when(phase == mid)
            def _():
                aim_copy.start()

            @pl.when(phase == top)
            def _():
                others(lambda to: copy_cot(to, me).start())

        @pl.when(phase == layer)
        def _():
            aim = target(layer) if layer < mid else (aim_mid[0] if layer == mid else cot_all[me])
            backward = dot_nt(aim, sws[layer][...])
            grad = 0.5 * (1.0 + bend) + 0.5 * inner * (1.0 - bend * bend) * GELU_A * (
                1.0 + 3.0 * GELU_B * squared
            )
            slope = (grad * backward).astype(BF16)
            if layer == top:
                slope_all[me] = slope
                both = jnp.concatenate(
                    [normed.astype(F32).T, active.astype(F32).T], axis=1
                ).astype(cols_send.dtype)
                rows_here = cols_send.shape[1]
                for d in range(replicas):
                    cols_send[d] = both[d * rows_here : (d + 1) * rows_here]
                cols_all[me] = cols_send[me]

                @others
                def _(to):
                    copy_cols(to, me).start()
                    copy_slope(to, me).start()

            elif layer == mid:
                mid_start(dot_tn(normed, slope))
            else:
                part = parts[layer]
                owners, _, rows_here, _ = part.shape
                for i, term in enumerate((dot_tn(normed, slope), dot_tn(active, aim))):
                    for w in range(owners):
                        part[w, i] = term[w * rows_here : (w + 1) * rows_here].astype(part.dtype)
                for w in range(owners):

                    @pl.when(group_of(layer)[2] != w)
                    def _():
                        near_copy(layer, w, group_of(layer)[2]).start()

        if layer == mid:

            @pl.when(phase == helper)
            def _():
                aim_copy.wait_recv()
                mid_start(dot_tn(active, aim_mid[1]))

        if layer == top:
            mid_pass()
        elif layer > 0:
            pass_on(layer - 1)

        if layer < 3:
            coarse = heights[layer + 1]
            pooled = []
            for m in range(micro):
                matrix = pool_matrix(pms[layer][m : m + 1, :], coarse)
                number = jnp.sum(matrix, axis=1, keepdims=True)
                sums = dot(matrix.astype(BF16), encoded[m * rows : (m + 1) * rows])
                pooled.append(sums / jnp.maximum(number, 1.0))
            x = dot(jnp.concatenate(pooled, axis=0).astype(BF16), cos[layer][...]).astype(BF16)

    decoded = encodes[3]
    for layer in range(3, -1, -1):
        rows, width = heights[layer], widths[layer]
        if layer < 3:
            coarse = heights[layer + 1]
            load(24 + layer).wait()
            mix = dot_nt if layer == 0 else dot
            lifted = mix(decoded, res[layer][...]).astype(BF16)
            ups = []
            for m in range(micro):
                at = base[layer] + m * rows
                matrix = one_hot(idx_t[at : at + rows, TAPS : TAPS + 1], coarse)
                ups.append(dot(matrix, lifted[m * coarse : (m + 1) * coarse]))
            decoded = (encodes[layer].astype(F32) + jnp.concatenate(ups, axis=0)).astype(BF16)

        @pl.when(phase == layer)
        def _():
            wide = decoded.astype(F32)
            for m in range(micro):
                own = wide[m * rows : (m + 1) * rows]
                if width < LANES:
                    small[...] = own
                    pack_d[pl.ds(m, rows // 2, stride=2), :] = jnp.concatenate(
                        [
                            small[pl.ds(0, rows // 2, stride=2), :],
                            small[pl.ds(1, rows // 2, stride=2), :],
                        ],
                        axis=1,
                    )
                else:
                    split = width // LANES
                    for h in range(split):
                        pack_d[pl.ds(2 * h + m, rows, stride=2 * split), :] = own[
                            :, h * LANES : (h + 1) * LANES
                        ]

    for j in range(chunks):
        dec_out[0, :, j * LANES : (j + 1) * LANES] = pack_d[2 * j : 2 * j + 2, :].astype(BF16)

    pack_g[...] = jnp.zeros(pack_g.shape, F32)

    def put_grad(layer, i, term):
        rows_here, width = term.shape
        term = term * (micro * replicas * heights[layer]) ** -0.5
        if width < LANES:
            small[0:rows_here, :] = term
            pack_g[pl.ds(i, rows_here // 2, stride=2), :] = jnp.concatenate(
                [
                    small[pl.ds(0, rows_here // 2, stride=2), :],
                    small[pl.ds(1, rows_here // 2, stride=2), :],
                ],
                axis=1,
            )
        else:
            split = width // LANES
            for h in range(split):
                pack_g[pl.ds(2 * h + i, rows_here, stride=2 * split), :] = term[
                    :, h * LANES : (h + 1) * LANES
                ]

    @pl.when(phase == helper)
    def _():
        mid_far(got_help, recv_help, 0).wait_send()

    @pl.when(phase == mid)
    def _():
        aim_copy.wait_send()
        group = group_of(mid)[1]

        @pl.when(group != 0)
        def _():
            mid_far(got2, recv_far, 0).wait_send()

        @pl.when(group == 0)
        def _():
            got2[0] = sum2[0]
            for i, (got, recv_sem) in enumerate(((got2, recv_far), (got_help, recv_help))):
                for sender in range(1 - i, mid_groups):
                    mid_far(got, recv_sem, sender).wait_recv()
                term = got[0].astype(F32)
                for sender in range(1, mid_groups):
                    term = term + got[sender].astype(F32)
                put_grad(mid, i, term)

    for layer in range(2):
        got = gots[layer]

        @pl.when(phase == layer)
        def _():
            owners, group, _ = group_of(layer)
            groups = replicas // owners

            @pl.when(group != 0)
            def _():
                far_copy(layer, group).wait_send()

            @pl.when(group == 0)
            def _():
                got[0] = sums_of[layer][0]
                for sender in range(1, groups):
                    far_copy(layer, sender).wait_recv()
                for i in range(2):
                    term = got[0, i].astype(F32)
                    for sender in range(1, groups):
                        term = term + got[sender, i].astype(F32)
                    put_grad(layer, i, term)

    @pl.when(phase == top)
    def _():
        span = micro * heights[top]

        def terms(sender):
            @pl.when(sender != me)
            def _():
                copy_cot(me, sender).wait_recv()
                copy_cols(me, sender).wait_recv()
                copy_slope(me, sender).wait_recv()

            cols = cols_all[sender].astype(BF16)
            return (
                dot(cols[:, :span], slope_all[sender]),
                dot(cols[:, span:], cot_all[sender]),
            )

        total = terms(0)
        if replicas <= 16:
            for sender in range(1, replicas):
                total = jax.tree.map(jnp.add, total, terms(sender))
        else:
            total = lax.fori_loop(
                1, replicas, lambda s, t: jax.tree.map(jnp.add, t, terms(s)), total
            )
        for i in range(2):
            put_grad(top, i, total[i])

        @others
        def _(to):
            copy_cot(to, me).wait_send()
            copy_cols(to, me).wait_send()
            copy_slope(to, me).wait_send()


    for q in range(grad_out.shape[2] // LANES):
        grad_out[0, :, q * LANES : (q + 1) * LANES] = pack_g[2 * q : 2 * q + 2, :]


def deliver(dec_in, grad_in, dec_out, grad_out, sem):
    copies = [
        pltpu.make_async_copy(grad_in, grad_out, sem.at[0]),
        pltpu.make_async_copy(dec_in, dec_out, sem.at[1]),
    ]
    for copy in copies:
        copy.start()
    for copy in copies:
        copy.wait()


def on_device(*arrays):
    features, kms, dws = arrays[0], arrays[2:6], arrays[9:13]
    arrays = list(arrays)
    arrays[1] = arrays[1].T
    arrays[2:6] = [jnp.transpose(km, (1, 0, 2)) for km in kms]
    arrays[24] = arrays[24].T
    widths = [taps.shape[1] for taps in dws]
    heights = [km.shape[2] for km in kms]
    micro, elements = features.shape
    replicas = lax.axis_size("dp")
    owned = widths[3] * widths[3] // replicas

    def narrow(rows):
        return BF16 if rows % 16 == 0 else F32

    parts, gots, nears, sums_of = [], [], [], []
    for layer in range(3):
        rows_here = min(widths[layer], owned // widths[layer])
        owners = widths[layer] // rows_here
        kind = narrow(rows_here)
        if layer == 2:
            shape = (rows_here, widths[2])
            for held, first in ((parts, owners), (gots, replicas // owners), (nears, owners), (sums_of, 1)):
                held.append(pltpu.VMEM((first, *shape), kind))
            break
        parts.append(pltpu.VMEM((owners, 2, rows_here, widths[layer]), kind))
        gots.append(pltpu.VMEM((replicas // owners, 2, rows_here, widths[layer]), kind))
        nears.append(pltpu.VMEM((owners, 2, rows_here, widths[layer]), kind))
        sums_of.append(pltpu.VMEM((1, 2, rows_here, widths[layer]), kind))
    top_rows = owned // widths[3]
    span = micro * heights[3]
    idx_lanes = -(-micro * sum(heights) // LANES) * LANES
    sem = pltpu.SemaphoreType.DMA((replicas,))
    scratch = [
        *[pltpu.VMEM(a.shape, a.dtype) for a in arrays],
        pltpu.SemaphoreType.DMA((len(arrays),)),
        pltpu.VMEM((2 * elements // LANES, LANES), F32),
        pltpu.VMEM((2 * elements // LANES, LANES), F32),
        pltpu.VMEM((2 * elements // LANES, LANES), F32),
        pltpu.VMEM((2 * owned // LANES, LANES), F32),
        pltpu.VMEM((heights[0], widths[0]), F32),
        pltpu.VMEM((-(-heights[0] // LANES), 2 * IDX_ROWS, LANES), F32),
        pltpu.VMEM((IDX_ROWS, idx_lanes), F32),
        pltpu.VMEM((idx_lanes, IDX_ROWS), F32),
        *parts,
        *gots,
        *nears,
        *sums_of,
        pltpu.VMEM((replicas, span, widths[3]), BF16),
        pltpu.VMEM((replicas, span, widths[3]), BF16),
        pltpu.VMEM((replicas, top_rows, 2 * span), narrow(top_rows)),
        pltpu.VMEM((replicas, top_rows, 2 * span), narrow(top_rows)),
        *[sem] * 10,
        pltpu.VMEM((2, micro * heights[2], widths[2]), BF16),
        gots[2],
        *[sem] * 7,
    ]
    held = pl.pallas_call(
        functools.partial(kernel, replicas, heights, widths, micro, len(arrays)),
        out_shape=(
            pltpu.VMEM((1, micro, elements), BF16),
            pltpu.VMEM((1, 2, owned), F32),
        ),
        in_specs=[pl.BlockSpec(memory_space=pltpu.HBM)] * len(arrays),
        out_specs=[pl.BlockSpec(memory_space=pltpu.VMEM)] * 2,
        scratch_shapes=scratch,
        compiler_params=pltpu.CompilerParams(
            collective_id=0, has_side_effects=True, vmem_limit_bytes=64 * 1024 * 1024 - 512 * 1024
        ),
    )(*arrays)
    return pl.pallas_call(
        deliver,
        out_shape=(
            jax.ShapeDtypeStruct((1, micro, elements), BF16),
            jax.ShapeDtypeStruct((1, 2, owned), F32),
        ),
        in_specs=[pl.BlockSpec(memory_space=pltpu.VMEM)] * 2,
        out_specs=[pl.BlockSpec(memory_space=pltpu.HBM)] * 2,
        scratch_shapes=[pltpu.SemaphoreType.DMA((2,))],
        compiler_params=pltpu.CompilerParams(vmem_limit_bytes=1024 * 1024),
    )(*[pltpu.with_memory_space_constraint(a, pltpu.VMEM) for a in held])


def solution(mesh):
    placed = (
        (P(None, "dp"), P(None, "dp"))
        + (P(None, None, "dp"),) * 4
        + (P(None, "dp"),) * 3
        + (P(),) * 18
        + (P("phase", None, "dp"),)
    )
    return jax.shard_map(
        on_device,
        mesh=mesh,
        in_specs=placed,
        out_specs=(P("phase", None, "dp"), P("phase", None, "dp")),
        check_vma=False,
    )
```

```python
import functools
import math

import jax
import jax.numpy as jnp
from jax import lax
from jax.experimental import pallas as pl
from jax.experimental.pallas import tpu as pltpu
from jax.sharding import PartitionSpec as P

LANES = 128
TAPS = 27
IDX_ROWS = 32
BATCH = 9
F32 = jnp.float32
BF16 = jnp.bfloat16
MESH = pl.DeviceIdType.MESH
GELU_A = math.sqrt(2.0 / math.pi)
GELU_B = 0.044715


def dot(a, b):
    return lax.dot_general(a, b, (((1,), (0,)), ((), ())), preferred_element_type=F32)


def dot_nt(a, b):
    return lax.dot_general(a, b, (((1,), (1,)), ((), ())), preferred_element_type=F32)


def dot_tn(a, b):
    return lax.dot_general(a, b, (((0,), (0,)), ((), ())), preferred_element_type=F32)


def one_hot(column, width):
    lanes = lax.broadcasted_iota(jnp.int32, (column.shape[0], width), 1).astype(F32)
    return jnp.where(column == lanes, 1.0, 0.0).astype(BF16)


def pool_matrix(parent_row, coarse):
    rows = lax.broadcasted_iota(jnp.int32, (coarse, parent_row.shape[1]), 0)
    return jnp.where(rows == parent_row, 1.0, 0.0).astype(F32)


def kernel(replicas, heights, widths, micro, count, *refs):
    sources, (dec_out, grad_out) = refs[:count], refs[count : count + 2]
    held, refs = refs[count + 2 : 2 * count + 2], refs[2 * count + 2 :]
    (
        load_sem,
        pack_f,
        pack_c,
        pack_d,
        pack_g,
        small,
        idx_raw,
        idx,
        idx_t,
        part0,
        part1,
        part2,
        got0,
        got1,
        got2,
        near0,
        near1,
        near2,
        sum0,
        sum1,
        sum2,
        cot_all,
        slope_all,
        cols_send,
        cols_all,
        send_part,
        recv_part,
        send_cot,
        recv_cot,
        send_slope,
        recv_slope,
        send_cols,
        recv_cols,
        send_near,
        recv_near,
        aim_mid,
        got_help,
        send_aim,
        recv_aim,
        send_mid,
        recv_mid,
        send_far,
        recv_far,
        recv_help,
        relay_cot,
        relay_slope,
    ) = refs
    nears, sums_of = (near0, near1, near2), (sum0, sum1, sum2)
    features, counts, cot = held[0], held[1], held[27]
    kms, pms, dws = held[2:6], held[6:9], held[9:13]
    fws, sws = held[13:17], held[17:21]
    cos, res = held[21:24], held[24:27]
    parts, gots = (part0, part1, part2), (got0, got1, got2)
    phase = lax.axis_index("phase")
    me = lax.axis_index("dp")
    chunks = features.shape[1] // LANES

    def peer(offset):
        return {"phase": phase, "dp": lax.rem(me + offset, replicas)}

    def load(i):
        return pltpu.make_async_copy(sources[i], held[i], load_sem.at[i])

    order = [0, 27, 2, 3, 4, 5, 6, 7, 8, 1, 9, 13, 17, 21, 10, 14, 18, 22, 11, 15, 19, 23, 12, 16, 20]
    for i in order + [26, 25, 24]:
        load(i).start()

    mid, helper = 2, 0
    barrier = pltpu.get_barrier_semaphore()

    @pl.loop(1, replicas)
    def _(offset):
        pl.semaphore_signal(barrier, inc=1, device_id=peer(offset), device_id_type=MESH)

    mid_owners = part2.shape[0]
    mid_groups = replicas // mid_owners

    @pl.when(phase == helper)
    def _():
        pl.semaphore_signal(barrier, inc=1, device_id={"phase": mid, "dp": me}, device_id_type=MESH)

    @pl.when((phase == mid) & (me < mid_owners))
    def _():
        @pl.loop(0, mid_groups)
        def _(group):
            pl.semaphore_signal(
                barrier,
                inc=1,
                device_id={"phase": helper, "dp": group * mid_owners + me},
                device_id_type=MESH,
            )

    for i in (0, 27):
        load(i).wait()

    for j in range(chunks):
        lanes = slice(j * LANES, (j + 1) * LANES)
        pack_f[2 * j : 2 * j + 2, :] = features[:, lanes].astype(F32)
        pack_c[2 * j : 2 * j + 2, :] = cot[0, :, lanes].astype(F32)

    def unpack(pack, layer, m):
        rows, width = heights[layer], widths[layer]
        if width < LANES:
            both = pack[pl.ds(m, rows // 2, stride=2), :]
            small[pl.ds(0, rows // 2, stride=2), :] = both[:, :width]
            small[pl.ds(1, rows // 2, stride=2), :] = both[:, width:]
            return small[...]
        split = width // LANES
        return jnp.concatenate(
            [pack[pl.ds(2 * h + m, rows, stride=2 * split), :] for h in range(split)], axis=1
        )

    def target(layer):
        return jnp.concatenate([unpack(pack_c, layer, m) for m in range(micro)], axis=0).astype(BF16)

    top = 3

    def all_send(source, gathered, send_sem, recv_sem, indexed):
        def copy(to, sender, send_sem=send_sem):
            return pltpu.make_async_remote_copy(
                src_ref=source.at[to] if indexed else source.at[sender],
                dst_ref=gathered.at[sender],
                send_sem=send_sem.at[to],
                recv_sem=recv_sem.at[sender],
                device_id={"phase": phase, "dp": to},
                device_id_type=MESH,
            )

        return copy

    copy_cot = all_send(cot_all, cot_all, send_cot, recv_cot, False)
    copy_slope = all_send(slope_all, slope_all, send_slope, recv_slope, False)
    copy_cols = all_send(cols_send, cols_all, send_cols, recv_cols, True)

    partner = me + 1 - 2 * lax.rem(me, 2)

    def alike(other):
        return lax.rem(other, 2) == lax.rem(me, 2)

    def others(body):
        @pl.loop(0, replicas)
        def _(other):
            @pl.when(other != me)
            def _():
                body(other)

    def direct(body):
        @others
        def _(to):
            @pl.when(alike(to) | (to == partner))
            def _():
                body(to)

    def column(body):
        @others
        def _(sender):
            @pl.when(alike(sender))
            def _():
                body(sender)

    def group_of(layer):
        owners = parts[layer].shape[0]
        return owners, lax.div(me, owners), lax.rem(me, owners)

    def near_copy(layer, w, sender):
        owners, group, _ = group_of(layer)
        return pltpu.make_async_remote_copy(
            src_ref=parts[layer].at[w],
            dst_ref=nears[layer].at[sender],
            send_sem=send_near.at[w],
            recv_sem=recv_near.at[sender],
            device_id={"phase": phase, "dp": group * owners + w},
            device_id_type=MESH,
        )

    def far_copy(layer, group):
        return pltpu.make_async_remote_copy(
            src_ref=sums_of[layer].at[0],
            dst_ref=gots[layer].at[group],
            send_sem=send_part.at[0],
            recv_sem=recv_part.at[group],
            device_id={"phase": phase, "dp": group_of(layer)[2]},
            device_id_type=MESH,
        )

    @pl.when(phase == top)
    def _():
        cot_all[me] = target(top)

    @pl.when(phase == mid)
    def _():
        aim_mid[0] = target(mid)

    aim_copy = pltpu.make_async_remote_copy(
        src_ref=aim_mid.at[0],
        dst_ref=aim_mid.at[1],
        send_sem=send_aim.at[0],
        recv_sem=recv_aim.at[0],
        device_id={"phase": helper, "dp": me},
        device_id_type=MESH,
    )

    def mid_near(w, sender):
        _, group, _ = group_of(mid)
        return pltpu.make_async_remote_copy(
            src_ref=part2.at[w],
            dst_ref=near2.at[sender],
            send_sem=send_mid.at[w],
            recv_sem=recv_mid.at[sender],
            device_id={"phase": phase, "dp": group * mid_owners + w},
            device_id_type=MESH,
        )

    def mid_far(got, recv_sem, group):
        return pltpu.make_async_remote_copy(
            src_ref=sum2.at[0],
            dst_ref=got.at[group],
            send_sem=send_far.at[0],
            recv_sem=recv_sem.at[group],
            device_id={"phase": mid, "dp": group_of(mid)[2]},
            device_id_type=MESH,
        )

    def mid_start(term):
        rows_here = part2.shape[1]
        member = group_of(mid)[2]
        for w in range(mid_owners):
            part2[w] = term[w * rows_here : (w + 1) * rows_here].astype(part2.dtype)
        for w in range(mid_owners):

            @pl.when(member != w)
            def _():
                mid_near(w, member).start()

    def mid_pass():
        @pl.when((phase == mid) | (phase == helper))
        def _():
            _, group, member = group_of(mid)
            near2[member] = part2[member]
            for w in range(mid_owners):

                @pl.when(member != w)
                def _():
                    mid_near(w, member).wait_send()
                    mid_near(w, w).wait_recv()

            term = near2[0].astype(F32)
            for w in range(1, mid_owners):
                term = term + near2[w].astype(F32)
            sum2[0] = term.astype(near2.dtype)

            @pl.when(phase == helper)
            def _():
                mid_far(got_help, recv_help, group).start()

            @pl.when((phase == mid) & (group != 0))
            def _():
                mid_far(got2, recv_far, group).start()

    for i in (2, 3, 4, 5, 6, 7, 8, 1):
        load(i).wait()
    idx[...] = jnp.full(idx.shape, -1.0, F32)
    base = []
    position = 0
    for layer in range(4):
        rows = heights[layer]
        base.append(position)
        pieces = [(at, min(LANES, rows - at)) for at in range(0, rows, LANES)]
        for k in range(TAPS):
            for piece, (at, span) in enumerate(pieces):
                idx_raw[piece, 2 * k : 2 * k + 2, 0:span] = kms[layer][k, :, at : at + span].astype(F32)
        for m in range(micro):
            at = position + m * rows
            values = jnp.concatenate(
                [
                    idx_raw.at[piece][pl.ds(m, TAPS, stride=2), :][:, :span]
                    for piece, (_, span) in enumerate(pieces)
                ],
                axis=1,
            )
            shift = m * rows if layer >= 2 else 0
            if shift:
                values = jnp.where(values < 0.0, values, values + float(shift))
            idx[0:TAPS, at : at + rows] = values
            if layer < 3:
                idx[TAPS : TAPS + 1, at : at + rows] = pms[layer][m : m + 1, :].astype(F32)
        position += micro * rows
    for j in range(idx.shape[1] // LANES):
        lanes = slice(j * LANES, (j + 1) * LANES)
        idx_t[lanes, :] = idx[:, lanes].T

    live = []
    for m in range(micro):
        block = unpack(pack_f, 0, m)
        site = lax.broadcasted_iota(jnp.int32, block.shape, 0)
        live.append(jnp.where(site < counts[:, m : m + 1], block, 0.0))
    x = jnp.concatenate(live, axis=0).astype(BF16)

    def pass_on(layer):
        part, near = parts[layer], nears[layer]

        @pl.when(phase == layer)
        def _():
            owners, group, member = group_of(layer)
            near[member] = part[member]
            for w in range(owners):

                @pl.when(member != w)
                def _():
                    near_copy(layer, w, member).wait_send()
                    near_copy(layer, w, w).wait_recv()

            for i in range(2):
                term = near[0, i].astype(F32)
                for w in range(1, owners):
                    term = term + near[w, i].astype(F32)
                sums_of[layer][0, i] = term.astype(near.dtype)

            @pl.when(group != 0)
            def _():
                far_copy(layer, group).start()

    encodes = []
    for layer in range(4):
        for i in (9 + layer, 13 + layer, 17 + layer) + ((21 + layer,) if layer < 3 else ()):
            load(i).wait()
        rows, width = heights[layer], widths[layer]
        group = rows if layer < 2 else micro * rows
        mixes = []
        for start in range(0, micro * rows, group):
            block = x[start : start + group]
            index = idx_t[base[layer] + start : base[layer] + start + group, :]
            mixed = jnp.zeros((group, width), F32)
            for first in range(0, TAPS, BATCH):
                hots = [one_hot(index[:, k : k + 1], group) for k in range(first, first + BATCH)]
                gathered = dot(jnp.concatenate(hots, axis=0), block)
                for k in range(BATCH):
                    tap = dws[layer][first + k : first + k + 1, :].astype(F32)
                    mixed = mixed + gathered[k * group : (k + 1) * group] * tap
            mixes.append(mixed)
        mixed = mixes[0] if len(mixes) == 1 else jnp.concatenate(mixes, axis=0)
        normed_f = mixed * lax.rsqrt(jnp.mean(mixed * mixed, axis=1, keepdims=True) + 1e-05)
        normed = normed_f.astype(BF16)
        inner = dot(normed, fws[layer][...])
        squared = inner * inner
        bend = jnp.tanh(GELU_A * inner * (1.0 + GELU_B * squared))
        active = (0.5 * inner * (1.0 + bend)).astype(BF16)
        encoded = (x.astype(F32) + dot(active, sws[layer][...])).astype(BF16)
        encodes.append(encoded)
        if layer == 0:
            paired = (phase == helper) | (phase == mid)

            @pl.when(paired)
            def _():
                pl.semaphore_wait(barrier, replicas)

            @pl.when(jnp.logical_not(paired))
            def _():
                pl.semaphore_wait(barrier, replicas - 1)

            @pl.when(phase == mid)
            def _():
                aim_copy.start()

            @pl.when(phase == top)
            def _():
                direct(lambda to: copy_cot(to, me).start())

        @pl.when(phase == layer)
        def _():
            aim = target(layer) if layer < mid else (aim_mid[0] if layer == mid else cot_all[me])
            backward = dot_nt(aim, sws[layer][...])
            grad = 0.5 * (1.0 + bend) + 0.5 * inner * (1.0 - bend * bend) * GELU_A * (
                1.0 + 3.0 * GELU_B * squared
            )
            slope = (grad * backward).astype(BF16)
            if layer == top:
                slope_all[me] = slope
                both = jnp.concatenate(
                    [normed.astype(F32).T, active.astype(F32).T], axis=1
                ).astype(cols_send.dtype)
                rows_here = cols_send.shape[1]
                for d in range(replicas):
                    cols_send[d] = both[d * rows_here : (d + 1) * rows_here]
                cols_all[me] = cols_send[me]

                @others
                def _(to):
                    copy_cols(to, me).start()

                @direct
                def _(to):
                    copy_slope(to, me).start()

            elif layer == mid:
                mid_start(dot_tn(normed, slope))
            else:
                part = parts[layer]
                owners, _, rows_here, _ = part.shape
                for i, term in enumerate((dot_tn(normed, slope), dot_tn(active, aim))):
                    for w in range(owners):
                        part[w, i] = term[w * rows_here : (w + 1) * rows_here].astype(part.dtype)
                for w in range(owners):

                    @pl.when(group_of(layer)[2] != w)
                    def _():
                        near_copy(layer, w, group_of(layer)[2]).start()

        if layer == mid:

            @pl.when(phase == helper)
            def _():
                aim_copy.wait_recv()
                mid_start(dot_tn(active, aim_mid[1]))

        if layer == top:
            mid_pass()
        elif layer > 0:
            pass_on(layer - 1)

        if layer < 3:
            coarse = heights[layer + 1]
            pooled = []
            for m in range(micro):
                matrix = pool_matrix(pms[layer][m : m + 1, :], coarse)
                number = jnp.sum(matrix, axis=1, keepdims=True)
                sums = dot(matrix.astype(BF16), encoded[m * rows : (m + 1) * rows])
                pooled.append(sums / jnp.maximum(number, 1.0))
            x = dot(jnp.concatenate(pooled, axis=0).astype(BF16), cos[layer][...]).astype(BF16)

    decoded = encodes[3]
    for layer in range(3, -1, -1):
        rows, width = heights[layer], widths[layer]
        if layer < 3:
            coarse = heights[layer + 1]
            load(24 + layer).wait()
            mix = dot_nt if layer == 0 else dot
            lifted = mix(decoded, res[layer][...]).astype(BF16)
            ups = []
            for m in range(micro):
                at = base[layer] + m * rows
                matrix = one_hot(idx_t[at : at + rows, TAPS : TAPS + 1], coarse)
                ups.append(dot(matrix, lifted[m * coarse : (m + 1) * coarse]))
            decoded = (encodes[layer].astype(F32) + jnp.concatenate(ups, axis=0)).astype(BF16)

        @pl.when(phase == layer)
        def _():
            wide = decoded.astype(F32)
            for m in range(micro):
                own = wide[m * rows : (m + 1) * rows]
                if width < LANES:
                    small[...] = own
                    pack_d[pl.ds(m, rows // 2, stride=2), :] = jnp.concatenate(
                        [
                            small[pl.ds(0, rows // 2, stride=2), :],
                            small[pl.ds(1, rows // 2, stride=2), :],
                        ],
                        axis=1,
                    )
                else:
                    split = width // LANES
                    for h in range(split):
                        pack_d[pl.ds(2 * h + m, rows, stride=2 * split), :] = own[
                            :, h * LANES : (h + 1) * LANES
                        ]

    for j in range(chunks):
        dec_out[0, :, j * LANES : (j + 1) * LANES] = pack_d[2 * j : 2 * j + 2, :].astype(BF16)

    pack_g[...] = jnp.zeros(pack_g.shape, F32)

    def put_grad(layer, i, term):
        rows_here, width = term.shape
        term = term * (micro * replicas * heights[layer]) ** -0.5
        if width < LANES:
            small[0:rows_here, :] = term
            pack_g[pl.ds(i, rows_here // 2, stride=2), :] = jnp.concatenate(
                [
                    small[pl.ds(0, rows_here // 2, stride=2), :],
                    small[pl.ds(1, rows_here // 2, stride=2), :],
                ],
                axis=1,
            )
        else:
            split = width // LANES
            for h in range(split):
                pack_g[pl.ds(2 * h + i, rows_here, stride=2 * split), :] = term[
                    :, h * LANES : (h + 1) * LANES
                ]

    @pl.when(phase == helper)
    def _():
        mid_far(got_help, recv_help, 0).wait_send()

    @pl.when(phase == mid)
    def _():
        aim_copy.wait_send()
        group = group_of(mid)[1]

        @pl.when(group != 0)
        def _():
            mid_far(got2, recv_far, 0).wait_send()

        @pl.when(group == 0)
        def _():
            got2[0] = sum2[0]
            for i, (got, recv_sem) in enumerate(((got2, recv_far), (got_help, recv_help))):
                for sender in range(1 - i, mid_groups):
                    mid_far(got, recv_sem, sender).wait_recv()
                term = got[0].astype(F32)
                for sender in range(1, mid_groups):
                    term = term + got[sender].astype(F32)
                put_grad(mid, i, term)

    for layer in range(2):
        got = gots[layer]

        @pl.when(phase == layer)
        def _():
            owners, group, _ = group_of(layer)
            groups = replicas // owners

            @pl.when(group != 0)
            def _():
                far_copy(layer, group).wait_send()

            @pl.when(group == 0)
            def _():
                got[0] = sums_of[layer][0]
                for sender in range(1, groups):
                    far_copy(layer, sender).wait_recv()
                for i in range(2):
                    term = got[0, i].astype(F32)
                    for sender in range(1, groups):
                        term = term + got[sender, i].astype(F32)
                    put_grad(layer, i, term)

    @pl.when(phase == top)
    def _():
        span = micro * heights[top]

        @column
        def _(sender):
            copy_cot(me, sender).wait_recv()
            copy_cot(partner, sender, relay_cot).start()

        def relay(sender):
            @pl.when(alike(sender) & (sender != me))
            def _():
                copy_slope(me, sender).wait_recv()
                copy_slope(partner, sender, relay_slope).start()

        def terms(sender):
            @pl.when(sender != me)
            def _():
                copy_cols(me, sender).wait_recv()

            @pl.when(jnp.logical_not(alike(sender)))
            def _():
                copy_cot(me, sender).wait_recv()
                copy_slope(me, sender).wait_recv()

            cols = cols_all[sender].astype(BF16)
            return (
                dot(cols[:, :span], slope_all[sender]),
                dot(cols[:, span:], cot_all[sender]),
            )

        if replicas <= 16:
            relay(0)
            relay(1)
            total = None
            for sender in range(replicas):
                if sender + 2 < replicas:
                    relay(sender + 2)
                new = terms(sender)
                total = new if total is None else jax.tree.map(jnp.add, total, new)
        else:
            pl.loop(0, replicas)(relay)
            total = lax.fori_loop(
                1, replicas, lambda s, t: jax.tree.map(jnp.add, t, terms(s)), terms(0)
            )
        for i in range(2):
            put_grad(top, i, total[i])

        @others
        def _(to):
            copy_cols(to, me).wait_send()

        @direct
        def _(to):
            copy_cot(to, me).wait_send()
            copy_slope(to, me).wait_send()

        @column
        def _(sender):
            copy_cot(partner, sender, relay_cot).wait_send()
            copy_slope(partner, sender, relay_slope).wait_send()


    for q in range(grad_out.shape[2] // LANES):
        grad_out[0, :, q * LANES : (q + 1) * LANES] = pack_g[2 * q : 2 * q + 2, :]


def deliver(dec_in, grad_in, dec_out, grad_out, sem):
    copies = [
        pltpu.make_async_copy(grad_in, grad_out, sem.at[0]),
        pltpu.make_async_copy(dec_in, dec_out, sem.at[1]),
    ]
    for copy in copies:
        copy.start()
    for copy in copies:
        copy.wait()


def on_device(*arrays):
    features, kms, dws = arrays[0], arrays[2:6], arrays[9:13]
    arrays = list(arrays)
    arrays[1] = arrays[1].T
    arrays[2:6] = [jnp.transpose(km, (1, 0, 2)) for km in kms]
    arrays[24] = arrays[24].T
    widths = [taps.shape[1] for taps in dws]
    heights = [km.shape[2] for km in kms]
    micro, elements = features.shape
    replicas = lax.axis_size("dp")
    owned = widths[3] * widths[3] // replicas

    def narrow(rows):
        return BF16 if rows % 16 == 0 else F32

    parts, gots, nears, sums_of = [], [], [], []
    for layer in range(3):
        rows_here = min(widths[layer], owned // widths[layer])
        owners = widths[layer] // rows_here
        kind = narrow(rows_here)
        if layer == 2:
            shape = (rows_here, widths[2])
            for held, first in ((parts, owners), (gots, replicas // owners), (nears, owners), (sums_of, 1)):
                held.append(pltpu.VMEM((first, *shape), kind))
            break
        parts.append(pltpu.VMEM((owners, 2, rows_here, widths[layer]), kind))
        gots.append(pltpu.VMEM((replicas // owners, 2, rows_here, widths[layer]), kind))
        nears.append(pltpu.VMEM((owners, 2, rows_here, widths[layer]), kind))
        sums_of.append(pltpu.VMEM((1, 2, rows_here, widths[layer]), kind))
    top_rows = owned // widths[3]
    span = micro * heights[3]
    idx_lanes = -(-micro * sum(heights) // LANES) * LANES
    sem = pltpu.SemaphoreType.DMA((replicas,))
    scratch = [
        *[pltpu.VMEM(a.shape, a.dtype) for a in arrays],
        pltpu.SemaphoreType.DMA((len(arrays),)),
        pltpu.VMEM((2 * elements // LANES, LANES), F32),
        pltpu.VMEM((2 * elements // LANES, LANES), F32),
        pltpu.VMEM((2 * elements // LANES, LANES), F32),
        pltpu.VMEM((2 * owned // LANES, LANES), F32),
        pltpu.VMEM((heights[0], widths[0]), F32),
        pltpu.VMEM((-(-heights[0] // LANES), 2 * IDX_ROWS, LANES), F32),
        pltpu.VMEM((IDX_ROWS, idx_lanes), F32),
        pltpu.VMEM((idx_lanes, IDX_ROWS), F32),
        *parts,
        *gots,
        *nears,
        *sums_of,
        pltpu.VMEM((replicas, span, widths[3]), BF16),
        pltpu.VMEM((replicas, span, widths[3]), BF16),
        pltpu.VMEM((replicas, top_rows, 2 * span), narrow(top_rows)),
        pltpu.VMEM((replicas, top_rows, 2 * span), narrow(top_rows)),
        *[sem] * 10,
        pltpu.VMEM((2, micro * heights[2], widths[2]), BF16),
        gots[2],
        *[sem] * 9,
    ]
    held = pl.pallas_call(
        functools.partial(kernel, replicas, heights, widths, micro, len(arrays)),
        out_shape=(
            pltpu.VMEM((1, micro, elements), BF16),
            pltpu.VMEM((1, 2, owned), F32),
        ),
        in_specs=[pl.BlockSpec(memory_space=pltpu.HBM)] * len(arrays),
        out_specs=[pl.BlockSpec(memory_space=pltpu.VMEM)] * 2,
        scratch_shapes=scratch,
        compiler_params=pltpu.CompilerParams(
            collective_id=0, has_side_effects=True, vmem_limit_bytes=64 * 1024 * 1024 - 512 * 1024
        ),
    )(*arrays)
    return pl.pallas_call(
        deliver,
        out_shape=(
            jax.ShapeDtypeStruct((1, micro, elements), BF16),
            jax.ShapeDtypeStruct((1, 2, owned), F32),
        ),
        in_specs=[pl.BlockSpec(memory_space=pltpu.VMEM)] * 2,
        out_specs=[pl.BlockSpec(memory_space=pltpu.HBM)] * 2,
        scratch_shapes=[pltpu.SemaphoreType.DMA((2,))],
        compiler_params=pltpu.CompilerParams(vmem_limit_bytes=1024 * 1024),
    )(*[pltpu.with_memory_space_constraint(a, pltpu.VMEM) for a in held])


def solution(mesh):
    placed = (
        (P(None, "dp"), P(None, "dp"))
        + (P(None, None, "dp"),) * 4
        + (P(None, "dp"),) * 3
        + (P(),) * 18
        + (P("phase", None, "dp"),)
    )
    return jax.shard_map(
        on_device,
        mesh=mesh,
        in_specs=placed,
        out_specs=(P("phase", None, "dp"), P("phase", None, "dp")),
        check_vma=False,
    )
```

```python
import functools
import math

import jax
import jax.numpy as jnp
from jax import lax
from jax.experimental import pallas as pl
from jax.experimental.pallas import tpu as pltpu
from jax.sharding import PartitionSpec as P

LANES = 128
TAPS = 27
IDX_ROWS = 32
BATCH = 9
F32 = jnp.float32
BF16 = jnp.bfloat16
MESH = pl.DeviceIdType.MESH
GELU_A = math.sqrt(2.0 / math.pi)
GELU_B = 0.044715


def dot(a, b):
    return lax.dot_general(a, b, (((1,), (0,)), ((), ())), preferred_element_type=F32)


def dot_nt(a, b):
    return lax.dot_general(a, b, (((1,), (1,)), ((), ())), preferred_element_type=F32)


def dot_tn(a, b):
    return lax.dot_general(a, b, (((0,), (0,)), ((), ())), preferred_element_type=F32)


def one_hot(column, width):
    lanes = lax.broadcasted_iota(jnp.int32, (column.shape[0], width), 1).astype(F32)
    return jnp.where(column == lanes, 1.0, 0.0).astype(BF16)


def pool_matrix(parent_row, coarse):
    rows = lax.broadcasted_iota(jnp.int32, (coarse, parent_row.shape[1]), 0)
    return jnp.where(rows == parent_row, 1.0, 0.0).astype(F32)


def kernel(replicas, heights, widths, micro, count, *refs):
    sources, (dec_out, grad_out) = refs[:count], refs[count : count + 2]
    held, refs = refs[count + 2 : 2 * count + 2], refs[2 * count + 2 :]
    (
        load_sem,
        pack_f,
        pack_c,
        pack_d,
        pack_g,
        small,
        idx_raw,
        idx,
        idx_t,
        part0,
        part1,
        part2,
        got0,
        got1,
        got2,
        near0,
        near1,
        near2,
        sum0,
        sum1,
        sum2,
        send_part,
        recv_part,
        send_near,
        recv_near,
        aim_mid,
        got_help,
        send_aim,
        recv_aim,
        send_mid,
        recv_mid,
        send_far,
        recv_far,
        recv_help,
        aim_top,
        pair_l,
        pair_r,
        held_sum,
        blocks,
        got_first,
        got_second,
        send_top,
        send_l,
        recv_l,
        send_r,
        recv_r,
        send_block,
        recv_first,
        recv_second,
    ) = refs
    nears, sums_of = (near0, near1, near2), (sum0, sum1, sum2)
    features, counts, cot = held[0], held[1], held[27]
    kms, pms, dws = held[2:6], held[6:9], held[9:13]
    fws, sws = held[13:17], held[17:21]
    cos, res = held[21:24], held[24:27]
    parts, gots = (part0, part1, part2), (got0, got1, got2)
    phase = lax.axis_index("phase")
    me = lax.axis_index("dp")
    chunks = features.shape[1] // LANES

    def peer(offset):
        return {"phase": phase, "dp": lax.rem(me + offset, replicas)}

    def load(i):
        return pltpu.make_async_copy(sources[i], held[i], load_sem.at[i])

    order = [0, 27, 2, 3, 4, 5, 6, 7, 8, 1, 9, 13, 17, 21, 10, 14, 18, 22, 11, 15, 19, 23, 12, 16, 20]
    for i in order + [26, 25, 24]:
        load(i).start()

    mid, helper, aid = 2, 0, 1
    half = replicas // 2
    partner = me + 1 - 2 * lax.rem(me, 2)
    odd = lax.rem(me, 2)
    barrier = pltpu.get_barrier_semaphore()

    @pl.loop(1, replicas)
    def _(offset):
        pl.semaphore_signal(barrier, inc=1, device_id=peer(offset), device_id_type=MESH)

    mid_owners = part2.shape[0]
    mid_groups = replicas // mid_owners

    @pl.when(phase == helper)
    def _():
        pl.semaphore_signal(barrier, inc=1, device_id={"phase": mid, "dp": me}, device_id_type=MESH)

    @pl.when((phase == mid) & (me < mid_owners))
    def _():
        @pl.loop(0, mid_groups)
        def _(group):
            pl.semaphore_signal(
                barrier,
                inc=1,
                device_id={"phase": helper, "dp": group * mid_owners + me},
                device_id_type=MESH,
            )

    @pl.when(phase == aid)
    def _():
        for to in (me, partner):
            pl.semaphore_signal(barrier, inc=1, device_id={"phase": 3, "dp": to}, device_id_type=MESH)

    @pl.when(phase == 3)
    def _():
        @pl.loop(0, half)
        def _(w):
            pl.semaphore_signal(
                barrier, inc=1, device_id={"phase": aid, "dp": 2 * w + odd}, device_id_type=MESH
            )

    for i in (0, 27):
        load(i).wait()

    for j in range(chunks):
        lanes = slice(j * LANES, (j + 1) * LANES)
        pack_f[2 * j : 2 * j + 2, :] = features[:, lanes].astype(F32)
        pack_c[2 * j : 2 * j + 2, :] = cot[0, :, lanes].astype(F32)

    def unpack(pack, layer, m):
        rows, width = heights[layer], widths[layer]
        if width < LANES:
            both = pack[pl.ds(m, rows // 2, stride=2), :]
            small[pl.ds(0, rows // 2, stride=2), :] = both[:, :width]
            small[pl.ds(1, rows // 2, stride=2), :] = both[:, width:]
            return small[...]
        split = width // LANES
        return jnp.concatenate(
            [pack[pl.ds(2 * h + m, rows, stride=2 * split), :] for h in range(split)], axis=1
        )

    def target(layer):
        return jnp.concatenate([unpack(pack_c, layer, m) for m in range(micro)], axis=0).astype(BF16)

    top = 3

    def aim_send(slot):
        return pltpu.make_async_remote_copy(
            src_ref=aim_top.at[0],
            dst_ref=pair_r.at[slot],
            send_sem=send_top.at[slot],
            recv_sem=recv_r.at[slot],
            device_id={"phase": aid, "dp": partner if slot else me},
            device_id_type=MESH,
        )

    def swap(pair, send_sem, recv_sem):
        return pltpu.make_async_remote_copy(
            src_ref=pair.at[0],
            dst_ref=pair.at[1],
            send_sem=send_sem.at[0],
            recv_sem=recv_sem.at[1],
            device_id={"phase": phase, "dp": partner},
            device_id_type=MESH,
        )

    swap_l, swap_r = swap(pair_l, send_l, recv_l), swap(pair_r, send_r, recv_r)

    def block_copy(got, recv_sem, w, sender):
        return pltpu.make_async_remote_copy(
            src_ref=blocks.at[w],
            dst_ref=got.at[sender],
            send_sem=send_block.at[w],
            recv_sem=recv_sem.at[sender],
            device_id={"phase": top, "dp": 2 * w + odd},
            device_id_type=MESH,
        )

    def outer(slot):
        turned = pair_l[slot].astype(F32).T
        rows_here = blocks.shape[1]
        picked = [
            jnp.where(
                odd == 0,
                turned[2 * w * rows_here : (2 * w + 1) * rows_here],
                turned[(2 * w + 1) * rows_here : (2 * w + 2) * rows_here],
            )
            for w in range(half)
        ]
        return dot(jnp.concatenate(picked, axis=0).astype(BF16), pair_r[slot])

    def pair_first():
        held_sum[...] = outer(0)

    def pair_second():
        rows_here = blocks.shape[1]
        total = held_sum[...] + outer(1)
        for w in range(half):
            blocks[w] = total[w * rows_here : (w + 1) * rows_here].astype(blocks.dtype)

    def group_of(layer):
        owners = parts[layer].shape[0]
        return owners, lax.div(me, owners), lax.rem(me, owners)

    def near_copy(layer, w, sender):
        owners, group, _ = group_of(layer)
        return pltpu.make_async_remote_copy(
            src_ref=parts[layer].at[w],
            dst_ref=nears[layer].at[sender],
            send_sem=send_near.at[w],
            recv_sem=recv_near.at[sender],
            device_id={"phase": phase, "dp": group * owners + w},
            device_id_type=MESH,
        )

    def far_copy(layer, group):
        return pltpu.make_async_remote_copy(
            src_ref=sums_of[layer].at[0],
            dst_ref=gots[layer].at[group],
            send_sem=send_part.at[0],
            recv_sem=recv_part.at[group],
            device_id={"phase": phase, "dp": group_of(layer)[2]},
            device_id_type=MESH,
        )

    @pl.when(phase == top)
    def _():
        aim_top[0] = target(top)

    @pl.when(phase == mid)
    def _():
        aim_mid[0] = target(mid)

    aim_copy = pltpu.make_async_remote_copy(
        src_ref=aim_mid.at[0],
        dst_ref=aim_mid.at[1],
        send_sem=send_aim.at[0],
        recv_sem=recv_aim.at[0],
        device_id={"phase": helper, "dp": me},
        device_id_type=MESH,
    )

    def mid_near(w, sender):
        _, group, _ = group_of(mid)
        return pltpu.make_async_remote_copy(
            src_ref=part2.at[w],
            dst_ref=near2.at[sender],
            send_sem=send_mid.at[w],
            recv_sem=recv_mid.at[sender],
            device_id={"phase": phase, "dp": group * mid_owners + w},
            device_id_type=MESH,
        )

    def mid_far(got, recv_sem, group):
        return pltpu.make_async_remote_copy(
            src_ref=sum2.at[0],
            dst_ref=got.at[group],
            send_sem=send_far.at[0],
            recv_sem=recv_sem.at[group],
            device_id={"phase": mid, "dp": group_of(mid)[2]},
            device_id_type=MESH,
        )

    def mid_start(term):
        rows_here = part2.shape[1]
        member = group_of(mid)[2]
        for w in range(mid_owners):
            part2[w] = term[w * rows_here : (w + 1) * rows_here].astype(part2.dtype)
        for w in range(mid_owners):

            @pl.when(member != w)
            def _():
                mid_near(w, member).start()

    def mid_pass():
        @pl.when((phase == mid) | (phase == helper))
        def _():
            _, group, member = group_of(mid)
            near2[member] = part2[member]
            for w in range(mid_owners):

                @pl.when(member != w)
                def _():
                    mid_near(w, member).wait_send()
                    mid_near(w, w).wait_recv()

            term = near2[0].astype(F32)
            for w in range(1, mid_owners):
                term = term + near2[w].astype(F32)
            sum2[0] = term.astype(near2.dtype)

            @pl.when(phase == helper)
            def _():
                mid_far(got_help, recv_help, group).start()

            @pl.when((phase == mid) & (group != 0))
            def _():
                mid_far(got2, recv_far, group).start()

    for i in (2, 3, 4, 5, 6, 7, 8, 1):
        load(i).wait()
    idx[...] = jnp.full(idx.shape, -1.0, F32)
    base = []
    position = 0
    for layer in range(4):
        rows = heights[layer]
        base.append(position)
        pieces = [(at, min(LANES, rows - at)) for at in range(0, rows, LANES)]
        for k in range(TAPS):
            for piece, (at, span) in enumerate(pieces):
                idx_raw[piece, 2 * k : 2 * k + 2, 0:span] = kms[layer][k, :, at : at + span].astype(F32)
        for m in range(micro):
            at = position + m * rows
            values = jnp.concatenate(
                [
                    idx_raw.at[piece][pl.ds(m, TAPS, stride=2), :][:, :span]
                    for piece, (_, span) in enumerate(pieces)
                ],
                axis=1,
            )
            shift = m * rows if layer >= 2 else 0
            if shift:
                values = jnp.where(values < 0.0, values, values + float(shift))
            idx[0:TAPS, at : at + rows] = values
            if layer < 3:
                idx[TAPS : TAPS + 1, at : at + rows] = pms[layer][m : m + 1, :].astype(F32)
        position += micro * rows
    for j in range(idx.shape[1] // LANES):
        lanes = slice(j * LANES, (j + 1) * LANES)
        idx_t[lanes, :] = idx[:, lanes].T

    live = []
    for m in range(micro):
        block = unpack(pack_f, 0, m)
        site = lax.broadcasted_iota(jnp.int32, block.shape, 0)
        live.append(jnp.where(site < counts[:, m : m + 1], block, 0.0))
    x = jnp.concatenate(live, axis=0).astype(BF16)

    def pass_on(layer):
        part, near = parts[layer], nears[layer]

        @pl.when(phase == layer)
        def _():
            owners, group, member = group_of(layer)
            near[member] = part[member]
            for w in range(owners):

                @pl.when(member != w)
                def _():
                    near_copy(layer, w, member).wait_send()
                    near_copy(layer, w, w).wait_recv()

            for i in range(2):
                term = near[0, i].astype(F32)
                for w in range(1, owners):
                    term = term + near[w, i].astype(F32)
                sums_of[layer][0, i] = term.astype(near.dtype)

            @pl.when(group != 0)
            def _():
                far_copy(layer, group).start()

    encodes = []
    for layer in range(4):
        for i in (9 + layer, 13 + layer, 17 + layer) + ((21 + layer,) if layer < 3 else ()):
            load(i).wait()
        rows, width = heights[layer], widths[layer]
        group = rows if layer < 2 else micro * rows
        mixes = []
        for start in range(0, micro * rows, group):
            block = x[start : start + group]
            index = idx_t[base[layer] + start : base[layer] + start + group, :]
            mixed = jnp.zeros((group, width), F32)
            for first in range(0, TAPS, BATCH):
                hots = [one_hot(index[:, k : k + 1], group) for k in range(first, first + BATCH)]
                gathered = dot(jnp.concatenate(hots, axis=0), block)
                for k in range(BATCH):
                    tap = dws[layer][first + k : first + k + 1, :].astype(F32)
                    mixed = mixed + gathered[k * group : (k + 1) * group] * tap
            mixes.append(mixed)
        mixed = mixes[0] if len(mixes) == 1 else jnp.concatenate(mixes, axis=0)
        normed_f = mixed * lax.rsqrt(jnp.mean(mixed * mixed, axis=1, keepdims=True) + 1e-05)
        normed = normed_f.astype(BF16)
        if layer == top:

            @pl.when(phase == top)
            def _():
                pair_l[0] = normed
                swap_l.start()

        inner = dot(normed, fws[layer][...])
        squared = inner * inner
        bend = jnp.tanh(GELU_A * inner * (1.0 + GELU_B * squared))
        active = (0.5 * inner * (1.0 + bend)).astype(BF16)
        if layer == top:

            @pl.when(phase == aid)
            def _():
                pair_l[0] = active
                swap_l.start()
                aim_send(0).wait_recv()
                pair_first()

        encoded = (x.astype(F32) + dot(active, sws[layer][...])).astype(BF16)
        encodes.append(encoded)
        if layer == 0:
            for which, count in (
                (helper, replicas),
                (mid, replicas),
                (aid, replicas - 1 + half),
                (top, replicas + 1),
            ):

                @pl.when(phase == which)
                def _():
                    pl.semaphore_wait(barrier, count)

            @pl.when(phase == mid)
            def _():
                aim_copy.start()

            @pl.when(phase == top)
            def _():
                aim_send(0).start()
                aim_send(1).start()

        @pl.when(phase == layer)
        def _():
            aim = target(layer) if layer < mid else (aim_mid[0] if layer == mid else aim_top[0])
            backward = dot_nt(aim, sws[layer][...])
            grad = 0.5 * (1.0 + bend) + 0.5 * inner * (1.0 - bend * bend) * GELU_A * (
                1.0 + 3.0 * GELU_B * squared
            )
            slope = (grad * backward).astype(BF16)
            if layer == top:
                pair_r[0] = slope
                swap_r.start()
                pair_first()
            elif layer == mid:
                mid_start(dot_tn(normed, slope))
            else:
                part = parts[layer]
                owners, _, rows_here, _ = part.shape
                for i, term in enumerate((dot_tn(normed, slope), dot_tn(active, aim))):
                    for w in range(owners):
                        part[w, i] = term[w * rows_here : (w + 1) * rows_here].astype(part.dtype)
                for w in range(owners):

                    @pl.when(group_of(layer)[2] != w)
                    def _():
                        near_copy(layer, w, group_of(layer)[2]).start()

        if layer == mid:

            @pl.when(phase == helper)
            def _():
                aim_copy.wait_recv()
                mid_start(dot_tn(active, aim_mid[1]))

        if layer == top:
            mid_pass()
        elif layer > 0:
            pass_on(layer - 1)

        if layer < 3:
            coarse = heights[layer + 1]
            pooled = []
            for m in range(micro):
                matrix = pool_matrix(pms[layer][m : m + 1, :], coarse)
                number = jnp.sum(matrix, axis=1, keepdims=True)
                sums = dot(matrix.astype(BF16), encoded[m * rows : (m + 1) * rows])
                pooled.append(sums / jnp.maximum(number, 1.0))
            x = dot(jnp.concatenate(pooled, axis=0).astype(BF16), cos[layer][...]).astype(BF16)

    decoded = encodes[3]
    for layer in range(3, -1, -1):
        rows, width = heights[layer], widths[layer]
        if layer < 3:
            coarse = heights[layer + 1]
            load(24 + layer).wait()
            mix = dot_nt if layer == 0 else dot
            lifted = mix(decoded, res[layer][...]).astype(BF16)
            ups = []
            for m in range(micro):
                at = base[layer] + m * rows
                matrix = one_hot(idx_t[at : at + rows, TAPS : TAPS + 1], coarse)
                ups.append(dot(matrix, lifted[m * coarse : (m + 1) * coarse]))
            decoded = (encodes[layer].astype(F32) + jnp.concatenate(ups, axis=0)).astype(BF16)

        @pl.when(phase == layer)
        def _():
            wide = decoded.astype(F32)
            for m in range(micro):
                own = wide[m * rows : (m + 1) * rows]
                if width < LANES:
                    small[...] = own
                    pack_d[pl.ds(m, rows // 2, stride=2), :] = jnp.concatenate(
                        [
                            small[pl.ds(0, rows // 2, stride=2), :],
                            small[pl.ds(1, rows // 2, stride=2), :],
                        ],
                        axis=1,
                    )
                else:
                    split = width // LANES
                    for h in range(split):
                        pack_d[pl.ds(2 * h + m, rows, stride=2 * split), :] = own[
                            :, h * LANES : (h + 1) * LANES
                        ]

    rank = lax.div(me, 2)

    @pl.when((phase == top) | (phase == aid))
    def _():
        swap_l.wait_recv()
        swap_r.wait_recv()
        pair_second()

        @pl.loop(0, half)
        def _(w):
            @pl.when(phase == aid)
            def _():
                block_copy(got_second, recv_second, w, rank).start()

            @pl.when((phase == top) & (w != rank))
            def _():
                block_copy(got_first, recv_first, w, rank).start()

    for j in range(chunks):
        dec_out[0, :, j * LANES : (j + 1) * LANES] = pack_d[2 * j : 2 * j + 2, :].astype(BF16)

    pack_g[...] = jnp.zeros(pack_g.shape, F32)

    def put_grad(layer, i, term):
        rows_here, width = term.shape
        term = term * (micro * replicas * heights[layer]) ** -0.5
        if width < LANES:
            small[0:rows_here, :] = term
            pack_g[pl.ds(i, rows_here // 2, stride=2), :] = jnp.concatenate(
                [
                    small[pl.ds(0, rows_here // 2, stride=2), :],
                    small[pl.ds(1, rows_here // 2, stride=2), :],
                ],
                axis=1,
            )
        else:
            split = width // LANES
            for h in range(split):
                pack_g[pl.ds(2 * h + i, rows_here, stride=2 * split), :] = term[
                    :, h * LANES : (h + 1) * LANES
                ]

    @pl.when(phase == helper)
    def _():
        mid_far(got_help, recv_help, 0).wait_send()

    @pl.when(phase == mid)
    def _():
        aim_copy.wait_send()
        group = group_of(mid)[1]

        @pl.when(group != 0)
        def _():
            mid_far(got2, recv_far, 0).wait_send()

        @pl.when(group == 0)
        def _():
            got2[0] = sum2[0]
            for i, (got, recv_sem) in enumerate(((got2, recv_far), (got_help, recv_help))):
                for sender in range(1 - i, mid_groups):
                    mid_far(got, recv_sem, sender).wait_recv()
                term = got[0].astype(F32)
                for sender in range(1, mid_groups):
                    term = term + got[sender].astype(F32)
                put_grad(mid, i, term)

    for layer in range(2):
        got = gots[layer]

        @pl.when(phase == layer)
        def _():
            owners, group, _ = group_of(layer)
            groups = replicas // owners

            @pl.when(group != 0)
            def _():
                far_copy(layer, group).wait_send()

            @pl.when(group == 0)
            def _():
                got[0] = sums_of[layer][0]
                for sender in range(1, groups):
                    far_copy(layer, sender).wait_recv()
                for i in range(2):
                    term = got[0, i].astype(F32)
                    for sender in range(1, groups):
                        term = term + got[sender, i].astype(F32)
                    put_grad(layer, i, term)

    @pl.when(phase == aid)
    def _():
        swap_l.wait_send()

        @pl.loop(0, half)
        def _(w):
            block_copy(got_second, recv_second, w, rank).wait_send()

    @pl.when(phase == top)
    def _():
        swap_l.wait_send()
        swap_r.wait_send()
        aim_send(0).wait_send()
        aim_send(1).wait_send()
        got_first[rank] = blocks[rank]

        def received(got, recv_sem, sender, own):
            @pl.when((sender != rank) | (not own))
            def _():
                block_copy(got, recv_sem, 0, sender).wait_recv()

            return got[sender].astype(F32)

        for i, (got, recv_sem) in enumerate(((got_second, recv_second), (got_first, recv_first))):
            first = functools.partial(received, got, recv_sem, own=i == 1)
            total = lax.fori_loop(1, half, lambda w, t: t + first(w), first(0)) if half > 8 else None
            if total is None:
                total = first(0)
                for w in range(1, half):
                    total = total + first(w)
            put_grad(top, 1 - i, total)

        @pl.loop(0, half)
        def _(w):
            @pl.when(w != rank)
            def _():
                block_copy(got_first, recv_first, w, rank).wait_send()

    for q in range(grad_out.shape[2] // LANES):
        grad_out[0, :, q * LANES : (q + 1) * LANES] = pack_g[2 * q : 2 * q + 2, :]


def deliver(dec_in, grad_in, dec_out, grad_out, sem):
    copies = [
        pltpu.make_async_copy(grad_in, grad_out, sem.at[0]),
        pltpu.make_async_copy(dec_in, dec_out, sem.at[1]),
    ]
    for copy in copies:
        copy.start()
    for copy in copies:
        copy.wait()


def on_device(*arrays):
    features, kms, dws = arrays[0], arrays[2:6], arrays[9:13]
    arrays = list(arrays)
    arrays[1] = arrays[1].T
    arrays[2:6] = [jnp.transpose(km, (1, 0, 2)) for km in kms]
    arrays[24] = arrays[24].T
    widths = [taps.shape[1] for taps in dws]
    heights = [km.shape[2] for km in kms]
    micro, elements = features.shape
    replicas = lax.axis_size("dp")
    owned = widths[3] * widths[3] // replicas

    def narrow(rows):
        return BF16 if rows % 16 == 0 else F32

    parts, gots, nears, sums_of = [], [], [], []
    for layer in range(3):
        rows_here = min(widths[layer], owned // widths[layer])
        owners = widths[layer] // rows_here
        kind = narrow(rows_here)
        if layer == 2:
            shape = (rows_here, widths[2])
            for held, first in ((parts, owners), (gots, replicas // owners), (nears, owners), (sums_of, 1)):
                held.append(pltpu.VMEM((first, *shape), kind))
            break
        parts.append(pltpu.VMEM((owners, 2, rows_here, widths[layer]), kind))
        gots.append(pltpu.VMEM((replicas // owners, 2, rows_here, widths[layer]), kind))
        nears.append(pltpu.VMEM((owners, 2, rows_here, widths[layer]), kind))
        sums_of.append(pltpu.VMEM((1, 2, rows_here, widths[layer]), kind))
    top_rows = owned // widths[3]
    span = micro * heights[3]
    idx_lanes = -(-micro * sum(heights) // LANES) * LANES
    sem = pltpu.SemaphoreType.DMA((replicas,))
    scratch = [
        *[pltpu.VMEM(a.shape, a.dtype) for a in arrays],
        pltpu.SemaphoreType.DMA((len(arrays),)),
        pltpu.VMEM((2 * elements // LANES, LANES), F32),
        pltpu.VMEM((2 * elements // LANES, LANES), F32),
        pltpu.VMEM((2 * elements // LANES, LANES), F32),
        pltpu.VMEM((2 * owned // LANES, LANES), F32),
        pltpu.VMEM((heights[0], widths[0]), F32),
        pltpu.VMEM((-(-heights[0] // LANES), 2 * IDX_ROWS, LANES), F32),
        pltpu.VMEM((IDX_ROWS, idx_lanes), F32),
        pltpu.VMEM((idx_lanes, IDX_ROWS), F32),
        *parts,
        *gots,
        *nears,
        *sums_of,
        *[sem] * 4,
        pltpu.VMEM((2, micro * heights[2], widths[2]), BF16),
        gots[2],
        *[sem] * 7,
        pltpu.VMEM((1, span, widths[3]), BF16),
        pltpu.VMEM((2, span, widths[3]), BF16),
        pltpu.VMEM((2, span, widths[3]), BF16),
        pltpu.VMEM((replicas // 2 * top_rows, widths[3]), F32),
        *[pltpu.VMEM((replicas // 2, top_rows, widths[3]), narrow(top_rows))] * 3,
        *[sem] * 8,
    ]
    held = pl.pallas_call(
        functools.partial(kernel, replicas, heights, widths, micro, len(arrays)),
        out_shape=(
            pltpu.VMEM((1, micro, elements), BF16),
            pltpu.VMEM((1, 2, owned), F32),
        ),
        in_specs=[pl.BlockSpec(memory_space=pltpu.HBM)] * len(arrays),
        out_specs=[pl.BlockSpec(memory_space=pltpu.VMEM)] * 2,
        scratch_shapes=scratch,
        compiler_params=pltpu.CompilerParams(
            collective_id=0, has_side_effects=True, vmem_limit_bytes=64 * 1024 * 1024 - 512 * 1024
        ),
    )(*arrays)
    return pl.pallas_call(
        deliver,
        out_shape=(
            jax.ShapeDtypeStruct((1, micro, elements), BF16),
            jax.ShapeDtypeStruct((1, 2, owned), F32),
        ),
        in_specs=[pl.BlockSpec(memory_space=pltpu.VMEM)] * 2,
        out_specs=[pl.BlockSpec(memory_space=pltpu.HBM)] * 2,
        scratch_shapes=[pltpu.SemaphoreType.DMA((2,))],
        compiler_params=pltpu.CompilerParams(vmem_limit_bytes=1024 * 1024),
    )(*[pltpu.with_memory_space_constraint(a, pltpu.VMEM) for a in held])


def solution(mesh):
    placed = (
        (P(None, "dp"), P(None, "dp"))
        + (P(None, None, "dp"),) * 4
        + (P(None, "dp"),) * 3
        + (P(),) * 18
        + (P("phase", None, "dp"),)
    )
    return jax.shard_map(
        on_device,
        mesh=mesh,
        in_specs=placed,
        out_specs=(P("phase", None, "dp"), P("phase", None, "dp")),
        check_vma=False,
    )
```

```python
import functools
import math

import jax
import jax.numpy as jnp
from jax import lax
from jax.experimental import pallas as pl
from jax.experimental.pallas import tpu as pltpu
from jax.sharding import PartitionSpec as P

LANES = 128
TAPS = 27
IDX_ROWS = 32
BATCH = 9
F32 = jnp.float32
BF16 = jnp.bfloat16
MESH = pl.DeviceIdType.MESH
GELU_A = math.sqrt(2.0 / math.pi)
GELU_B = 0.044715


def dot(a, b):
    return lax.dot_general(a, b, (((1,), (0,)), ((), ())), preferred_element_type=F32)


def dot_nt(a, b):
    return lax.dot_general(a, b, (((1,), (1,)), ((), ())), preferred_element_type=F32)


def dot_tn(a, b):
    return lax.dot_general(a, b, (((0,), (0,)), ((), ())), preferred_element_type=F32)


def one_hot(column, width):
    lanes = lax.broadcasted_iota(jnp.int32, (column.shape[0], width), 1).astype(F32)
    return jnp.where(column == lanes, 1.0, 0.0).astype(BF16)


def pool_matrix(parent_row, coarse):
    rows = lax.broadcasted_iota(jnp.int32, (coarse, parent_row.shape[1]), 0)
    return jnp.where(rows == parent_row, 1.0, 0.0).astype(F32)


def kernel(replicas, heights, widths, micro, count, *refs):
    sources, (dec_out, grad_out) = refs[:count], refs[count : count + 2]
    held, refs = refs[count + 2 : 2 * count + 2], refs[2 * count + 2 :]
    (
        load_sem,
        pack_f,
        pack_c,
        pack_d,
        pack_g,
        small,
        idx_raw,
        idx,
        idx_t,
        part0,
        part1,
        part2,
        got0,
        got1,
        got2,
        near0,
        near1,
        sum0,
        sum1,
        cot_all,
        slope_all,
        cols_send,
        cols_all,
        send_part,
        recv_part,
        send_cot,
        recv_cot,
        send_slope,
        recv_slope,
        send_cols,
        recv_cols,
        send_near,
        recv_near,
        aim_mid,
        got_help,
        send_aim,
        recv_aim,
        send_mid,
        recv_mid,
        recv_help,
        aim_top,
        send_top,
        recv_top,
        send_front,
        recv_front,
    ) = refs
    nears, sums_of = (near0, near1), (sum0, sum1)
    features, counts, cot = held[0], held[1], held[27]
    kms, pms, dws = held[2:6], held[6:9], held[9:13]
    fws, sws = held[13:17], held[17:21]
    cos, res = held[21:24], held[24:27]
    parts, gots = (part0, part1, part2), (got0, got1, got2)
    phase = lax.axis_index("phase")
    me = lax.axis_index("dp")
    chunks = features.shape[1] // LANES

    def peer(offset):
        return {"phase": phase, "dp": lax.rem(me + offset, replicas)}

    def load(i):
        return pltpu.make_async_copy(sources[i], held[i], load_sem.at[i])

    order = [0, 27, 2, 3, 4, 5, 6, 7, 8, 1, 9, 13, 17, 21, 10, 14, 18, 22, 11, 15, 19, 23, 12, 16, 20]
    for i in order + [26, 25, 24]:
        load(i).start()

    mid, helper, aid = 2, 0, 1
    cut = cot_all.shape[1] // 2
    barrier = pltpu.get_barrier_semaphore()

    @pl.loop(1, replicas)
    def _(offset):
        pl.semaphore_signal(barrier, inc=1, device_id=peer(offset), device_id_type=MESH)

    mid_owners = part2.shape[0]

    @pl.when(phase == helper)
    def _():
        pl.semaphore_signal(barrier, inc=1, device_id={"phase": mid, "dp": me}, device_id_type=MESH)

    @pl.when((phase == mid) & (me < mid_owners))
    def _():
        @pl.loop(0, replicas)
        def _(to):
            pl.semaphore_signal(
                barrier, inc=1, device_id={"phase": helper, "dp": to}, device_id_type=MESH
            )

    @pl.when(phase == aid)
    def _():
        pl.semaphore_signal(barrier, inc=1, device_id={"phase": 3, "dp": me}, device_id_type=MESH)

    @pl.when(phase == 3)
    def _():
        @pl.loop(1, replicas)
        def _(offset):
            pl.semaphore_signal(
                barrier,
                inc=1,
                device_id={"phase": aid, "dp": lax.rem(me + offset, replicas)},
                device_id_type=MESH,
            )

    for i in (0, 27):
        load(i).wait()

    for j in range(chunks):
        lanes = slice(j * LANES, (j + 1) * LANES)
        pack_f[2 * j : 2 * j + 2, :] = features[:, lanes].astype(F32)
        pack_c[2 * j : 2 * j + 2, :] = cot[0, :, lanes].astype(F32)

    def unpack(pack, layer, m):
        rows, width = heights[layer], widths[layer]
        if width < LANES:
            both = pack[pl.ds(m, rows // 2, stride=2), :]
            small[pl.ds(0, rows // 2, stride=2), :] = both[:, :width]
            small[pl.ds(1, rows // 2, stride=2), :] = both[:, width:]
            return small[...]
        split = width // LANES
        return jnp.concatenate(
            [pack[pl.ds(2 * h + m, rows, stride=2 * split), :] for h in range(split)], axis=1
        )

    def target(layer):
        return jnp.concatenate([unpack(pack_c, layer, m) for m in range(micro)], axis=0).astype(BF16)

    top = 3

    def top_copy(source, landing, send_sem, recv_sem, to, sender):
        return pltpu.make_async_remote_copy(
            src_ref=source,
            dst_ref=landing,
            send_sem=send_sem.at[to],
            recv_sem=recv_sem.at[sender],
            device_id={"phase": top, "dp": to},
            device_id_type=MESH,
        )

    def copy_cot(to, sender):
        return top_copy(cot_all.at[sender], cot_all.at[sender], send_cot, recv_cot, to, sender)

    def copy_cols(to, sender):
        return top_copy(cols_send.at[to], cols_all.at[sender], send_cols, recv_cols, to, sender)

    def copy_front(to, sender):
        rows = slope_all.at[sender, pl.ds(0, cut)]
        return top_copy(rows, rows, send_front, recv_front, to, sender)

    def copy_back(to, sender):
        rows = slope_all.at[sender, pl.ds(cut, cut)]
        return top_copy(rows, rows, send_slope, recv_slope, to, sender)

    top_aim = pltpu.make_async_remote_copy(
        src_ref=cot_all.at[me],
        dst_ref=aim_top.at[0],
        send_sem=send_top.at[0],
        recv_sem=recv_top.at[0],
        device_id={"phase": aid, "dp": me},
        device_id_type=MESH,
    )

    def others(body):
        @pl.loop(0, replicas)
        def _(other):
            @pl.when(other != me)
            def _():
                body(other)

    def group_of(layer):
        owners = parts[layer].shape[0]
        return owners, lax.div(me, owners), lax.rem(me, owners)

    def near_copy(layer, w, sender):
        owners, group, _ = group_of(layer)
        return pltpu.make_async_remote_copy(
            src_ref=parts[layer].at[w],
            dst_ref=nears[layer].at[sender],
            send_sem=send_near.at[w],
            recv_sem=recv_near.at[sender],
            device_id={"phase": phase, "dp": group * owners + w},
            device_id_type=MESH,
        )

    def far_copy(layer, group):
        return pltpu.make_async_remote_copy(
            src_ref=sums_of[layer].at[0],
            dst_ref=gots[layer].at[group],
            send_sem=send_part.at[0],
            recv_sem=recv_part.at[group],
            device_id={"phase": phase, "dp": group_of(layer)[2]},
            device_id_type=MESH,
        )

    @pl.when(phase == top)
    def _():
        cot_all[me] = target(top)

    @pl.when(phase == mid)
    def _():
        aim_mid[0] = target(mid)

    aim_copy = pltpu.make_async_remote_copy(
        src_ref=aim_mid.at[0],
        dst_ref=aim_mid.at[1],
        send_sem=send_aim.at[0],
        recv_sem=recv_aim.at[0],
        device_id={"phase": helper, "dp": me},
        device_id_type=MESH,
    )

    def mid_copy(got, recv_sem, w, sender):
        return pltpu.make_async_remote_copy(
            src_ref=part2.at[w],
            dst_ref=got.at[sender],
            send_sem=send_mid.at[w],
            recv_sem=recv_sem.at[sender],
            device_id={"phase": mid, "dp": w},
            device_id_type=MESH,
        )

    def mid_start(term, helping):
        rows_here = part2.shape[1]
        for w in range(mid_owners):
            part2[w] = term[w * rows_here : (w + 1) * rows_here].astype(part2.dtype)
        mid_each(lambda copy: copy.start(), helping)

    def mid_each(act, helping):
        for w in range(mid_owners):
            if helping:
                act(mid_copy(got_help, recv_help, w, me))
            else:

                @pl.when(me != w)
                def _():
                    act(mid_copy(got2, recv_mid, w, me))

    def top_cols(normed, active):
        both = jnp.concatenate([normed.astype(F32).T, active.astype(F32).T], axis=1).astype(cols_send.dtype)
        rows_here = cols_send.shape[1]
        for d in range(replicas):
            cols_send[d] = both[d * rows_here : (d + 1) * rows_here]

    for i in (2, 3, 4, 5, 6, 7, 8, 1):
        load(i).wait()
    idx[...] = jnp.full(idx.shape, -1.0, F32)
    base = []
    position = 0
    for layer in range(4):
        rows = heights[layer]
        base.append(position)
        pieces = [(at, min(LANES, rows - at)) for at in range(0, rows, LANES)]
        for k in range(TAPS):
            for piece, (at, span) in enumerate(pieces):
                idx_raw[piece, 2 * k : 2 * k + 2, 0:span] = kms[layer][k, :, at : at + span].astype(F32)
        for m in range(micro):
            at = position + m * rows
            values = jnp.concatenate(
                [
                    idx_raw.at[piece][pl.ds(m, TAPS, stride=2), :][:, :span]
                    for piece, (_, span) in enumerate(pieces)
                ],
                axis=1,
            )
            shift = m * rows if layer >= 2 else 0
            if shift:
                values = jnp.where(values < 0.0, values, values + float(shift))
            idx[0:TAPS, at : at + rows] = values
            if layer < 3:
                idx[TAPS : TAPS + 1, at : at + rows] = pms[layer][m : m + 1, :].astype(F32)
        position += micro * rows
    for j in range(idx.shape[1] // LANES):
        lanes = slice(j * LANES, (j + 1) * LANES)
        idx_t[lanes, :] = idx[:, lanes].T

    live = []
    for m in range(micro):
        block = unpack(pack_f, 0, m)
        site = lax.broadcasted_iota(jnp.int32, block.shape, 0)
        live.append(jnp.where(site < counts[:, m : m + 1], block, 0.0))
    x = jnp.concatenate(live, axis=0).astype(BF16)

    def pass_on(layer):
        part, near = parts[layer], nears[layer]

        @pl.when(phase == layer)
        def _():
            owners, group, member = group_of(layer)
            near[member] = part[member]
            for w in range(owners):

                @pl.when(member != w)
                def _():
                    near_copy(layer, w, member).wait_send()
                    near_copy(layer, w, w).wait_recv()

            for i in range(2):
                term = near[0, i].astype(F32)
                for w in range(1, owners):
                    term = term + near[w, i].astype(F32)
                sums_of[layer][0, i] = term.astype(near.dtype)

            @pl.when(group != 0)
            def _():
                far_copy(layer, group).start()

    @pl.when(phase == top)
    def _():
        pl.semaphore_wait(barrier, replicas)
        top_aim.start()
        others(lambda to: copy_cot(to, me).start())

    def bent(inner, bend, squared):
        return 0.5 * (1.0 + bend) + 0.5 * inner * (1.0 - bend * bend) * GELU_A * (
            1.0 + 3.0 * GELU_B * squared
        )

    encodes = []
    for layer in range(4):
        for i in (9 + layer, 13 + layer, 17 + layer) + ((21 + layer,) if layer < 3 else ()):
            load(i).wait()
        rows, width = heights[layer], widths[layer]
        group = rows if layer < 2 else micro * rows
        mixes = []
        for start in range(0, micro * rows, group):
            block = x[start : start + group]
            index = idx_t[base[layer] + start : base[layer] + start + group, :]
            mixed = jnp.zeros((group, width), F32)
            for first in range(0, TAPS, BATCH):
                hots = [one_hot(index[:, k : k + 1], group) for k in range(first, first + BATCH)]
                gathered = dot(jnp.concatenate(hots, axis=0), block)
                for k in range(BATCH):
                    tap = dws[layer][first + k : first + k + 1, :].astype(F32)
                    mixed = mixed + gathered[k * group : (k + 1) * group] * tap
            mixes.append(mixed)
        mixed = mixes[0] if len(mixes) == 1 else jnp.concatenate(mixes, axis=0)
        normed_f = mixed * lax.rsqrt(jnp.mean(mixed * mixed, axis=1, keepdims=True) + 1e-05)
        normed = normed_f.astype(BF16)
        inner = dot(normed, fws[layer][...])
        squared = inner * inner
        bend = jnp.tanh(GELU_A * inner * (1.0 + GELU_B * squared))
        active = (0.5 * inner * (1.0 + bend)).astype(BF16)
        encoded = (x.astype(F32) + dot(active, sws[layer][...])).astype(BF16)
        encodes.append(encoded)
        if layer == 0:
            for which, count in ((helper, replicas - 1 + mid_owners), (mid, replicas), (aid, 2 * replicas - 2)):

                @pl.when(phase == which)
                def _():
                    pl.semaphore_wait(barrier, count)

            @pl.when(phase == mid)
            def _():
                aim_copy.start()

        @pl.when(phase == layer)
        def _():
            aim = target(layer) if layer < mid else (aim_mid[0] if layer == mid else cot_all[me])
            backward = dot_nt(aim, sws[layer][...])
            slope = (bent(inner, bend, squared) * backward).astype(BF16)
            if layer == top:
                slope_all[me] = slope
                others(lambda to: copy_back(to, me).start())
                top_cols(normed, active)
                cols_all[me] = cols_send[me]
            elif layer == mid:
                mid_start(dot_tn(normed, slope), False)
            else:
                part = parts[layer]
                owners, _, rows_here, _ = part.shape
                for i, term in enumerate((dot_tn(normed, slope), dot_tn(active, aim))):
                    for w in range(owners):
                        part[w, i] = term[w * rows_here : (w + 1) * rows_here].astype(part.dtype)
                for w in range(owners):

                    @pl.when(group_of(layer)[2] != w)
                    def _():
                        near_copy(layer, w, group_of(layer)[2]).start()

        if layer == mid:

            @pl.when(phase == helper)
            def _():
                aim_copy.wait_recv()
                mid_start(dot_tn(active, aim_mid[1]), True)

        if layer == top:

            @pl.when(phase == aid)
            def _():
                top_cols(normed, active)
                others(lambda to: copy_cols(to, me).start())
                top_aim.wait_recv()
                backward = dot_nt(aim_top[0, 0:cut], sws[layer][...])
                front = bent(inner[0:cut], bend[0:cut], squared[0:cut]) * backward
                slope_all[me, 0:cut] = front.astype(BF16)
                others(lambda to: copy_front(to, me).start())

        elif layer > 0:
            pass_on(layer - 1)

        if layer < 3:
            coarse = heights[layer + 1]
            pooled = []
            for m in range(micro):
                matrix = pool_matrix(pms[layer][m : m + 1, :], coarse)
                number = jnp.sum(matrix, axis=1, keepdims=True)
                sums = dot(matrix.astype(BF16), encoded[m * rows : (m + 1) * rows])
                pooled.append(sums / jnp.maximum(number, 1.0))
            x = dot(jnp.concatenate(pooled, axis=0).astype(BF16), cos[layer][...]).astype(BF16)

    decoded = encodes[3]
    for layer in range(3, -1, -1):
        rows, width = heights[layer], widths[layer]
        if layer < 3:
            coarse = heights[layer + 1]
            load(24 + layer).wait()
            mix = dot_nt if layer == 0 else dot
            lifted = mix(decoded, res[layer][...]).astype(BF16)
            ups = []
            for m in range(micro):
                at = base[layer] + m * rows
                matrix = one_hot(idx_t[at : at + rows, TAPS : TAPS + 1], coarse)
                ups.append(dot(matrix, lifted[m * coarse : (m + 1) * coarse]))
            decoded = (encodes[layer].astype(F32) + jnp.concatenate(ups, axis=0)).astype(BF16)

        @pl.when(phase == layer)
        def _():
            wide = decoded.astype(F32)
            for m in range(micro):
                own = wide[m * rows : (m + 1) * rows]
                if width < LANES:
                    small[...] = own
                    pack_d[pl.ds(m, rows // 2, stride=2), :] = jnp.concatenate(
                        [
                            small[pl.ds(0, rows // 2, stride=2), :],
                            small[pl.ds(1, rows // 2, stride=2), :],
                        ],
                        axis=1,
                    )
                else:
                    split = width // LANES
                    for h in range(split):
                        pack_d[pl.ds(2 * h + m, rows, stride=2 * split), :] = own[
                            :, h * LANES : (h + 1) * LANES
                        ]

    for j in range(chunks):
        dec_out[0, :, j * LANES : (j + 1) * LANES] = pack_d[2 * j : 2 * j + 2, :].astype(BF16)

    pack_g[...] = jnp.zeros(pack_g.shape, F32)

    def put_grad(layer, i, term):
        rows_here, width = term.shape
        term = term * (micro * replicas * heights[layer]) ** -0.5
        if width < LANES:
            small[0:rows_here, :] = term
            pack_g[pl.ds(i, rows_here // 2, stride=2), :] = jnp.concatenate(
                [
                    small[pl.ds(0, rows_here // 2, stride=2), :],
                    small[pl.ds(1, rows_here // 2, stride=2), :],
                ],
                axis=1,
            )
        else:
            split = width // LANES
            for h in range(split):
                pack_g[pl.ds(2 * h + i, rows_here, stride=2 * split), :] = term[
                    :, h * LANES : (h + 1) * LANES
                ]

    @pl.when(phase == helper)
    def _():
        mid_each(lambda copy: copy.wait_send(), True)

    @pl.when(phase == aid)
    def _():
        @others
        def _(to):
            copy_cols(to, me).wait_send()
            copy_front(to, me).wait_send()

    @pl.when(phase == mid)
    def _():
        aim_copy.wait_send()
        mid_each(lambda copy: copy.wait_send(), False)

        @pl.when(me < mid_owners)
        def _():
            got2[me] = part2[me]

            def received(got, recv_sem, sender):
                if recv_sem is recv_help:
                    mid_copy(got, recv_sem, 0, sender).wait_recv()
                else:

                    @pl.when(sender != me)
                    def _():
                        mid_copy(got, recv_sem, 0, sender).wait_recv()

                return got[sender].astype(F32)

            for i, (got, recv_sem) in enumerate(((got2, recv_mid), (got_help, recv_help))):
                total = received(got, recv_sem, 0)
                if replicas <= 16:
                    for sender in range(1, replicas):
                        total = total + received(got, recv_sem, sender)
                else:
                    total = lax.fori_loop(
                        1, replicas, lambda s, t: t + received(got, recv_sem, s), total
                    )
                put_grad(mid, i, total)

    for layer in range(2):
        got = gots[layer]

        @pl.when(phase == layer)
        def _():
            owners, group, _ = group_of(layer)
            groups = replicas // owners

            @pl.when(group != 0)
            def _():
                far_copy(layer, group).wait_send()

            @pl.when(group == 0)
            def _():
                got[0] = sums_of[layer][0]
                for sender in range(1, groups):
                    far_copy(layer, sender).wait_recv()
                for i in range(2):
                    term = got[0, i].astype(F32)
                    for sender in range(1, groups):
                        term = term + got[sender, i].astype(F32)
                    put_grad(layer, i, term)

    @pl.when(phase == top)
    def _():
        span = micro * heights[top]

        def terms(sender):
            @pl.when(sender != me)
            def _():
                copy_cot(me, sender).wait_recv()
                copy_cols(me, sender).wait_recv()
                copy_front(me, sender).wait_recv()
                copy_back(me, sender).wait_recv()

            cols = cols_all[sender].astype(BF16)
            return (
                dot(cols[:, :span], slope_all[sender]),
                dot(cols[:, span:], cot_all[sender]),
            )

        total = terms(0)
        if replicas <= 16:
            for sender in range(1, replicas):
                total = jax.tree.map(jnp.add, total, terms(sender))
        else:
            total = lax.fori_loop(
                1, replicas, lambda s, t: jax.tree.map(jnp.add, t, terms(s)), total
            )
        for i in range(2):
            put_grad(top, i, total[i])

        @others
        def _(to):
            copy_cot(to, me).wait_send()
            copy_back(to, me).wait_send()

        top_aim.wait_send()


    for q in range(grad_out.shape[2] // LANES):
        grad_out[0, :, q * LANES : (q + 1) * LANES] = pack_g[2 * q : 2 * q + 2, :]


def deliver(dec_in, grad_in, dec_out, grad_out, sem):
    copies = [
        pltpu.make_async_copy(grad_in, grad_out, sem.at[0]),
        pltpu.make_async_copy(dec_in, dec_out, sem.at[1]),
    ]
    for copy in copies:
        copy.start()
    for copy in copies:
        copy.wait()


def on_device(*arrays):
    features, kms, dws = arrays[0], arrays[2:6], arrays[9:13]
    arrays = list(arrays)
    arrays[1] = arrays[1].T
    arrays[2:6] = [jnp.transpose(km, (1, 0, 2)) for km in kms]
    arrays[24] = arrays[24].T
    widths = [taps.shape[1] for taps in dws]
    heights = [km.shape[2] for km in kms]
    micro, elements = features.shape
    replicas = lax.axis_size("dp")
    owned = widths[3] * widths[3] // replicas

    def narrow(rows):
        return BF16 if rows % 16 == 0 else F32

    parts, gots, nears, sums_of = [], [], [], []
    for layer in range(3):
        rows_here = min(widths[layer], owned // widths[layer])
        owners = widths[layer] // rows_here
        kind = narrow(rows_here)
        if layer == 2:
            shape = (rows_here, widths[2])
            parts.append(pltpu.VMEM((owners, *shape), kind))
            gots.append(pltpu.VMEM((replicas, *shape), kind))
            break
        parts.append(pltpu.VMEM((owners, 2, rows_here, widths[layer]), kind))
        gots.append(pltpu.VMEM((replicas // owners, 2, rows_here, widths[layer]), kind))
        nears.append(pltpu.VMEM((owners, 2, rows_here, widths[layer]), kind))
        sums_of.append(pltpu.VMEM((1, 2, rows_here, widths[layer]), kind))
    top_rows = owned // widths[3]
    span = micro * heights[3]
    idx_lanes = -(-micro * sum(heights) // LANES) * LANES
    sem = pltpu.SemaphoreType.DMA((replicas,))
    scratch = [
        *[pltpu.VMEM(a.shape, a.dtype) for a in arrays],
        pltpu.SemaphoreType.DMA((len(arrays),)),
        pltpu.VMEM((2 * elements // LANES, LANES), F32),
        pltpu.VMEM((2 * elements // LANES, LANES), F32),
        pltpu.VMEM((2 * elements // LANES, LANES), F32),
        pltpu.VMEM((2 * owned // LANES, LANES), F32),
        pltpu.VMEM((heights[0], widths[0]), F32),
        pltpu.VMEM((-(-heights[0] // LANES), 2 * IDX_ROWS, LANES), F32),
        pltpu.VMEM((IDX_ROWS, idx_lanes), F32),
        pltpu.VMEM((idx_lanes, IDX_ROWS), F32),
        *parts,
        *gots,
        *nears,
        *sums_of,
        pltpu.VMEM((replicas, span, widths[3]), BF16),
        pltpu.VMEM((replicas, span, widths[3]), BF16),
        pltpu.VMEM((replicas, top_rows, 2 * span), narrow(top_rows)),
        pltpu.VMEM((replicas, top_rows, 2 * span), narrow(top_rows)),
        *[sem] * 10,
        pltpu.VMEM((2, micro * heights[2], widths[2]), BF16),
        gots[2],
        *[sem] * 5,
        pltpu.VMEM((1, span, widths[3]), BF16),
        *[sem] * 4,
    ]
    held = pl.pallas_call(
        functools.partial(kernel, replicas, heights, widths, micro, len(arrays)),
        out_shape=(
            pltpu.VMEM((1, micro, elements), BF16),
            pltpu.VMEM((1, 2, owned), F32),
        ),
        in_specs=[pl.BlockSpec(memory_space=pltpu.HBM)] * len(arrays),
        out_specs=[pl.BlockSpec(memory_space=pltpu.VMEM)] * 2,
        scratch_shapes=scratch,
        compiler_params=pltpu.CompilerParams(
            collective_id=0, has_side_effects=True, vmem_limit_bytes=64 * 1024 * 1024 - 512 * 1024
        ),
    )(*arrays)
    return pl.pallas_call(
        deliver,
        out_shape=(
            jax.ShapeDtypeStruct((1, micro, elements), BF16),
            jax.ShapeDtypeStruct((1, 2, owned), F32),
        ),
        in_specs=[pl.BlockSpec(memory_space=pltpu.VMEM)] * 2,
        out_specs=[pl.BlockSpec(memory_space=pltpu.HBM)] * 2,
        scratch_shapes=[pltpu.SemaphoreType.DMA((2,))],
        compiler_params=pltpu.CompilerParams(vmem_limit_bytes=1024 * 1024),
    )(*[pltpu.with_memory_space_constraint(a, pltpu.VMEM) for a in held])


def solution(mesh):
    placed = (
        (P(None, "dp"), P(None, "dp"))
        + (P(None, None, "dp"),) * 4
        + (P(None, "dp"),) * 3
        + (P(),) * 18
        + (P("phase", None, "dp"),)
    )
    return jax.shard_map(
        on_device,
        mesh=mesh,
        in_specs=placed,
        out_specs=(P("phase", None, "dp"), P("phase", None, "dp")),
        check_vma=False,
    )
```

```python
import functools
import math

import jax
import jax.numpy as jnp
from jax import lax
from jax.experimental import pallas as pl
from jax.experimental.pallas import tpu as pltpu
from jax.sharding import PartitionSpec as P

LANES = 128
TAPS = 27
IDX_ROWS = 32
BATCH = 9
F32 = jnp.float32
BF16 = jnp.bfloat16
MESH = pl.DeviceIdType.MESH
GELU_A = math.sqrt(2.0 / math.pi)
GELU_B = 0.044715


def dot(a, b):
    return lax.dot_general(a, b, (((1,), (0,)), ((), ())), preferred_element_type=F32)


def dot_nt(a, b):
    return lax.dot_general(a, b, (((1,), (1,)), ((), ())), preferred_element_type=F32)


def dot_tn(a, b):
    return lax.dot_general(a, b, (((0,), (0,)), ((), ())), preferred_element_type=F32)


def one_hot(column, width):
    lanes = lax.broadcasted_iota(jnp.int32, (column.shape[0], width), 1).astype(F32)
    return jnp.where(column == lanes, 1.0, 0.0).astype(BF16)


def pool_matrix(parent_row, coarse):
    rows = lax.broadcasted_iota(jnp.int32, (coarse, parent_row.shape[1]), 0)
    return jnp.where(rows == parent_row, 1.0, 0.0).astype(F32)


def kernel(replicas, heights, widths, micro, count, *refs):
    sources, (dec_out, grad_out) = refs[:count], refs[count : count + 2]
    held, refs = refs[count + 2 : 2 * count + 2], refs[2 * count + 2 :]
    (
        load_sem,
        pack_f,
        pack_c,
        pack_d,
        pack_g,
        small,
        idx_raw,
        idx,
        idx_t,
        part0,
        part1,
        part2,
        got0,
        got1,
        got2,
        near0,
        near1,
        near2,
        sum0,
        sum1,
        sum2,
        cot_all,
        slope_all,
        cols_send,
        cols_all,
        send_part,
        recv_part,
        send_cot,
        recv_cot,
        send_slope,
        recv_slope,
        send_cols,
        recv_cols,
        send_near,
        recv_near,
        aim_mid,
        got_help,
        send_aim,
        recv_aim,
        send_mid,
        recv_mid,
        send_far,
        recv_far,
        recv_help,
        aim_top,
        send_top,
        recv_top,
        send_front,
        recv_front,
    ) = refs
    nears, sums_of = (near0, near1, near2), (sum0, sum1, sum2)
    features, counts, cot = held[0], held[1], held[27]
    kms, pms, dws = held[2:6], held[6:9], held[9:13]
    fws, sws = held[13:17], held[17:21]
    cos, res = held[21:24], held[24:27]
    parts, gots = (part0, part1, part2), (got0, got1, got2)
    phase = lax.axis_index("phase")
    me = lax.axis_index("dp")
    chunks = features.shape[1] // LANES

    def peer(offset):
        return {"phase": phase, "dp": lax.rem(me + offset, replicas)}

    def load(i):
        return pltpu.make_async_copy(sources[i], held[i], load_sem.at[i])

    order = [0, 27, 2, 3, 4, 5, 6, 7, 8, 1, 9, 13, 17, 21, 10, 14, 18, 22, 11, 15, 19, 23, 12, 16, 20]
    for i in order + [26, 25, 24]:
        load(i).start()

    mid, helper, aid = 2, 0, 1
    cut = cot_all.shape[1] // 4
    barrier = pltpu.get_barrier_semaphore()

    @pl.loop(1, replicas)
    def _(offset):
        pl.semaphore_signal(barrier, inc=1, device_id=peer(offset), device_id_type=MESH)

    mid_owners = part2.shape[0]
    mid_groups = replicas // mid_owners

    @pl.when(phase == helper)
    def _():
        pl.semaphore_signal(barrier, inc=1, device_id={"phase": mid, "dp": me}, device_id_type=MESH)

    @pl.when((phase == mid) & (me < mid_owners))
    def _():
        @pl.loop(0, mid_groups)
        def _(group):
            pl.semaphore_signal(
                barrier,
                inc=1,
                device_id={"phase": helper, "dp": group * mid_owners + me},
                device_id_type=MESH,
            )

    @pl.when(phase == aid)
    def _():
        pl.semaphore_signal(barrier, inc=1, device_id={"phase": 3, "dp": me}, device_id_type=MESH)

    @pl.when(phase == 3)
    def _():
        @pl.loop(1, replicas)
        def _(offset):
            pl.semaphore_signal(
                barrier,
                inc=1,
                device_id={"phase": aid, "dp": lax.rem(me + offset, replicas)},
                device_id_type=MESH,
            )

    for i in (0, 27):
        load(i).wait()

    for j in range(chunks):
        lanes = slice(j * LANES, (j + 1) * LANES)
        pack_f[2 * j : 2 * j + 2, :] = features[:, lanes].astype(F32)
        pack_c[2 * j : 2 * j + 2, :] = cot[0, :, lanes].astype(F32)

    def unpack(pack, layer, m):
        rows, width = heights[layer], widths[layer]
        if width < LANES:
            both = pack[pl.ds(m, rows // 2, stride=2), :]
            small[pl.ds(0, rows // 2, stride=2), :] = both[:, :width]
            small[pl.ds(1, rows // 2, stride=2), :] = both[:, width:]
            return small[...]
        split = width // LANES
        return jnp.concatenate(
            [pack[pl.ds(2 * h + m, rows, stride=2 * split), :] for h in range(split)], axis=1
        )

    def target(layer):
        return jnp.concatenate([unpack(pack_c, layer, m) for m in range(micro)], axis=0).astype(BF16)

    top = 3

    def top_copy(source, landing, send_sem, recv_sem, to, sender):
        return pltpu.make_async_remote_copy(
            src_ref=source,
            dst_ref=landing,
            send_sem=send_sem.at[to],
            recv_sem=recv_sem.at[sender],
            device_id={"phase": top, "dp": to},
            device_id_type=MESH,
        )

    def copy_cot(to, sender):
        return top_copy(cot_all.at[sender], cot_all.at[sender], send_cot, recv_cot, to, sender)

    def copy_cols(to, sender):
        return top_copy(cols_send.at[to], cols_all.at[sender], send_cols, recv_cols, to, sender)

    def copy_front(to, sender):
        rows = slope_all.at[sender, pl.ds(0, cut)]
        return top_copy(rows, rows, send_front, recv_front, to, sender)

    def copy_back(to, sender):
        rows = slope_all.at[sender, pl.ds(cut, cot_all.shape[1] - cut)]
        return top_copy(rows, rows, send_slope, recv_slope, to, sender)

    top_aim = pltpu.make_async_remote_copy(
        src_ref=cot_all.at[me],
        dst_ref=aim_top.at[0],
        send_sem=send_top.at[0],
        recv_sem=recv_top.at[0],
        device_id={"phase": aid, "dp": me},
        device_id_type=MESH,
    )

    def others(body):
        @pl.loop(0, replicas)
        def _(other):
            @pl.when(other != me)
            def _():
                body(other)

    def group_of(layer):
        owners = parts[layer].shape[0]
        return owners, lax.div(me, owners), lax.rem(me, owners)

    def near_copy(layer, w, sender):
        owners, group, _ = group_of(layer)
        return pltpu.make_async_remote_copy(
            src_ref=parts[layer].at[w],
            dst_ref=nears[layer].at[sender],
            send_sem=send_near.at[w],
            recv_sem=recv_near.at[sender],
            device_id={"phase": phase, "dp": group * owners + w},
            device_id_type=MESH,
        )

    def far_copy(layer, group):
        return pltpu.make_async_remote_copy(
            src_ref=sums_of[layer].at[0],
            dst_ref=gots[layer].at[group],
            send_sem=send_part.at[0],
            recv_sem=recv_part.at[group],
            device_id={"phase": phase, "dp": group_of(layer)[2]},
            device_id_type=MESH,
        )

    @pl.when(phase == top)
    def _():
        cot_all[me] = target(top)

    @pl.when(phase == mid)
    def _():
        aim_mid[0] = target(mid)

    aim_copy = pltpu.make_async_remote_copy(
        src_ref=aim_mid.at[0],
        dst_ref=aim_mid.at[1],
        send_sem=send_aim.at[0],
        recv_sem=recv_aim.at[0],
        device_id={"phase": helper, "dp": me},
        device_id_type=MESH,
    )

    def mid_near(w, sender):
        _, group, _ = group_of(mid)
        return pltpu.make_async_remote_copy(
            src_ref=part2.at[w],
            dst_ref=near2.at[sender],
            send_sem=send_mid.at[w],
            recv_sem=recv_mid.at[sender],
            device_id={"phase": phase, "dp": group * mid_owners + w},
            device_id_type=MESH,
        )

    def mid_far(got, recv_sem, group):
        return pltpu.make_async_remote_copy(
            src_ref=sum2.at[0],
            dst_ref=got.at[group],
            send_sem=send_far.at[0],
            recv_sem=recv_sem.at[group],
            device_id={"phase": mid, "dp": group_of(mid)[2]},
            device_id_type=MESH,
        )

    def mid_start(term):
        rows_here = part2.shape[1]
        member = group_of(mid)[2]
        for w in range(mid_owners):
            part2[w] = term[w * rows_here : (w + 1) * rows_here].astype(part2.dtype)
        for w in range(mid_owners):

            @pl.when(member != w)
            def _():
                mid_near(w, member).start()

    def mid_pass():
        @pl.when((phase == mid) | (phase == helper))
        def _():
            _, group, member = group_of(mid)
            near2[member] = part2[member]
            for w in range(mid_owners):

                @pl.when(member != w)
                def _():
                    mid_near(w, member).wait_send()
                    mid_near(w, w).wait_recv()

            term = near2[0].astype(F32)
            for w in range(1, mid_owners):
                term = term + near2[w].astype(F32)
            sum2[0] = term.astype(near2.dtype)

            @pl.when(phase == helper)
            def _():
                mid_far(got_help, recv_help, group).start()

            @pl.when((phase == mid) & (group != 0))
            def _():
                mid_far(got2, recv_far, group).start()

    def top_cols(normed, active):
        both = jnp.concatenate([normed.astype(F32).T, active.astype(F32).T], axis=1).astype(cols_send.dtype)
        rows_here = cols_send.shape[1]
        for d in range(replicas):
            cols_send[d] = both[d * rows_here : (d + 1) * rows_here]

    for i in (2, 3, 4, 5, 6, 7, 8, 1):
        load(i).wait()
    idx[...] = jnp.full(idx.shape, -1.0, F32)
    base = []
    position = 0
    for layer in range(4):
        rows = heights[layer]
        base.append(position)
        pieces = [(at, min(LANES, rows - at)) for at in range(0, rows, LANES)]
        for k in range(TAPS):
            for piece, (at, span) in enumerate(pieces):
                idx_raw[piece, 2 * k : 2 * k + 2, 0:span] = kms[layer][k, :, at : at + span].astype(F32)
        for m in range(micro):
            at = position + m * rows
            values = jnp.concatenate(
                [
                    idx_raw.at[piece][pl.ds(m, TAPS, stride=2), :][:, :span]
                    for piece, (_, span) in enumerate(pieces)
                ],
                axis=1,
            )
            shift = m * rows if layer >= 2 else 0
            if shift:
                values = jnp.where(values < 0.0, values, values + float(shift))
            idx[0:TAPS, at : at + rows] = values
            if layer < 3:
                idx[TAPS : TAPS + 1, at : at + rows] = pms[layer][m : m + 1, :].astype(F32)
        position += micro * rows
    for j in range(idx.shape[1] // LANES):
        lanes = slice(j * LANES, (j + 1) * LANES)
        idx_t[lanes, :] = idx[:, lanes].T

    live = []
    for m in range(micro):
        block = unpack(pack_f, 0, m)
        site = lax.broadcasted_iota(jnp.int32, block.shape, 0)
        live.append(jnp.where(site < counts[:, m : m + 1], block, 0.0))
    x = jnp.concatenate(live, axis=0).astype(BF16)

    def pass_on(layer):
        part, near = parts[layer], nears[layer]

        @pl.when(phase == layer)
        def _():
            owners, group, member = group_of(layer)
            near[member] = part[member]
            for w in range(owners):

                @pl.when(member != w)
                def _():
                    near_copy(layer, w, member).wait_send()
                    near_copy(layer, w, w).wait_recv()

            for i in range(2):
                term = near[0, i].astype(F32)
                for w in range(1, owners):
                    term = term + near[w, i].astype(F32)
                sums_of[layer][0, i] = term.astype(near.dtype)

            @pl.when(group != 0)
            def _():
                far_copy(layer, group).start()

    @pl.when(phase == top)
    def _():
        pl.semaphore_wait(barrier, replicas)
        top_aim.start()
        others(lambda to: copy_cot(to, me).start())

    def bent(inner, bend, squared):
        return 0.5 * (1.0 + bend) + 0.5 * inner * (1.0 - bend * bend) * GELU_A * (
            1.0 + 3.0 * GELU_B * squared
        )

    encodes = []
    for layer in range(4):
        for i in (9 + layer, 13 + layer, 17 + layer) + ((21 + layer,) if layer < 3 else ()):
            load(i).wait()
        rows, width = heights[layer], widths[layer]
        group = rows if layer < 2 else micro * rows
        mixes = []
        for start in range(0, micro * rows, group):
            block = x[start : start + group]
            index = idx_t[base[layer] + start : base[layer] + start + group, :]
            mixed = jnp.zeros((group, width), F32)
            for first in range(0, TAPS, BATCH):
                hots = [one_hot(index[:, k : k + 1], group) for k in range(first, first + BATCH)]
                gathered = dot(jnp.concatenate(hots, axis=0), block)
                for k in range(BATCH):
                    tap = dws[layer][first + k : first + k + 1, :].astype(F32)
                    mixed = mixed + gathered[k * group : (k + 1) * group] * tap
            mixes.append(mixed)
        mixed = mixes[0] if len(mixes) == 1 else jnp.concatenate(mixes, axis=0)
        normed_f = mixed * lax.rsqrt(jnp.mean(mixed * mixed, axis=1, keepdims=True) + 1e-05)
        normed = normed_f.astype(BF16)
        inner = dot(normed, fws[layer][...])
        squared = inner * inner
        bend = jnp.tanh(GELU_A * inner * (1.0 + GELU_B * squared))
        active = (0.5 * inner * (1.0 + bend)).astype(BF16)
        encoded = (x.astype(F32) + dot(active, sws[layer][...])).astype(BF16)
        encodes.append(encoded)
        if layer == 0:
            for which, count in ((helper, replicas), (mid, replicas), (aid, 2 * replicas - 2)):

                @pl.when(phase == which)
                def _():
                    pl.semaphore_wait(barrier, count)

            @pl.when(phase == mid)
            def _():
                aim_copy.start()

        @pl.when(phase == layer)
        def _():
            aim = target(layer) if layer < mid else (aim_mid[0] if layer == mid else cot_all[me])
            backward = dot_nt(aim, sws[layer][...])
            slope = (bent(inner, bend, squared) * backward).astype(BF16)
            if layer == top:
                slope_all[me] = slope
                others(lambda to: copy_back(to, me).start())
                top_cols(normed, active)
                cols_all[me] = cols_send[me]
            elif layer == mid:
                mid_start(dot_tn(normed, slope))
            else:
                part = parts[layer]
                owners, _, rows_here, _ = part.shape
                for i, term in enumerate((dot_tn(normed, slope), dot_tn(active, aim))):
                    for w in range(owners):
                        part[w, i] = term[w * rows_here : (w + 1) * rows_here].astype(part.dtype)
                for w in range(owners):

                    @pl.when(group_of(layer)[2] != w)
                    def _():
                        near_copy(layer, w, group_of(layer)[2]).start()

        if layer == mid:

            @pl.when(phase == helper)
            def _():
                aim_copy.wait_recv()
                mid_start(dot_tn(active, aim_mid[1]))

        if layer == top:
            mid_pass()

            @pl.when(phase == aid)
            def _():
                top_cols(normed, active)
                others(lambda to: copy_cols(to, me).start())
                top_aim.wait_recv()
                backward = dot_nt(aim_top[0, 0:cut], sws[layer][...])
                front = bent(inner[0:cut], bend[0:cut], squared[0:cut]) * backward
                slope_all[me, 0:cut] = front.astype(BF16)
                others(lambda to: copy_front(to, me).start())

        elif layer > 0:
            pass_on(layer - 1)

        if layer < 3:
            coarse = heights[layer + 1]
            pooled = []
            for m in range(micro):
                matrix = pool_matrix(pms[layer][m : m + 1, :], coarse)
                number = jnp.sum(matrix, axis=1, keepdims=True)
                sums = dot(matrix.astype(BF16), encoded[m * rows : (m + 1) * rows])
                pooled.append(sums / jnp.maximum(number, 1.0))
            x = dot(jnp.concatenate(pooled, axis=0).astype(BF16), cos[layer][...]).astype(BF16)

    decoded = encodes[3]
    for layer in range(3, -1, -1):
        rows, width = heights[layer], widths[layer]
        if layer < 3:
            coarse = heights[layer + 1]
            load(24 + layer).wait()
            mix = dot_nt if layer == 0 else dot
            lifted = mix(decoded, res[layer][...]).astype(BF16)
            ups = []
            for m in range(micro):
                at = base[layer] + m * rows
                matrix = one_hot(idx_t[at : at + rows, TAPS : TAPS + 1], coarse)
                ups.append(dot(matrix, lifted[m * coarse : (m + 1) * coarse]))
            decoded = (encodes[layer].astype(F32) + jnp.concatenate(ups, axis=0)).astype(BF16)

        @pl.when(phase == layer)
        def _():
            wide = decoded.astype(F32)
            for m in range(micro):
                own = wide[m * rows : (m + 1) * rows]
                if width < LANES:
                    small[...] = own
                    pack_d[pl.ds(m, rows // 2, stride=2), :] = jnp.concatenate(
                        [
                            small[pl.ds(0, rows // 2, stride=2), :],
                            small[pl.ds(1, rows // 2, stride=2), :],
                        ],
                        axis=1,
                    )
                else:
                    split = width // LANES
                    for h in range(split):
                        pack_d[pl.ds(2 * h + m, rows, stride=2 * split), :] = own[
                            :, h * LANES : (h + 1) * LANES
                        ]

    for j in range(chunks):
        dec_out[0, :, j * LANES : (j + 1) * LANES] = pack_d[2 * j : 2 * j + 2, :].astype(BF16)

    pack_g[...] = jnp.zeros(pack_g.shape, F32)

    def put_grad(layer, i, term):
        rows_here, width = term.shape
        term = term * (micro * replicas * heights[layer]) ** -0.5
        if width < LANES:
            small[0:rows_here, :] = term
            pack_g[pl.ds(i, rows_here // 2, stride=2), :] = jnp.concatenate(
                [
                    small[pl.ds(0, rows_here // 2, stride=2), :],
                    small[pl.ds(1, rows_here // 2, stride=2), :],
                ],
                axis=1,
            )
        else:
            split = width // LANES
            for h in range(split):
                pack_g[pl.ds(2 * h + i, rows_here, stride=2 * split), :] = term[
                    :, h * LANES : (h + 1) * LANES
                ]

    @pl.when(phase == aid)
    def _():
        @others
        def _(to):
            copy_cols(to, me).wait_send()
            copy_front(to, me).wait_send()

    @pl.when(phase == helper)
    def _():
        mid_far(got_help, recv_help, 0).wait_send()

    @pl.when(phase == mid)
    def _():
        aim_copy.wait_send()
        group = group_of(mid)[1]

        @pl.when(group != 0)
        def _():
            mid_far(got2, recv_far, 0).wait_send()

        @pl.when(group == 0)
        def _():
            got2[0] = sum2[0]
            for i, (got, recv_sem) in enumerate(((got2, recv_far), (got_help, recv_help))):
                for sender in range(1 - i, mid_groups):
                    mid_far(got, recv_sem, sender).wait_recv()
                term = got[0].astype(F32)
                for sender in range(1, mid_groups):
                    term = term + got[sender].astype(F32)
                put_grad(mid, i, term)

    for layer in range(2):
        got = gots[layer]

        @pl.when(phase == layer)
        def _():
            owners, group, _ = group_of(layer)
            groups = replicas // owners

            @pl.when(group != 0)
            def _():
                far_copy(layer, group).wait_send()

            @pl.when(group == 0)
            def _():
                got[0] = sums_of[layer][0]
                for sender in range(1, groups):
                    far_copy(layer, sender).wait_recv()
                for i in range(2):
                    term = got[0, i].astype(F32)
                    for sender in range(1, groups):
                        term = term + got[sender, i].astype(F32)
                    put_grad(layer, i, term)

    @pl.when(phase == top)
    def _():
        span = micro * heights[top]

        def terms(sender):
            @pl.when(sender != me)
            def _():
                copy_cot(me, sender).wait_recv()
                copy_cols(me, sender).wait_recv()
                copy_front(me, sender).wait_recv()
                copy_back(me, sender).wait_recv()

            cols = cols_all[sender].astype(BF16)
            return (
                dot(cols[:, :span], slope_all[sender]),
                dot(cols[:, span:], cot_all[sender]),
            )

        total = terms(0)
        if replicas <= 16:
            for sender in range(1, replicas):
                total = jax.tree.map(jnp.add, total, terms(sender))
        else:
            total = lax.fori_loop(
                1, replicas, lambda s, t: jax.tree.map(jnp.add, t, terms(s)), total
            )
        for i in range(2):
            put_grad(top, i, total[i])

        @others
        def _(to):
            copy_cot(to, me).wait_send()
            copy_back(to, me).wait_send()

        top_aim.wait_send()


    for q in range(grad_out.shape[2] // LANES):
        grad_out[0, :, q * LANES : (q + 1) * LANES] = pack_g[2 * q : 2 * q + 2, :]


def deliver(dec_in, grad_in, dec_out, grad_out, sem):
    copies = [
        pltpu.make_async_copy(grad_in, grad_out, sem.at[0]),
        pltpu.make_async_copy(dec_in, dec_out, sem.at[1]),
    ]
    for copy in copies:
        copy.start()
    for copy in copies:
        copy.wait()


def on_device(*arrays):
    features, kms, dws = arrays[0], arrays[2:6], arrays[9:13]
    arrays = list(arrays)
    arrays[1] = arrays[1].T
    arrays[2:6] = [jnp.transpose(km, (1, 0, 2)) for km in kms]
    arrays[24] = arrays[24].T
    widths = [taps.shape[1] for taps in dws]
    heights = [km.shape[2] for km in kms]
    micro, elements = features.shape
    replicas = lax.axis_size("dp")
    owned = widths[3] * widths[3] // replicas

    def narrow(rows):
        return BF16 if rows % 16 == 0 else F32

    parts, gots, nears, sums_of = [], [], [], []
    for layer in range(3):
        rows_here = min(widths[layer], owned // widths[layer])
        owners = widths[layer] // rows_here
        kind = narrow(rows_here)
        if layer == 2:
            shape = (rows_here, widths[2])
            for held, first in ((parts, owners), (gots, replicas // owners), (nears, owners), (sums_of, 1)):
                held.append(pltpu.VMEM((first, *shape), kind))
            break
        parts.append(pltpu.VMEM((owners, 2, rows_here, widths[layer]), kind))
        gots.append(pltpu.VMEM((replicas // owners, 2, rows_here, widths[layer]), kind))
        nears.append(pltpu.VMEM((owners, 2, rows_here, widths[layer]), kind))
        sums_of.append(pltpu.VMEM((1, 2, rows_here, widths[layer]), kind))
    top_rows = owned // widths[3]
    span = micro * heights[3]
    idx_lanes = -(-micro * sum(heights) // LANES) * LANES
    sem = pltpu.SemaphoreType.DMA((replicas,))
    scratch = [
        *[pltpu.VMEM(a.shape, a.dtype) for a in arrays],
        pltpu.SemaphoreType.DMA((len(arrays),)),
        pltpu.VMEM((2 * elements // LANES, LANES), F32),
        pltpu.VMEM((2 * elements // LANES, LANES), F32),
        pltpu.VMEM((2 * elements // LANES, LANES), F32),
        pltpu.VMEM((2 * owned // LANES, LANES), F32),
        pltpu.VMEM((heights[0], widths[0]), F32),
        pltpu.VMEM((-(-heights[0] // LANES), 2 * IDX_ROWS, LANES), F32),
        pltpu.VMEM((IDX_ROWS, idx_lanes), F32),
        pltpu.VMEM((idx_lanes, IDX_ROWS), F32),
        *parts,
        *gots,
        *nears,
        *sums_of,
        pltpu.VMEM((replicas, span, widths[3]), BF16),
        pltpu.VMEM((replicas, span, widths[3]), BF16),
        pltpu.VMEM((replicas, top_rows, 2 * span), narrow(top_rows)),
        pltpu.VMEM((replicas, top_rows, 2 * span), narrow(top_rows)),
        *[sem] * 10,
        pltpu.VMEM((2, micro * heights[2], widths[2]), BF16),
        gots[2],
        *[sem] * 7,
        pltpu.VMEM((1, span, widths[3]), BF16),
        *[sem] * 4,
    ]
    held = pl.pallas_call(
        functools.partial(kernel, replicas, heights, widths, micro, len(arrays)),
        out_shape=(
            pltpu.VMEM((1, micro, elements), BF16),
            pltpu.VMEM((1, 2, owned), F32),
        ),
        in_specs=[pl.BlockSpec(memory_space=pltpu.HBM)] * len(arrays),
        out_specs=[pl.BlockSpec(memory_space=pltpu.VMEM)] * 2,
        scratch_shapes=scratch,
        compiler_params=pltpu.CompilerParams(
            collective_id=0, has_side_effects=True, vmem_limit_bytes=64 * 1024 * 1024 - 512 * 1024
        ),
    )(*arrays)
    return pl.pallas_call(
        deliver,
        out_shape=(
            jax.ShapeDtypeStruct((1, micro, elements), BF16),
            jax.ShapeDtypeStruct((1, 2, owned), F32),
        ),
        in_specs=[pl.BlockSpec(memory_space=pltpu.VMEM)] * 2,
        out_specs=[pl.BlockSpec(memory_space=pltpu.HBM)] * 2,
        scratch_shapes=[pltpu.SemaphoreType.DMA((2,))],
        compiler_params=pltpu.CompilerParams(vmem_limit_bytes=1024 * 1024),
    )(*[pltpu.with_memory_space_constraint(a, pltpu.VMEM) for a in held])


def solution(mesh):
    placed = (
        (P(None, "dp"), P(None, "dp"))
        + (P(None, None, "dp"),) * 4
        + (P(None, "dp"),) * 3
        + (P(),) * 18
        + (P("phase", None, "dp"),)
    )
    return jax.shard_map(
        on_device,
        mesh=mesh,
        in_specs=placed,
        out_specs=(P("phase", None, "dp"), P("phase", None, "dp")),
        check_vma=False,
    )
```

```python
import functools
import math

import jax
import jax.numpy as jnp
from jax import lax
from jax.experimental import pallas as pl
from jax.experimental.pallas import tpu as pltpu
from jax.sharding import PartitionSpec as P

LANES = 128
TAPS = 27
IDX_ROWS = 32
BATCH = 9
F32 = jnp.float32
BF16 = jnp.bfloat16
MESH = pl.DeviceIdType.MESH
GELU_A = math.sqrt(2.0 / math.pi)
GELU_B = 0.044715


def dot(a, b):
    return lax.dot_general(a, b, (((1,), (0,)), ((), ())), preferred_element_type=F32)


def dot_nt(a, b):
    return lax.dot_general(a, b, (((1,), (1,)), ((), ())), preferred_element_type=F32)


def dot_tn(a, b):
    return lax.dot_general(a, b, (((0,), (0,)), ((), ())), preferred_element_type=F32)


def one_hot(column, width):
    lanes = lax.broadcasted_iota(jnp.int32, (column.shape[0], width), 1).astype(F32).astype(BF16)
    wide = jnp.broadcast_to(column, lanes.shape).astype(BF16)
    return jnp.where(wide == lanes, jnp.ones_like(lanes), jnp.zeros_like(lanes))


def pool_matrix(parent_row, coarse):
    rows = lax.broadcasted_iota(jnp.int32, (coarse, parent_row.shape[1]), 0)
    return jnp.where(rows == parent_row, 1.0, 0.0).astype(F32)


def kernel(replicas, heights, widths, micro, count, *refs):
    sources, (dec_out, grad_out) = refs[:count], refs[count : count + 2]
    held, refs = refs[count + 2 : 2 * count + 2], refs[2 * count + 2 :]
    (
        load_sem,
        pack_f,
        pack_c,
        pack_d,
        pack_g,
        small,
        idx_raw,
        idx,
        idx_t,
        part0,
        part1,
        part2,
        got0,
        got1,
        got2,
        near0,
        near1,
        near2,
        sum0,
        sum1,
        sum2,
        cot_all,
        slope_all,
        cols_send,
        cols_all,
        send_part,
        recv_part,
        send_cot,
        recv_cot,
        send_slope,
        recv_slope,
        send_cols,
        recv_cols,
        send_near,
        recv_near,
        aim_mid,
        got_help,
        send_aim,
        recv_aim,
        send_mid,
        recv_mid,
        send_far,
        recv_far,
        recv_help,
        aim_top,
        send_top,
        recv_top,
        send_front,
        recv_front,
    ) = refs
    nears, sums_of = (near0, near1, near2), (sum0, sum1, sum2)
    features, counts, cot = held[0], held[1], held[27]
    kms, pms, dws = held[2:6], held[6:9], held[9:13]
    fws, sws = held[13:17], held[17:21]
    cos, res = held[21:24], held[24:27]
    parts, gots = (part0, part1, part2), (got0, got1, got2)
    phase = lax.axis_index("phase")
    me = lax.axis_index("dp")
    chunks = features.shape[1] // LANES

    def peer(offset):
        return {"phase": phase, "dp": lax.rem(me + offset, replicas)}

    def load(i):
        return pltpu.make_async_copy(sources[i], held[i], load_sem.at[i])

    order = [0, 27, 2, 3, 4, 5, 6, 7, 8, 1, 9, 13, 17, 21, 10, 14, 18, 22, 11, 15, 19, 23, 12, 16, 20]
    for i in order + [26, 25, 24]:
        load(i).start()

    mid, helper, aid = 2, 0, 1
    cut = cot_all.shape[1] // 4
    barrier = pltpu.get_barrier_semaphore()

    @pl.loop(1, replicas)
    def _(offset):
        pl.semaphore_signal(barrier, inc=1, device_id=peer(offset), device_id_type=MESH)

    mid_owners = part2.shape[0]
    mid_groups = replicas // mid_owners

    @pl.when(phase == helper)
    def _():
        pl.semaphore_signal(barrier, inc=1, device_id={"phase": mid, "dp": me}, device_id_type=MESH)

    @pl.when((phase == mid) & (me < mid_owners))
    def _():
        @pl.loop(0, mid_groups)
        def _(group):
            pl.semaphore_signal(
                barrier,
                inc=1,
                device_id={"phase": helper, "dp": group * mid_owners + me},
                device_id_type=MESH,
            )

    @pl.when(phase == aid)
    def _():
        pl.semaphore_signal(barrier, inc=1, device_id={"phase": 3, "dp": me}, device_id_type=MESH)

    @pl.when(phase == 3)
    def _():
        @pl.loop(1, replicas)
        def _(offset):
            pl.semaphore_signal(
                barrier,
                inc=1,
                device_id={"phase": aid, "dp": lax.rem(me + offset, replicas)},
                device_id_type=MESH,
            )

    for i in (0, 27):
        load(i).wait()

    for j in range(chunks):
        lanes = slice(j * LANES, (j + 1) * LANES)
        pack_f[2 * j : 2 * j + 2, :] = features[:, lanes].astype(F32)
        pack_c[2 * j : 2 * j + 2, :] = cot[0, :, lanes].astype(F32)

    def unpack(pack, layer, m):
        rows, width = heights[layer], widths[layer]
        if width < LANES:
            both = pack[pl.ds(m, rows // 2, stride=2), :]
            small[pl.ds(0, rows // 2, stride=2), :] = both[:, :width]
            small[pl.ds(1, rows // 2, stride=2), :] = both[:, width:]
            return small[...]
        split = width // LANES
        return jnp.concatenate(
            [pack[pl.ds(2 * h + m, rows, stride=2 * split), :] for h in range(split)], axis=1
        )

    def target(layer):
        return jnp.concatenate([unpack(pack_c, layer, m) for m in range(micro)], axis=0).astype(BF16)

    top = 3

    def top_copy(source, landing, send_sem, recv_sem, to, sender):
        return pltpu.make_async_remote_copy(
            src_ref=source,
            dst_ref=landing,
            send_sem=send_sem.at[to],
            recv_sem=recv_sem.at[sender],
            device_id={"phase": top, "dp": to},
            device_id_type=MESH,
        )

    def copy_cot(to, sender):
        return top_copy(cot_all.at[sender], cot_all.at[sender], send_cot, recv_cot, to, sender)

    def copy_cols(to, sender):
        return top_copy(cols_send.at[to], cols_all.at[sender], send_cols, recv_cols, to, sender)

    def copy_front(to, sender):
        rows = slope_all.at[sender, pl.ds(0, cut)]
        return top_copy(rows, rows, send_front, recv_front, to, sender)

    def copy_back(to, sender):
        rows = slope_all.at[sender, pl.ds(cut, cot_all.shape[1] - cut)]
        return top_copy(rows, rows, send_slope, recv_slope, to, sender)

    top_aim = pltpu.make_async_remote_copy(
        src_ref=cot_all.at[me],
        dst_ref=aim_top.at[0],
        send_sem=send_top.at[0],
        recv_sem=recv_top.at[0],
        device_id={"phase": aid, "dp": me},
        device_id_type=MESH,
    )

    def others(body):
        @pl.loop(0, replicas)
        def _(other):
            @pl.when(other != me)
            def _():
                body(other)

    def group_of(layer):
        owners = parts[layer].shape[0]
        return owners, lax.div(me, owners), lax.rem(me, owners)

    def near_copy(layer, w, sender):
        owners, group, _ = group_of(layer)
        return pltpu.make_async_remote_copy(
            src_ref=parts[layer].at[w],
            dst_ref=nears[layer].at[sender],
            send_sem=send_near.at[w],
            recv_sem=recv_near.at[sender],
            device_id={"phase": phase, "dp": group * owners + w},
            device_id_type=MESH,
        )

    def far_copy(layer, group):
        return pltpu.make_async_remote_copy(
            src_ref=sums_of[layer].at[0],
            dst_ref=gots[layer].at[group],
            send_sem=send_part.at[0],
            recv_sem=recv_part.at[group],
            device_id={"phase": phase, "dp": group_of(layer)[2]},
            device_id_type=MESH,
        )

    @pl.when(phase == top)
    def _():
        cot_all[me] = target(top)

    @pl.when(phase == mid)
    def _():
        aim_mid[0] = target(mid)

    aim_copy = pltpu.make_async_remote_copy(
        src_ref=aim_mid.at[0],
        dst_ref=aim_mid.at[1],
        send_sem=send_aim.at[0],
        recv_sem=recv_aim.at[0],
        device_id={"phase": helper, "dp": me},
        device_id_type=MESH,
    )

    def mid_near(w, sender):
        _, group, _ = group_of(mid)
        return pltpu.make_async_remote_copy(
            src_ref=part2.at[w],
            dst_ref=near2.at[sender],
            send_sem=send_mid.at[w],
            recv_sem=recv_mid.at[sender],
            device_id={"phase": phase, "dp": group * mid_owners + w},
            device_id_type=MESH,
        )

    def mid_far(got, recv_sem, group):
        return pltpu.make_async_remote_copy(
            src_ref=sum2.at[0],
            dst_ref=got.at[group],
            send_sem=send_far.at[0],
            recv_sem=recv_sem.at[group],
            device_id={"phase": mid, "dp": group_of(mid)[2]},
            device_id_type=MESH,
        )

    def mid_start(term):
        rows_here = part2.shape[1]
        member = group_of(mid)[2]
        for w in range(mid_owners):
            part2[w] = term[w * rows_here : (w + 1) * rows_here].astype(part2.dtype)
        for w in range(mid_owners):

            @pl.when(member != w)
            def _():
                mid_near(w, member).start()

    def mid_pass():
        @pl.when((phase == mid) | (phase == helper))
        def _():
            _, group, member = group_of(mid)
            near2[member] = part2[member]
            for w in range(mid_owners):

                @pl.when(member != w)
                def _():
                    mid_near(w, member).wait_send()
                    mid_near(w, w).wait_recv()

            term = near2[0].astype(F32)
            for w in range(1, mid_owners):
                term = term + near2[w].astype(F32)
            sum2[0] = term.astype(near2.dtype)

            @pl.when(phase == helper)
            def _():
                mid_far(got_help, recv_help, group).start()

            @pl.when((phase == mid) & (group != 0))
            def _():
                mid_far(got2, recv_far, group).start()

    def top_cols(normed, active):
        both = jnp.concatenate([normed.astype(F32).T, active.astype(F32).T], axis=1).astype(cols_send.dtype)
        rows_here = cols_send.shape[1]
        for d in range(replicas):
            cols_send[d] = both[d * rows_here : (d + 1) * rows_here]

    for i in (2, 3, 4, 5, 6, 7, 8, 1):
        load(i).wait()
    idx[...] = jnp.full(idx.shape, -1.0, F32)
    base = []
    position = 0
    for layer in range(4):
        rows = heights[layer]
        base.append(position)
        pieces = [(at, min(LANES, rows - at)) for at in range(0, rows, LANES)]
        for k in range(TAPS):
            for piece, (at, span) in enumerate(pieces):
                idx_raw[piece, 2 * k : 2 * k + 2, 0:span] = kms[layer][k, :, at : at + span].astype(F32)
        for m in range(micro):
            at = position + m * rows
            values = jnp.concatenate(
                [
                    idx_raw.at[piece][pl.ds(m, TAPS, stride=2), :][:, :span]
                    for piece, (_, span) in enumerate(pieces)
                ],
                axis=1,
            )
            shift = m * rows if layer >= 2 else 0
            if shift:
                values = jnp.where(values < 0.0, values, values + float(shift))
            idx[0:TAPS, at : at + rows] = values
            if layer < 3:
                idx[TAPS : TAPS + 1, at : at + rows] = pms[layer][m : m + 1, :].astype(F32)
        position += micro * rows
    for j in range(idx.shape[1] // LANES):
        lanes = slice(j * LANES, (j + 1) * LANES)
        idx_t[lanes, :] = idx[:, lanes].T

    live = []
    for m in range(micro):
        block = unpack(pack_f, 0, m)
        site = lax.broadcasted_iota(jnp.int32, block.shape, 0)
        live.append(jnp.where(site < counts[:, m : m + 1], block, 0.0))
    x = jnp.concatenate(live, axis=0).astype(BF16)

    def pass_on(layer):
        part, near = parts[layer], nears[layer]

        @pl.when(phase == layer)
        def _():
            owners, group, member = group_of(layer)
            near[member] = part[member]
            for w in range(owners):

                @pl.when(member != w)
                def _():
                    near_copy(layer, w, member).wait_send()
                    near_copy(layer, w, w).wait_recv()

            for i in range(2):
                term = near[0, i].astype(F32)
                for w in range(1, owners):
                    term = term + near[w, i].astype(F32)
                sums_of[layer][0, i] = term.astype(near.dtype)

            @pl.when(group != 0)
            def _():
                far_copy(layer, group).start()

    @pl.when(phase == top)
    def _():
        pl.semaphore_wait(barrier, replicas)
        top_aim.start()
        others(lambda to: copy_cot(to, me).start())

    def bent(inner, bend, squared):
        return 0.5 * (1.0 + bend) + 0.5 * inner * (1.0 - bend * bend) * GELU_A * (
            1.0 + 3.0 * GELU_B * squared
        )

    encodes = []
    for layer in range(4):
        for i in (9 + layer, 13 + layer, 17 + layer) + ((21 + layer,) if layer < 3 else ()):
            load(i).wait()
        rows, width = heights[layer], widths[layer]
        group = rows if layer < 2 else micro * rows
        mixes = []
        for start in range(0, micro * rows, group):
            block = x[start : start + group]
            index = idx_t[base[layer] + start : base[layer] + start + group, :]
            taps = dws[layer][...]
            scaled = jnp.concatenate([block * taps[k : k + 1, :] for k in range(TAPS)], axis=0)
            hots = jnp.concatenate([one_hot(index[:, k : k + 1], group) for k in range(TAPS)], axis=1)
            mixed = dot(hots, scaled)
            mixes.append(mixed)
        mixed = mixes[0] if len(mixes) == 1 else jnp.concatenate(mixes, axis=0)
        normed_f = mixed * lax.rsqrt(jnp.mean(mixed * mixed, axis=1, keepdims=True) + 1e-05)
        normed = normed_f.astype(BF16)
        inner = dot(normed, fws[layer][...])
        squared = inner * inner
        bend = jnp.tanh(GELU_A * inner * (1.0 + GELU_B * squared))
        active = (0.5 * inner * (1.0 + bend)).astype(BF16)
        encoded = (x.astype(F32) + dot(active, sws[layer][...])).astype(BF16)
        encodes.append(encoded)
        if layer == 0:
            for which, count in ((helper, replicas), (mid, replicas), (aid, 2 * replicas - 2)):

                @pl.when(phase == which)
                def _():
                    pl.semaphore_wait(barrier, count)

            @pl.when(phase == mid)
            def _():
                aim_copy.start()

        @pl.when(phase == layer)
        def _():
            aim = target(layer) if layer < mid else (aim_mid[0] if layer == mid else cot_all[me])
            backward = dot_nt(aim, sws[layer][...])
            slope = (bent(inner, bend, squared) * backward).astype(BF16)
            if layer == top:
                slope_all[me] = slope
                others(lambda to: copy_back(to, me).start())
                top_cols(normed, active)
                cols_all[me] = cols_send[me]
            elif layer == mid:
                mid_start(dot_tn(normed, slope))
            else:
                part = parts[layer]
                owners, _, rows_here, _ = part.shape
                for i, term in enumerate((dot_tn(normed, slope), dot_tn(active, aim))):
                    for w in range(owners):
                        part[w, i] = term[w * rows_here : (w + 1) * rows_here].astype(part.dtype)
                for w in range(owners):

                    @pl.when(group_of(layer)[2] != w)
                    def _():
                        near_copy(layer, w, group_of(layer)[2]).start()

        if layer == mid:

            @pl.when(phase == helper)
            def _():
                aim_copy.wait_recv()
                mid_start(dot_tn(active, aim_mid[1]))

        if layer == top:
            mid_pass()

            @pl.when(phase == aid)
            def _():
                top_cols(normed, active)
                others(lambda to: copy_cols(to, me).start())
                top_aim.wait_recv()
                backward = dot_nt(aim_top[0, 0:cut], sws[layer][...])
                front = bent(inner[0:cut], bend[0:cut], squared[0:cut]) * backward
                slope_all[me, 0:cut] = front.astype(BF16)
                others(lambda to: copy_front(to, me).start())

        elif layer > 0:
            pass_on(layer - 1)

        if layer < 3:
            coarse = heights[layer + 1]
            pooled = []
            for m in range(micro):
                matrix = pool_matrix(pms[layer][m : m + 1, :], coarse)
                number = jnp.sum(matrix, axis=1, keepdims=True)
                sums = dot(matrix.astype(BF16), encoded[m * rows : (m + 1) * rows])
                pooled.append(sums / jnp.maximum(number, 1.0))
            x = dot(jnp.concatenate(pooled, axis=0).astype(BF16), cos[layer][...]).astype(BF16)

    decoded = encodes[3]
    for layer in range(3, -1, -1):
        rows, width = heights[layer], widths[layer]
        if layer < 3:
            coarse = heights[layer + 1]
            load(24 + layer).wait()
            mix = dot_nt if layer == 0 else dot
            lifted = mix(decoded, res[layer][...]).astype(BF16)
            ups = []
            for m in range(micro):
                at = base[layer] + m * rows
                matrix = one_hot(idx_t[at : at + rows, TAPS : TAPS + 1], coarse)
                ups.append(dot(matrix, lifted[m * coarse : (m + 1) * coarse]))
            decoded = (encodes[layer].astype(F32) + jnp.concatenate(ups, axis=0)).astype(BF16)

        @pl.when(phase == layer)
        def _():
            wide = decoded.astype(F32)
            for m in range(micro):
                own = wide[m * rows : (m + 1) * rows]
                if width < LANES:
                    small[...] = own
                    pack_d[pl.ds(m, rows // 2, stride=2), :] = jnp.concatenate(
                        [
                            small[pl.ds(0, rows // 2, stride=2), :],
                            small[pl.ds(1, rows // 2, stride=2), :],
                        ],
                        axis=1,
                    )
                else:
                    split = width // LANES
                    for h in range(split):
                        pack_d[pl.ds(2 * h + m, rows, stride=2 * split), :] = own[
                            :, h * LANES : (h + 1) * LANES
                        ]

    for j in range(chunks):
        dec_out[0, :, j * LANES : (j + 1) * LANES] = pack_d[2 * j : 2 * j + 2, :].astype(BF16)

    pack_g[...] = jnp.zeros(pack_g.shape, F32)

    def put_grad(layer, i, term):
        rows_here, width = term.shape
        term = term * (micro * replicas * heights[layer]) ** -0.5
        if width < LANES:
            small[0:rows_here, :] = term
            pack_g[pl.ds(i, rows_here // 2, stride=2), :] = jnp.concatenate(
                [
                    small[pl.ds(0, rows_here // 2, stride=2), :],
                    small[pl.ds(1, rows_here // 2, stride=2), :],
                ],
                axis=1,
            )
        else:
            split = width // LANES
            for h in range(split):
                pack_g[pl.ds(2 * h + i, rows_here, stride=2 * split), :] = term[
                    :, h * LANES : (h + 1) * LANES
                ]

    @pl.when(phase == aid)
    def _():
        @others
        def _(to):
            copy_cols(to, me).wait_send()
            copy_front(to, me).wait_send()

    @pl.when(phase == helper)
    def _():
        mid_far(got_help, recv_help, 0).wait_send()

    @pl.when(phase == mid)
    def _():
        aim_copy.wait_send()
        group = group_of(mid)[1]

        @pl.when(group != 0)
        def _():
            mid_far(got2, recv_far, 0).wait_send()

        @pl.when(group == 0)
        def _():
            got2[0] = sum2[0]
            for i, (got, recv_sem) in enumerate(((got2, recv_far), (got_help, recv_help))):
                for sender in range(1 - i, mid_groups):
                    mid_far(got, recv_sem, sender).wait_recv()
                term = got[0].astype(F32)
                for sender in range(1, mid_groups):
                    term = term + got[sender].astype(F32)
                put_grad(mid, i, term)

    for layer in range(2):
        got = gots[layer]

        @pl.when(phase == layer)
        def _():
            owners, group, _ = group_of(layer)
            groups = replicas // owners

            @pl.when(group != 0)
            def _():
                far_copy(layer, group).wait_send()

            @pl.when(group == 0)
            def _():
                got[0] = sums_of[layer][0]
                for sender in range(1, groups):
                    far_copy(layer, sender).wait_recv()
                for i in range(2):
                    term = got[0, i].astype(F32)
                    for sender in range(1, groups):
                        term = term + got[sender, i].astype(F32)
                    put_grad(layer, i, term)

    @pl.when(phase == top)
    def _():
        span = micro * heights[top]

        def terms(sender):
            @pl.when(sender != me)
            def _():
                copy_cot(me, sender).wait_recv()
                copy_cols(me, sender).wait_recv()
                copy_front(me, sender).wait_recv()
                copy_back(me, sender).wait_recv()

            cols = cols_all[sender].astype(BF16)
            return (
                dot(cols[:, :span], slope_all[sender]),
                dot(cols[:, span:], cot_all[sender]),
            )

        total = terms(0)
        if replicas <= 16:
            for sender in range(1, replicas):
                total = jax.tree.map(jnp.add, total, terms(sender))
        else:
            total = lax.fori_loop(
                1, replicas, lambda s, t: jax.tree.map(jnp.add, t, terms(s)), total
            )
        for i in range(2):
            put_grad(top, i, total[i])

        @others
        def _(to):
            copy_cot(to, me).wait_send()
            copy_back(to, me).wait_send()

        top_aim.wait_send()


    for q in range(grad_out.shape[2] // LANES):
        grad_out[0, :, q * LANES : (q + 1) * LANES] = pack_g[2 * q : 2 * q + 2, :]


def deliver(dec_in, grad_in, dec_out, grad_out, sem):
    copies = [
        pltpu.make_async_copy(grad_in, grad_out, sem.at[0]),
        pltpu.make_async_copy(dec_in, dec_out, sem.at[1]),
    ]
    for copy in copies:
        copy.start()
    for copy in copies:
        copy.wait()


def on_device(*arrays):
    features, kms, dws = arrays[0], arrays[2:6], arrays[9:13]
    arrays = list(arrays)
    arrays[1] = arrays[1].T
    arrays[2:6] = [jnp.transpose(km, (1, 0, 2)) for km in kms]
    arrays[24] = arrays[24].T
    widths = [taps.shape[1] for taps in dws]
    heights = [km.shape[2] for km in kms]
    micro, elements = features.shape
    replicas = lax.axis_size("dp")
    owned = widths[3] * widths[3] // replicas

    def narrow(rows):
        return BF16 if rows % 16 == 0 else F32

    parts, gots, nears, sums_of = [], [], [], []
    for layer in range(3):
        rows_here = min(widths[layer], owned // widths[layer])
        owners = widths[layer] // rows_here
        kind = narrow(rows_here)
        if layer == 2:
            shape = (rows_here, widths[2])
            for held, first in ((parts, owners), (gots, replicas // owners), (nears, owners), (sums_of, 1)):
                held.append(pltpu.VMEM((first, *shape), kind))
            break
        parts.append(pltpu.VMEM((owners, 2, rows_here, widths[layer]), kind))
        gots.append(pltpu.VMEM((replicas // owners, 2, rows_here, widths[layer]), kind))
        nears.append(pltpu.VMEM((owners, 2, rows_here, widths[layer]), kind))
        sums_of.append(pltpu.VMEM((1, 2, rows_here, widths[layer]), kind))
    top_rows = owned // widths[3]
    span = micro * heights[3]
    idx_lanes = -(-micro * sum(heights) // LANES) * LANES
    sem = pltpu.SemaphoreType.DMA((replicas,))
    scratch = [
        *[pltpu.VMEM(a.shape, a.dtype) for a in arrays],
        pltpu.SemaphoreType.DMA((len(arrays),)),
        pltpu.VMEM((2 * elements // LANES, LANES), F32),
        pltpu.VMEM((2 * elements // LANES, LANES), F32),
        pltpu.VMEM((2 * elements // LANES, LANES), F32),
        pltpu.VMEM((2 * owned // LANES, LANES), F32),
        pltpu.VMEM((heights[0], widths[0]), F32),
        pltpu.VMEM((-(-heights[0] // LANES), 2 * IDX_ROWS, LANES), F32),
        pltpu.VMEM((IDX_ROWS, idx_lanes), F32),
        pltpu.VMEM((idx_lanes, IDX_ROWS), F32),
        *parts,
        *gots,
        *nears,
        *sums_of,
        pltpu.VMEM((replicas, span, widths[3]), BF16),
        pltpu.VMEM((replicas, span, widths[3]), BF16),
        pltpu.VMEM((replicas, top_rows, 2 * span), narrow(top_rows)),
        pltpu.VMEM((replicas, top_rows, 2 * span), narrow(top_rows)),
        *[sem] * 10,
        pltpu.VMEM((2, micro * heights[2], widths[2]), BF16),
        gots[2],
        *[sem] * 7,
        pltpu.VMEM((1, span, widths[3]), BF16),
        *[sem] * 4,
    ]
    held = pl.pallas_call(
        functools.partial(kernel, replicas, heights, widths, micro, len(arrays)),
        out_shape=(
            pltpu.VMEM((1, micro, elements), BF16),
            pltpu.VMEM((1, 2, owned), F32),
        ),
        in_specs=[pl.BlockSpec(memory_space=pltpu.HBM)] * len(arrays),
        out_specs=[pl.BlockSpec(memory_space=pltpu.VMEM)] * 2,
        scratch_shapes=scratch,
        compiler_params=pltpu.CompilerParams(
            collective_id=0, has_side_effects=True, vmem_limit_bytes=64 * 1024 * 1024 - 512 * 1024
        ),
    )(*arrays)
    return pl.pallas_call(
        deliver,
        out_shape=(
            jax.ShapeDtypeStruct((1, micro, elements), BF16),
            jax.ShapeDtypeStruct((1, 2, owned), F32),
        ),
        in_specs=[pl.BlockSpec(memory_space=pltpu.VMEM)] * 2,
        out_specs=[pl.BlockSpec(memory_space=pltpu.HBM)] * 2,
        scratch_shapes=[pltpu.SemaphoreType.DMA((2,))],
        compiler_params=pltpu.CompilerParams(vmem_limit_bytes=1024 * 1024),
    )(*[pltpu.with_memory_space_constraint(a, pltpu.VMEM) for a in held])


def solution(mesh):
    placed = (
        (P(None, "dp"), P(None, "dp"))
        + (P(None, None, "dp"),) * 4
        + (P(None, "dp"),) * 3
        + (P(),) * 18
        + (P("phase", None, "dp"),)
    )
    return jax.shard_map(
        on_device,
        mesh=mesh,
        in_specs=placed,
        out_specs=(P("phase", None, "dp"), P("phase", None, "dp")),
        check_vma=False,
    )
```

```python
import functools
import math

import jax
import jax.numpy as jnp
from jax import lax
from jax.experimental import pallas as pl
from jax.experimental.pallas import tpu as pltpu
from jax.sharding import PartitionSpec as P

LANES = 128
TAPS = 27
IDX_ROWS = 32
BATCH = 9
F32 = jnp.float32
BF16 = jnp.bfloat16
MESH = pl.DeviceIdType.MESH
GELU_A = math.sqrt(2.0 / math.pi)
GELU_B = 0.044715


def dot(a, b):
    return lax.dot_general(a, b, (((1,), (0,)), ((), ())), preferred_element_type=F32)


def dot_nt(a, b):
    return lax.dot_general(a, b, (((1,), (1,)), ((), ())), preferred_element_type=F32)


def dot_tn(a, b):
    return lax.dot_general(a, b, (((0,), (0,)), ((), ())), preferred_element_type=F32)


def one_hot(column, width):
    lanes = lax.broadcasted_iota(jnp.int32, (column.shape[0], width), 1).astype(F32).astype(BF16)
    wide = jnp.broadcast_to(column, lanes.shape).astype(BF16)
    return jnp.where(wide == lanes, jnp.ones_like(lanes), jnp.zeros_like(lanes))


def pool_matrix(parent_row, coarse):
    rows = lax.broadcasted_iota(jnp.int32, (coarse, parent_row.shape[1]), 0)
    return jnp.where(rows == parent_row, 1.0, 0.0).astype(F32)


def kernel(replicas, heights, widths, micro, count, *refs):
    sources, (dec_out, grad_out) = refs[:count], refs[count : count + 2]
    held, refs = refs[count + 2 : 2 * count + 2], refs[2 * count + 2 :]
    (
        load_sem,
        pack_f,
        pack_c,
        pack_d,
        pack_g,
        small,
        idx_raw,
        idx,
        idx_t,
        part0,
        part1,
        part2,
        got0,
        got1,
        got2,
        near0,
        near1,
        near2,
        sum0,
        sum1,
        sum2,
        cot_all,
        slope_all,
        cols_send,
        cols_all,
        send_part,
        recv_part,
        send_cot,
        recv_cot,
        send_slope,
        recv_slope,
        send_cols,
        recv_cols,
        send_near,
        recv_near,
        aim_mid,
        got_help,
        send_aim,
        recv_aim,
        send_mid,
        recv_mid,
        send_far,
        recv_help,
        aim_top,
        send_top,
        recv_top,
        send_front,
        recv_front,
    ) = refs
    nears, sums_of = (near0, near1, near2), (sum0, sum1, sum2)
    features, counts, cot = held[0], held[1], held[27]
    kms, pms, dws = held[2:6], held[6:9], held[9:13]
    fws, sws = held[13:17], held[17:21]
    cos, res = held[21:24], held[24:27]
    parts, gots = (part0, part1, part2), (got0, got1, got2)
    phase = lax.axis_index("phase")
    me = lax.axis_index("dp")
    chunks = features.shape[1] // LANES

    def peer(offset):
        return {"phase": phase, "dp": lax.rem(me + offset, replicas)}

    def load(i):
        return pltpu.make_async_copy(sources[i], held[i], load_sem.at[i])

    order = [0, 27, 2, 3, 4, 5, 6, 7, 8, 1, 9, 13, 17, 21, 10, 14, 18, 22, 11, 15, 19, 23, 12, 16, 20]
    for i in order + [26, 25, 24]:
        load(i).start()

    mid, helper, aid = 2, 0, 1
    cut = cot_all.shape[1] // 4
    barrier = pltpu.get_barrier_semaphore()

    @pl.loop(1, replicas)
    def _(offset):
        pl.semaphore_signal(barrier, inc=1, device_id=peer(offset), device_id_type=MESH)

    mid_owners = part2.shape[0]
    mid_groups = replicas // mid_owners

    @pl.when(phase == helper)
    def _():
        pl.semaphore_signal(barrier, inc=1, device_id={"phase": mid, "dp": me}, device_id_type=MESH)

    @pl.when((phase == mid) & (me < mid_owners))
    def _():
        @pl.loop(0, mid_groups)
        def _(group):
            pl.semaphore_signal(
                barrier,
                inc=1,
                device_id={"phase": helper, "dp": group * mid_owners + me},
                device_id_type=MESH,
            )

    @pl.when(phase == aid)
    def _():
        pl.semaphore_signal(barrier, inc=1, device_id={"phase": 3, "dp": me}, device_id_type=MESH)

    @pl.when(phase == 3)
    def _():
        @pl.loop(1, replicas)
        def _(offset):
            pl.semaphore_signal(
                barrier,
                inc=1,
                device_id={"phase": aid, "dp": lax.rem(me + offset, replicas)},
                device_id_type=MESH,
            )

    for i in (0, 27):
        load(i).wait()

    for j in range(chunks):
        lanes = slice(j * LANES, (j + 1) * LANES)
        pack_f[2 * j : 2 * j + 2, :] = features[:, lanes].astype(F32)
        pack_c[2 * j : 2 * j + 2, :] = cot[0, :, lanes].astype(F32)

    def unpack(pack, layer, m):
        rows, width = heights[layer], widths[layer]
        if width < LANES:
            both = pack[pl.ds(m, rows // 2, stride=2), :]
            small[pl.ds(0, rows // 2, stride=2), :] = both[:, :width]
            small[pl.ds(1, rows // 2, stride=2), :] = both[:, width:]
            return small[...]
        split = width // LANES
        return jnp.concatenate(
            [pack[pl.ds(2 * h + m, rows, stride=2 * split), :] for h in range(split)], axis=1
        )

    def target(layer):
        return jnp.concatenate([unpack(pack_c, layer, m) for m in range(micro)], axis=0).astype(BF16)

    top = 3

    def top_copy(source, landing, send_sem, recv_sem, to, sender):
        return pltpu.make_async_remote_copy(
            src_ref=source,
            dst_ref=landing,
            send_sem=send_sem.at[to],
            recv_sem=recv_sem.at[sender],
            device_id={"phase": top, "dp": to},
            device_id_type=MESH,
        )

    def copy_cot(to, sender):
        return top_copy(cot_all.at[sender], cot_all.at[sender], send_cot, recv_cot, to, sender)

    def copy_cols(to, sender):
        return top_copy(cols_send.at[to], cols_all.at[sender], send_cols, recv_cols, to, sender)

    def copy_front(to, sender):
        rows = slope_all.at[sender, pl.ds(0, cut)]
        return top_copy(rows, rows, send_front, recv_front, to, sender)

    def copy_back(to, sender):
        rows = slope_all.at[sender, pl.ds(cut, cot_all.shape[1] - cut)]
        return top_copy(rows, rows, send_slope, recv_slope, to, sender)

    top_aim = pltpu.make_async_remote_copy(
        src_ref=cot_all.at[me],
        dst_ref=aim_top.at[0],
        send_sem=send_top.at[0],
        recv_sem=recv_top.at[0],
        device_id={"phase": aid, "dp": me},
        device_id_type=MESH,
    )

    def others(body):
        @pl.loop(0, replicas)
        def _(other):
            @pl.when(other != me)
            def _():
                body(other)

    def group_of(layer):
        owners = parts[layer].shape[0]
        return owners, lax.div(me, owners), lax.rem(me, owners)

    def near_copy(layer, w, sender):
        owners, group, _ = group_of(layer)
        return pltpu.make_async_remote_copy(
            src_ref=parts[layer].at[w],
            dst_ref=nears[layer].at[sender],
            send_sem=send_near.at[w],
            recv_sem=recv_near.at[sender],
            device_id={"phase": phase, "dp": group * owners + w},
            device_id_type=MESH,
        )

    def far_copy(layer, group):
        return pltpu.make_async_remote_copy(
            src_ref=sums_of[layer].at[0],
            dst_ref=gots[layer].at[group],
            send_sem=send_part.at[0],
            recv_sem=recv_part.at[group],
            device_id={"phase": phase, "dp": group_of(layer)[2]},
            device_id_type=MESH,
        )

    @pl.when(phase == top)
    def _():
        cot_all[me] = target(top)

    @pl.when(phase == mid)
    def _():
        aim_mid[0] = target(mid)

    aim_copy = pltpu.make_async_remote_copy(
        src_ref=aim_mid.at[0],
        dst_ref=aim_mid.at[1],
        send_sem=send_aim.at[0],
        recv_sem=recv_aim.at[0],
        device_id={"phase": helper, "dp": me},
        device_id_type=MESH,
    )

    def mid_near(w, sender):
        _, group, _ = group_of(mid)
        return pltpu.make_async_remote_copy(
            src_ref=part2.at[w],
            dst_ref=near2.at[sender],
            send_sem=send_mid.at[w],
            recv_sem=recv_mid.at[sender],
            device_id={"phase": phase, "dp": group * mid_owners + w},
            device_id_type=MESH,
        )

    def mid_far(got, recv_sem, group):
        return pltpu.make_async_remote_copy(
            src_ref=sum2.at[0],
            dst_ref=got.at[group],
            send_sem=send_far.at[0],
            recv_sem=recv_sem.at[group],
            device_id={"phase": mid, "dp": group_of(mid)[2]},
            device_id_type=MESH,
        )

    def mid_direct(w, sender):
        return pltpu.make_async_remote_copy(
            src_ref=part2.at[w],
            dst_ref=got2.at[sender],
            send_sem=send_mid.at[w],
            recv_sem=recv_mid.at[sender],
            device_id={"phase": mid, "dp": w},
            device_id_type=MESH,
        )

    def mid_start(term, helping):
        rows_here = part2.shape[1]
        member = group_of(mid)[2]
        for w in range(mid_owners):
            part2[w] = term[w * rows_here : (w + 1) * rows_here].astype(part2.dtype)
        for w in range(mid_owners):
            if helping:

                @pl.when(member != w)
                def _():
                    mid_near(w, member).start()
            else:

                @pl.when(me != w)
                def _():
                    mid_direct(w, me).start()

    def mid_pass():
        @pl.when(phase == helper)
        def _():
            _, group, member = group_of(mid)
            near2[member] = part2[member]
            for w in range(mid_owners):

                @pl.when(member != w)
                def _():
                    mid_near(w, member).wait_send()
                    mid_near(w, w).wait_recv()

            term = near2[0].astype(F32)
            for w in range(1, mid_owners):
                term = term + near2[w].astype(F32)
            sum2[0] = term.astype(near2.dtype)

            mid_far(got_help, recv_help, group).start()

    def top_cols(normed, active):
        both = jnp.concatenate([normed.astype(F32).T, active.astype(F32).T], axis=1).astype(cols_send.dtype)
        rows_here = cols_send.shape[1]
        for d in range(replicas):
            cols_send[d] = both[d * rows_here : (d + 1) * rows_here]

    for i in (2, 3, 4, 5, 6, 7, 8, 1):
        load(i).wait()
    idx[...] = jnp.full(idx.shape, -1.0, F32)
    base = []
    position = 0
    for layer in range(4):
        rows = heights[layer]
        base.append(position)
        pieces = [(at, min(LANES, rows - at)) for at in range(0, rows, LANES)]
        for k in range(TAPS):
            for piece, (at, span) in enumerate(pieces):
                idx_raw[piece, 2 * k : 2 * k + 2, 0:span] = kms[layer][k, :, at : at + span].astype(F32)
        for m in range(micro):
            at = position + m * rows
            values = jnp.concatenate(
                [
                    idx_raw.at[piece][pl.ds(m, TAPS, stride=2), :][:, :span]
                    for piece, (_, span) in enumerate(pieces)
                ],
                axis=1,
            )
            shift = m * rows if layer >= 2 else 0
            if shift:
                values = jnp.where(values < 0.0, values, values + float(shift))
            idx[0:TAPS, at : at + rows] = values
            if layer < 3:
                idx[TAPS : TAPS + 1, at : at + rows] = pms[layer][m : m + 1, :].astype(F32)
        position += micro * rows
    for j in range(idx.shape[1] // LANES):
        lanes = slice(j * LANES, (j + 1) * LANES)
        idx_t[lanes, :] = idx[:, lanes].T

    live = []
    for m in range(micro):
        block = unpack(pack_f, 0, m)
        site = lax.broadcasted_iota(jnp.int32, block.shape, 0)
        live.append(jnp.where(site < counts[:, m : m + 1], block, 0.0))
    x = jnp.concatenate(live, axis=0).astype(BF16)

    def pass_on(layer):
        part, near = parts[layer], nears[layer]

        @pl.when(phase == layer)
        def _():
            owners, group, member = group_of(layer)
            near[member] = part[member]
            for w in range(owners):

                @pl.when(member != w)
                def _():
                    near_copy(layer, w, member).wait_send()
                    near_copy(layer, w, w).wait_recv()

            for i in range(2):
                term = near[0, i].astype(F32)
                for w in range(1, owners):
                    term = term + near[w, i].astype(F32)
                sums_of[layer][0, i] = term.astype(near.dtype)

            @pl.when(group != 0)
            def _():
                far_copy(layer, group).start()

    @pl.when(phase == top)
    def _():
        pl.semaphore_wait(barrier, replicas)
        top_aim.start()
        others(lambda to: copy_cot(to, me).start())

    def bent(inner, bend, squared):
        return 0.5 * (1.0 + bend) + 0.5 * inner * (1.0 - bend * bend) * GELU_A * (
            1.0 + 3.0 * GELU_B * squared
        )

    encodes = []
    for layer in range(4):
        for i in (9 + layer, 13 + layer, 17 + layer) + ((21 + layer,) if layer < 3 else ()):
            load(i).wait()
        rows, width = heights[layer], widths[layer]
        group = rows if layer < 2 else micro * rows
        mixes = []
        for start in range(0, micro * rows, group):
            block = x[start : start + group]
            index = idx_t[base[layer] + start : base[layer] + start + group, :]
            mixed = jnp.zeros((group, width), F32)
            for first in range(0, TAPS, BATCH):
                hots = [one_hot(index[:, k : k + 1], group) for k in range(first, first + BATCH)]
                gathered = dot(jnp.concatenate(hots, axis=0), block)
                for k in range(BATCH):
                    tap = dws[layer][first + k : first + k + 1, :].astype(F32)
                    mixed = mixed + gathered[k * group : (k + 1) * group] * tap
            mixes.append(mixed)
        mixed = mixes[0] if len(mixes) == 1 else jnp.concatenate(mixes, axis=0)
        normed_f = mixed * lax.rsqrt(jnp.mean(mixed * mixed, axis=1, keepdims=True) + 1e-05)
        normed = normed_f.astype(BF16)
        inner = dot(normed, fws[layer][...])
        squared = inner * inner
        bend = jnp.tanh(GELU_A * inner * (1.0 + GELU_B * squared))
        active = (0.5 * inner * (1.0 + bend)).astype(BF16)
        encoded = (x.astype(F32) + dot(active, sws[layer][...])).astype(BF16)
        encodes.append(encoded)
        if layer == 0:
            for which, count in ((helper, replicas), (mid, replicas), (aid, 2 * replicas - 2)):

                @pl.when(phase == which)
                def _():
                    pl.semaphore_wait(barrier, count)

            @pl.when(phase == mid)
            def _():
                aim_copy.start()

        @pl.when(phase == layer)
        def _():
            aim = target(layer) if layer < mid else (aim_mid[0] if layer == mid else cot_all[me])
            backward = dot_nt(aim, sws[layer][...])
            slope = (bent(inner, bend, squared) * backward).astype(BF16)
            if layer == top:
                slope_all[me] = slope
                others(lambda to: copy_back(to, me).start())
                top_cols(normed, active)
                cols_all[me] = cols_send[me]
            elif layer == mid:
                mid_start(dot_tn(normed, slope), False)
            else:
                part = parts[layer]
                owners, _, rows_here, _ = part.shape
                for i, term in enumerate((dot_tn(normed, slope), dot_tn(active, aim))):
                    for w in range(owners):
                        part[w, i] = term[w * rows_here : (w + 1) * rows_here].astype(part.dtype)
                for w in range(owners):

                    @pl.when(group_of(layer)[2] != w)
                    def _():
                        near_copy(layer, w, group_of(layer)[2]).start()

        if layer == mid:

            @pl.when(phase == helper)
            def _():
                aim_copy.wait_recv()
                mid_start(dot_tn(active, aim_mid[1]), True)

        if layer == top:
            mid_pass()

            @pl.when(phase == aid)
            def _():
                top_cols(normed, active)
                others(lambda to: copy_cols(to, me).start())
                top_aim.wait_recv()
                backward = dot_nt(aim_top[0, 0:cut], sws[layer][...])
                front = bent(inner[0:cut], bend[0:cut], squared[0:cut]) * backward
                slope_all[me, 0:cut] = front.astype(BF16)
                others(lambda to: copy_front(to, me).start())

        elif layer > 0:
            pass_on(layer - 1)

        if layer < 3:
            coarse = heights[layer + 1]
            pooled = []
            for m in range(micro):
                matrix = pool_matrix(pms[layer][m : m + 1, :], coarse)
                number = jnp.sum(matrix, axis=1, keepdims=True)
                sums = dot(matrix.astype(BF16), encoded[m * rows : (m + 1) * rows])
                pooled.append(sums / jnp.maximum(number, 1.0))
            x = dot(jnp.concatenate(pooled, axis=0).astype(BF16), cos[layer][...]).astype(BF16)

    decoded = encodes[3]
    for layer in range(3, -1, -1):
        rows, width = heights[layer], widths[layer]
        if layer < 3:
            coarse = heights[layer + 1]
            load(24 + layer).wait()
            mix = dot_nt if layer == 0 else dot
            lifted = mix(decoded, res[layer][...]).astype(BF16)
            ups = []
            for m in range(micro):
                at = base[layer] + m * rows
                matrix = one_hot(idx_t[at : at + rows, TAPS : TAPS + 1], coarse)
                ups.append(dot(matrix, lifted[m * coarse : (m + 1) * coarse]))
            decoded = (encodes[layer].astype(F32) + jnp.concatenate(ups, axis=0)).astype(BF16)

        @pl.when(phase == layer)
        def _():
            wide = decoded.astype(F32)
            for m in range(micro):
                own = wide[m * rows : (m + 1) * rows]
                if width < LANES:
                    small[...] = own
                    pack_d[pl.ds(m, rows // 2, stride=2), :] = jnp.concatenate(
                        [
                            small[pl.ds(0, rows // 2, stride=2), :],
                            small[pl.ds(1, rows // 2, stride=2), :],
                        ],
                        axis=1,
                    )
                else:
                    split = width // LANES
                    for h in range(split):
                        pack_d[pl.ds(2 * h + m, rows, stride=2 * split), :] = own[
                            :, h * LANES : (h + 1) * LANES
                        ]

    for j in range(chunks):
        dec_out[0, :, j * LANES : (j + 1) * LANES] = pack_d[2 * j : 2 * j + 2, :].astype(BF16)

    pack_g[...] = jnp.zeros(pack_g.shape, F32)

    def put_grad(layer, i, term):
        rows_here, width = term.shape
        term = term * (micro * replicas * heights[layer]) ** -0.5
        if width < LANES:
            small[0:rows_here, :] = term
            pack_g[pl.ds(i, rows_here // 2, stride=2), :] = jnp.concatenate(
                [
                    small[pl.ds(0, rows_here // 2, stride=2), :],
                    small[pl.ds(1, rows_here // 2, stride=2), :],
                ],
                axis=1,
            )
        else:
            split = width // LANES
            for h in range(split):
                pack_g[pl.ds(2 * h + i, rows_here, stride=2 * split), :] = term[
                    :, h * LANES : (h + 1) * LANES
                ]

    @pl.when(phase == aid)
    def _():
        @others
        def _(to):
            copy_cols(to, me).wait_send()
            copy_front(to, me).wait_send()

    @pl.when(phase == helper)
    def _():
        mid_far(got_help, recv_help, 0).wait_send()

    @pl.when(phase == mid)
    def _():
        aim_copy.wait_send()

        for w in range(mid_owners):

            @pl.when(me != w)
            def _():
                mid_direct(w, me).wait_send()

        @pl.when(me < mid_owners)
        def _():
            got2[me] = part2[me]

            def received(sender):
                @pl.when(sender != me)
                def _():
                    mid_direct(0, sender).wait_recv()

                return got2[sender].astype(F32)

            total = received(0)
            if replicas <= 16:
                for sender in range(1, replicas):
                    total = total + received(sender)
            else:
                total = lax.fori_loop(1, replicas, lambda s, t: t + received(s), total)
            put_grad(mid, 0, total)
            for sender in range(mid_groups):
                mid_far(got_help, recv_help, sender).wait_recv()
            term = got_help[0].astype(F32)
            for sender in range(1, mid_groups):
                term = term + got_help[sender].astype(F32)
            put_grad(mid, 1, term)

    for layer in range(2):
        got = gots[layer]

        @pl.when(phase == layer)
        def _():
            owners, group, _ = group_of(layer)
            groups = replicas // owners

            @pl.when(group != 0)
            def _():
                far_copy(layer, group).wait_send()

            @pl.when(group == 0)
            def _():
                got[0] = sums_of[layer][0]
                for sender in range(1, groups):
                    far_copy(layer, sender).wait_recv()
                for i in range(2):
                    term = got[0, i].astype(F32)
                    for sender in range(1, groups):
                        term = term + got[sender, i].astype(F32)
                    put_grad(layer, i, term)

    @pl.when(phase == top)
    def _():
        span = micro * heights[top]

        def terms(sender):
            @pl.when(sender != me)
            def _():
                copy_cot(me, sender).wait_recv()
                copy_cols(me, sender).wait_recv()
                copy_front(me, sender).wait_recv()
                copy_back(me, sender).wait_recv()

            cols = cols_all[sender].astype(BF16)
            return (
                dot(cols[:, :span], slope_all[sender]),
                dot(cols[:, span:], cot_all[sender]),
            )

        total = terms(0)
        if replicas <= 16:
            for sender in range(1, replicas):
                total = jax.tree.map(jnp.add, total, terms(sender))
        else:
            total = lax.fori_loop(
                1, replicas, lambda s, t: jax.tree.map(jnp.add, t, terms(s)), total
            )
        for i in range(2):
            put_grad(top, i, total[i])

        @others
        def _(to):
            copy_cot(to, me).wait_send()
            copy_back(to, me).wait_send()

        top_aim.wait_send()


    for q in range(grad_out.shape[2] // LANES):
        grad_out[0, :, q * LANES : (q + 1) * LANES] = pack_g[2 * q : 2 * q + 2, :]


def deliver(dec_in, grad_in, dec_out, grad_out, sem):
    copies = [
        pltpu.make_async_copy(grad_in, grad_out, sem.at[0]),
        pltpu.make_async_copy(dec_in, dec_out, sem.at[1]),
    ]
    for copy in copies:
        copy.start()
    for copy in copies:
        copy.wait()


def on_device(*arrays):
    features, kms, dws = arrays[0], arrays[2:6], arrays[9:13]
    arrays = list(arrays)
    arrays[1] = arrays[1].T
    arrays[2:6] = [jnp.transpose(km, (1, 0, 2)) for km in kms]
    arrays[24] = arrays[24].T
    widths = [taps.shape[1] for taps in dws]
    heights = [km.shape[2] for km in kms]
    micro, elements = features.shape
    replicas = lax.axis_size("dp")
    owned = widths[3] * widths[3] // replicas

    def narrow(rows):
        return BF16 if rows % 16 == 0 else F32

    parts, gots, nears, sums_of = [], [], [], []
    for layer in range(3):
        rows_here = min(widths[layer], owned // widths[layer])
        owners = widths[layer] // rows_here
        kind = narrow(rows_here)
        if layer == 2:
            shape = (rows_here, widths[2])
            for held, first in ((parts, owners), (gots, replicas), (nears, owners), (sums_of, 1)):
                held.append(pltpu.VMEM((first, *shape), kind))
            break
        parts.append(pltpu.VMEM((owners, 2, rows_here, widths[layer]), kind))
        gots.append(pltpu.VMEM((replicas // owners, 2, rows_here, widths[layer]), kind))
        nears.append(pltpu.VMEM((owners, 2, rows_here, widths[layer]), kind))
        sums_of.append(pltpu.VMEM((1, 2, rows_here, widths[layer]), kind))
    top_rows = owned // widths[3]
    span = micro * heights[3]
    idx_lanes = -(-micro * sum(heights) // LANES) * LANES
    sem = pltpu.SemaphoreType.DMA((replicas,))
    scratch = [
        *[pltpu.VMEM(a.shape, a.dtype) for a in arrays],
        pltpu.SemaphoreType.DMA((len(arrays),)),
        pltpu.VMEM((2 * elements // LANES, LANES), F32),
        pltpu.VMEM((2 * elements // LANES, LANES), F32),
        pltpu.VMEM((2 * elements // LANES, LANES), F32),
        pltpu.VMEM((2 * owned // LANES, LANES), F32),
        pltpu.VMEM((heights[0], widths[0]), F32),
        pltpu.VMEM((-(-heights[0] // LANES), 2 * IDX_ROWS, LANES), F32),
        pltpu.VMEM((IDX_ROWS, idx_lanes), F32),
        pltpu.VMEM((idx_lanes, IDX_ROWS), F32),
        *parts,
        *gots,
        *nears,
        *sums_of,
        pltpu.VMEM((replicas, span, widths[3]), BF16),
        pltpu.VMEM((replicas, span, widths[3]), BF16),
        pltpu.VMEM((replicas, top_rows, 2 * span), narrow(top_rows)),
        pltpu.VMEM((replicas, top_rows, 2 * span), narrow(top_rows)),
        *[sem] * 10,
        pltpu.VMEM((2, micro * heights[2], widths[2]), BF16),
        gots[2],
        *[sem] * 6,
        pltpu.VMEM((1, span, widths[3]), BF16),
        *[sem] * 4,
    ]
    held = pl.pallas_call(
        functools.partial(kernel, replicas, heights, widths, micro, len(arrays)),
        out_shape=(
            pltpu.VMEM((1, micro, elements), BF16),
            pltpu.VMEM((1, 2, owned), F32),
        ),
        in_specs=[pl.BlockSpec(memory_space=pltpu.HBM)] * len(arrays),
        out_specs=[pl.BlockSpec(memory_space=pltpu.VMEM)] * 2,
        scratch_shapes=scratch,
        compiler_params=pltpu.CompilerParams(
            collective_id=0, has_side_effects=True, vmem_limit_bytes=64 * 1024 * 1024 - 512 * 1024
        ),
    )(*arrays)
    return pl.pallas_call(
        deliver,
        out_shape=(
            jax.ShapeDtypeStruct((1, micro, elements), BF16),
            jax.ShapeDtypeStruct((1, 2, owned), F32),
        ),
        in_specs=[pl.BlockSpec(memory_space=pltpu.VMEM)] * 2,
        out_specs=[pl.BlockSpec(memory_space=pltpu.HBM)] * 2,
        scratch_shapes=[pltpu.SemaphoreType.DMA((2,))],
        compiler_params=pltpu.CompilerParams(vmem_limit_bytes=1024 * 1024),
    )(*[pltpu.with_memory_space_constraint(a, pltpu.VMEM) for a in held])


def solution(mesh):
    placed = (
        (P(None, "dp"), P(None, "dp"))
        + (P(None, None, "dp"),) * 4
        + (P(None, "dp"),) * 3
        + (P(),) * 18
        + (P("phase", None, "dp"),)
    )
    return jax.shard_map(
        on_device,
        mesh=mesh,
        in_specs=placed,
        out_specs=(P("phase", None, "dp"), P("phase", None, "dp")),
        check_vma=False,
    )
```

```python
import functools
import math

import jax
import jax.numpy as jnp
from jax import lax
from jax.experimental import pallas as pl
from jax.experimental.pallas import tpu as pltpu
from jax.sharding import PartitionSpec as P

LANES = 128
TAPS = 27
IDX_ROWS = 32
BATCH = 9
F32 = jnp.float32
BF16 = jnp.bfloat16
MESH = pl.DeviceIdType.MESH
GELU_A = math.sqrt(2.0 / math.pi)
GELU_B = 0.044715


def dot(a, b):
    return lax.dot_general(a, b, (((1,), (0,)), ((), ())), preferred_element_type=F32)


def dot_nt(a, b):
    return lax.dot_general(a, b, (((1,), (1,)), ((), ())), preferred_element_type=F32)


def dot_tn(a, b):
    return lax.dot_general(a, b, (((0,), (0,)), ((), ())), preferred_element_type=F32)


def one_hot(column, width):
    lanes = lax.broadcasted_iota(jnp.int32, (column.shape[0], width), 1).astype(F32).astype(BF16)
    wide = jnp.broadcast_to(column, lanes.shape).astype(BF16)
    return jnp.where(wide == lanes, jnp.ones_like(lanes), jnp.zeros_like(lanes))


def pool_matrix(parent_row, coarse):
    rows = lax.broadcasted_iota(jnp.int32, (coarse, parent_row.shape[1]), 0)
    return jnp.where(rows == parent_row, 1.0, 0.0).astype(F32)


def kernel(replicas, heights, widths, micro, count, *refs):
    sources, (dec_out, grad_out) = refs[:count], refs[count : count + 2]
    held, refs = refs[count + 2 : 2 * count + 2], refs[2 * count + 2 :]
    (
        load_sem,
        pack_f,
        pack_c,
        pack_d,
        pack_g,
        small,
        idx_raw,
        idx,
        idx_t,
        part0,
        part1,
        part2,
        got0,
        got1,
        got2,
        near0,
        near1,
        near2,
        sum0,
        sum1,
        sum2,
        cot_all,
        slope_all,
        cols_send,
        cols_all,
        send_part,
        recv_part,
        send_cot,
        recv_cot,
        send_slope,
        recv_slope,
        send_cols,
        recv_cols,
        send_near,
        recv_near,
        aim_mid,
        got_help,
        send_aim,
        recv_aim,
        send_mid,
        recv_mid,
        send_far,
        recv_help,
        aim_top,
        send_top,
        recv_top,
        send_front,
        recv_front,
    ) = refs
    nears, sums_of = (near0, near1, near2), (sum0, sum1, sum2)
    features, counts, cot = held[0], held[1], held[27]
    kms, pms, dws = held[2:6], held[6:9], held[9:13]
    fws, sws = held[13:17], held[17:21]
    cos, res = held[21:24], held[24:27]
    parts, gots = (part0, part1, part2), (got0, got1, got2)
    phase = lax.axis_index("phase")
    me = lax.axis_index("dp")
    chunks = features.shape[1] // LANES

    def peer(offset):
        return {"phase": phase, "dp": lax.rem(me + offset, replicas)}

    def load(i):
        return pltpu.make_async_copy(sources[i], held[i], load_sem.at[i])

    order = [0, 27, 2, 3, 4, 5, 6, 7, 8, 1, 9, 13, 17, 21, 10, 14, 18, 22, 11, 15, 19, 23, 12, 16, 20]
    for i in order + [26, 25, 24]:
        load(i).start()

    mid, helper, aid = 2, 0, 1
    cut = cot_all.shape[1] // 4
    barrier = pltpu.get_barrier_semaphore()

    @pl.loop(1, replicas)
    def _(offset):
        pl.semaphore_signal(barrier, inc=1, device_id=peer(offset), device_id_type=MESH)

    mid_owners = part2.shape[0]
    mid_groups = replicas // mid_owners

    @pl.when(phase == helper)
    def _():
        pl.semaphore_signal(barrier, inc=1, device_id={"phase": mid, "dp": me}, device_id_type=MESH)

    @pl.when((phase == mid) & (me < mid_owners))
    def _():
        @pl.loop(0, mid_groups)
        def _(group):
            pl.semaphore_signal(
                barrier,
                inc=1,
                device_id={"phase": helper, "dp": group * mid_owners + me},
                device_id_type=MESH,
            )

    @pl.when(phase == aid)
    def _():
        pl.semaphore_signal(barrier, inc=1, device_id={"phase": 3, "dp": me}, device_id_type=MESH)

    @pl.when(phase == 3)
    def _():
        @pl.loop(1, replicas)
        def _(offset):
            pl.semaphore_signal(
                barrier,
                inc=1,
                device_id={"phase": aid, "dp": lax.rem(me + offset, replicas)},
                device_id_type=MESH,
            )

    for i in (0, 27):
        load(i).wait()

    for j in range(chunks):
        lanes = slice(j * LANES, (j + 1) * LANES)
        pack_f[2 * j : 2 * j + 2, :] = features[:, lanes].astype(F32)
        pack_c[2 * j : 2 * j + 2, :] = cot[0, :, lanes].astype(F32)

    def unpack(pack, layer, m):
        rows, width = heights[layer], widths[layer]
        if width < LANES:
            both = pack[pl.ds(m, rows // 2, stride=2), :]
            small[pl.ds(0, rows // 2, stride=2), :] = both[:, :width]
            small[pl.ds(1, rows // 2, stride=2), :] = both[:, width:]
            return small[...]
        split = width // LANES
        return jnp.concatenate(
            [pack[pl.ds(2 * h + m, rows, stride=2 * split), :] for h in range(split)], axis=1
        )

    def target(layer):
        return jnp.concatenate([unpack(pack_c, layer, m) for m in range(micro)], axis=0).astype(BF16)

    top = 3

    def top_copy(source, landing, send_sem, recv_sem, to, sender):
        return pltpu.make_async_remote_copy(
            src_ref=source,
            dst_ref=landing,
            send_sem=send_sem.at[to],
            recv_sem=recv_sem.at[sender],
            device_id={"phase": top, "dp": to},
            device_id_type=MESH,
        )

    def copy_cot(to, sender):
        return top_copy(cot_all.at[sender], cot_all.at[sender], send_cot, recv_cot, to, sender)

    def copy_cols(to, sender):
        return top_copy(cols_send.at[to], cols_all.at[sender], send_cols, recv_cols, to, sender)

    def copy_front(to, sender):
        rows = slope_all.at[sender, pl.ds(0, cut)]
        return top_copy(rows, rows, send_front, recv_front, to, sender)

    def copy_back(to, sender):
        rows = slope_all.at[sender, pl.ds(cut, cot_all.shape[1] - cut)]
        return top_copy(rows, rows, send_slope, recv_slope, to, sender)

    top_aim = pltpu.make_async_remote_copy(
        src_ref=cot_all.at[me],
        dst_ref=aim_top.at[0],
        send_sem=send_top.at[0],
        recv_sem=recv_top.at[0],
        device_id={"phase": aid, "dp": me},
        device_id_type=MESH,
    )

    def others(body):
        @pl.loop(0, replicas)
        def _(other):
            @pl.when(other != me)
            def _():
                body(other)

    def group_of(layer):
        owners = parts[layer].shape[0]
        return owners, lax.div(me, owners), lax.rem(me, owners)

    def near_copy(layer, w, sender):
        owners, group, _ = group_of(layer)
        return pltpu.make_async_remote_copy(
            src_ref=parts[layer].at[w],
            dst_ref=nears[layer].at[sender],
            send_sem=send_near.at[w],
            recv_sem=recv_near.at[sender],
            device_id={"phase": phase, "dp": group * owners + w},
            device_id_type=MESH,
        )

    def far_copy(layer, group):
        return pltpu.make_async_remote_copy(
            src_ref=sums_of[layer].at[0],
            dst_ref=gots[layer].at[group],
            send_sem=send_part.at[0],
            recv_sem=recv_part.at[group],
            device_id={"phase": phase, "dp": group_of(layer)[2]},
            device_id_type=MESH,
        )

    @pl.when(phase == top)
    def _():
        cot_all[me] = target(top)

    @pl.when(phase == mid)
    def _():
        aim_mid[0] = target(mid)

    aim_copy = pltpu.make_async_remote_copy(
        src_ref=aim_mid.at[0],
        dst_ref=aim_mid.at[1],
        send_sem=send_aim.at[0],
        recv_sem=recv_aim.at[0],
        device_id={"phase": helper, "dp": me},
        device_id_type=MESH,
    )

    def mid_near(w, sender):
        _, group, _ = group_of(mid)
        return pltpu.make_async_remote_copy(
            src_ref=part2.at[w],
            dst_ref=near2.at[sender],
            send_sem=send_mid.at[w],
            recv_sem=recv_mid.at[sender],
            device_id={"phase": phase, "dp": group * mid_owners + w},
            device_id_type=MESH,
        )

    def mid_far(got, recv_sem, group):
        return pltpu.make_async_remote_copy(
            src_ref=sum2.at[0],
            dst_ref=got.at[group],
            send_sem=send_far.at[0],
            recv_sem=recv_sem.at[group],
            device_id={"phase": mid, "dp": group_of(mid)[2]},
            device_id_type=MESH,
        )

    def mid_direct(w, sender):
        return pltpu.make_async_remote_copy(
            src_ref=part2.at[w],
            dst_ref=got2.at[sender],
            send_sem=send_mid.at[w],
            recv_sem=recv_mid.at[sender],
            device_id={"phase": mid, "dp": w},
            device_id_type=MESH,
        )

    def mid_start(term, helping):
        rows_here = part2.shape[1]
        member = group_of(mid)[2]
        for w in range(mid_owners):
            part2[w] = term[w * rows_here : (w + 1) * rows_here].astype(part2.dtype)
        for w in range(mid_owners):
            if helping:

                @pl.when(member != w)
                def _():
                    mid_near(w, member).start()
            else:

                @pl.when(me != w)
                def _():
                    mid_direct(w, me).start()

    def mid_pass():
        @pl.when(phase == helper)
        def _():
            _, group, member = group_of(mid)
            near2[member] = part2[member]
            for w in range(mid_owners):

                @pl.when(member != w)
                def _():
                    mid_near(w, member).wait_send()
                    mid_near(w, w).wait_recv()

            term = near2[0].astype(F32)
            for w in range(1, mid_owners):
                term = term + near2[w].astype(F32)
            sum2[0] = term.astype(near2.dtype)

            mid_far(got_help, recv_help, group).start()

    def top_cols(normed, active):
        both = jnp.concatenate([normed.astype(F32).T, active.astype(F32).T], axis=1).astype(cols_send.dtype)
        rows_here = cols_send.shape[1]
        for d in range(replicas):
            cols_send[d] = both[d * rows_here : (d + 1) * rows_here]

    for i in (2, 3, 4, 5, 6, 7, 8, 1):
        load(i).wait()
    idx[...] = jnp.full(idx.shape, -1.0, F32)
    base = []
    position = 0
    for layer in range(4):
        rows = heights[layer]
        base.append(position)
        pieces = [(at, min(LANES, rows - at)) for at in range(0, rows, LANES)]
        for k in range(TAPS):
            for piece, (at, span) in enumerate(pieces):
                idx_raw[piece, 2 * k : 2 * k + 2, 0:span] = kms[layer][k, :, at : at + span].astype(F32)
        for m in range(micro):
            at = position + m * rows
            values = jnp.concatenate(
                [
                    idx_raw.at[piece][pl.ds(m, TAPS, stride=2), :][:, :span]
                    for piece, (_, span) in enumerate(pieces)
                ],
                axis=1,
            )
            shift = m * rows if layer >= 2 else 0
            if shift:
                values = jnp.where(values < 0.0, values, values + float(shift))
            idx[0:TAPS, at : at + rows] = values
            if layer < 3:
                idx[TAPS : TAPS + 1, at : at + rows] = pms[layer][m : m + 1, :].astype(F32)
        position += micro * rows
    for j in range(idx.shape[1] // LANES):
        lanes = slice(j * LANES, (j + 1) * LANES)
        idx_t[lanes, :] = idx[:, lanes].T

    live = []
    for m in range(micro):
        block = unpack(pack_f, 0, m)
        site = lax.broadcasted_iota(jnp.int32, block.shape, 0)
        live.append(jnp.where(site < counts[:, m : m + 1], block, 0.0))
    x = jnp.concatenate(live, axis=0).astype(BF16)

    def pass_on(layer):
        part, near = parts[layer], nears[layer]

        @pl.when(phase == layer)
        def _():
            owners, group, member = group_of(layer)
            near[member] = part[member]
            for w in range(owners):

                @pl.when(member != w)
                def _():
                    near_copy(layer, w, member).wait_send()
                    near_copy(layer, w, w).wait_recv()

            for i in range(2):
                term = near[0, i].astype(F32)
                for w in range(1, owners):
                    term = term + near[w, i].astype(F32)
                sums_of[layer][0, i] = term.astype(near.dtype)

            @pl.when(group != 0)
            def _():
                far_copy(layer, group).start()

    @pl.when(phase == top)
    def _():
        pl.semaphore_wait(barrier, replicas)
        top_aim.start()
        others(lambda to: copy_cot(to, me).start())

    def bent(inner, bend, squared):
        return 0.5 * (1.0 + bend) + 0.5 * inner * (1.0 - bend * bend) * GELU_A * (
            1.0 + 3.0 * GELU_B * squared
        )

    encodes = []
    for layer in range(4):
        for i in (9 + layer, 13 + layer, 17 + layer) + ((21 + layer,) if layer < 3 else ()):
            load(i).wait()
        rows, width = heights[layer], widths[layer]
        group = rows if layer < 2 else micro * rows
        mixes = []
        for start in range(0, micro * rows, group):
            block = x[start : start + group]
            index = idx_t[base[layer] + start : base[layer] + start + group, :]
            taps = dws[layer][...]
            scaled = jnp.concatenate([block * taps[k : k + 1, :] for k in range(TAPS)], axis=0)
            hots = jnp.concatenate([one_hot(index[:, k : k + 1], group) for k in range(TAPS)], axis=1)
            mixed = dot(hots, scaled)
            mixes.append(mixed)
        mixed = mixes[0] if len(mixes) == 1 else jnp.concatenate(mixes, axis=0)
        normed_f = mixed * lax.rsqrt(jnp.mean(mixed * mixed, axis=1, keepdims=True) + 1e-05)
        normed = normed_f.astype(BF16)
        inner = dot(normed, fws[layer][...])
        squared = inner * inner
        bend = jnp.tanh(GELU_A * inner * (1.0 + GELU_B * squared))
        active = (0.5 * inner * (1.0 + bend)).astype(BF16)
        encoded = (x.astype(F32) + dot(active, sws[layer][...])).astype(BF16)
        encodes.append(encoded)
        if layer == 0:
            for which, count in ((helper, replicas), (mid, replicas), (aid, 2 * replicas - 2)):

                @pl.when(phase == which)
                def _():
                    pl.semaphore_wait(barrier, count)

            @pl.when(phase == mid)
            def _():
                aim_copy.start()

        @pl.when(phase == layer)
        def _():
            aim = target(layer) if layer < mid else (aim_mid[0] if layer == mid else cot_all[me])
            backward = dot_nt(aim, sws[layer][...])
            slope = (bent(inner, bend, squared) * backward).astype(BF16)
            if layer == top:
                slope_all[me] = slope
                others(lambda to: copy_back(to, me).start())
                top_cols(normed, active)
                cols_all[me] = cols_send[me]
            elif layer == mid:
                mid_start(dot_tn(normed, slope), False)
            else:
                part = parts[layer]
                owners, _, rows_here, _ = part.shape
                for i, term in enumerate((dot_tn(normed, slope), dot_tn(active, aim))):
                    for w in range(owners):
                        part[w, i] = term[w * rows_here : (w + 1) * rows_here].astype(part.dtype)
                for w in range(owners):

                    @pl.when(group_of(layer)[2] != w)
                    def _():
                        near_copy(layer, w, group_of(layer)[2]).start()

        if layer == mid:

            @pl.when(phase == helper)
            def _():
                aim_copy.wait_recv()
                mid_start(dot_tn(active, aim_mid[1]), True)

        if layer == top:
            mid_pass()

            @pl.when(phase == aid)
            def _():
                top_cols(normed, active)
                others(lambda to: copy_cols(to, me).start())
                top_aim.wait_recv()
                backward = dot_nt(aim_top[0, 0:cut], sws[layer][...])
                front = bent(inner[0:cut], bend[0:cut], squared[0:cut]) * backward
                slope_all[me, 0:cut] = front.astype(BF16)
                others(lambda to: copy_front(to, me).start())

        elif layer > 0:
            pass_on(layer - 1)

        if layer < 3:
            coarse = heights[layer + 1]
            pooled = []
            for m in range(micro):
                matrix = pool_matrix(pms[layer][m : m + 1, :], coarse)
                number = jnp.sum(matrix, axis=1, keepdims=True)
                sums = dot(matrix.astype(BF16), encoded[m * rows : (m + 1) * rows])
                pooled.append(sums / jnp.maximum(number, 1.0))
            x = dot(jnp.concatenate(pooled, axis=0).astype(BF16), cos[layer][...]).astype(BF16)

    decoded = encodes[3]
    for layer in range(3, -1, -1):
        rows, width = heights[layer], widths[layer]
        if layer < 3:
            coarse = heights[layer + 1]
            load(24 + layer).wait()
            mix = dot_nt if layer == 0 else dot
            lifted = mix(decoded, res[layer][...]).astype(BF16)
            ups = []
            for m in range(micro):
                at = base[layer] + m * rows
                matrix = one_hot(idx_t[at : at + rows, TAPS : TAPS + 1], coarse)
                ups.append(dot(matrix, lifted[m * coarse : (m + 1) * coarse]))
            decoded = (encodes[layer].astype(F32) + jnp.concatenate(ups, axis=0)).astype(BF16)

        @pl.when(phase == layer)
        def _():
            wide = decoded.astype(F32)
            for m in range(micro):
                own = wide[m * rows : (m + 1) * rows]
                if width < LANES:
                    small[...] = own
                    pack_d[pl.ds(m, rows // 2, stride=2), :] = jnp.concatenate(
                        [
                            small[pl.ds(0, rows // 2, stride=2), :],
                            small[pl.ds(1, rows // 2, stride=2), :],
                        ],
                        axis=1,
                    )
                else:
                    split = width // LANES
                    for h in range(split):
                        pack_d[pl.ds(2 * h + m, rows, stride=2 * split), :] = own[
                            :, h * LANES : (h + 1) * LANES
                        ]

    for j in range(chunks):
        dec_out[0, :, j * LANES : (j + 1) * LANES] = pack_d[2 * j : 2 * j + 2, :].astype(BF16)

    pack_g[...] = jnp.zeros(pack_g.shape, F32)

    def put_grad(layer, i, term):
        rows_here, width = term.shape
        term = term * (micro * replicas * heights[layer]) ** -0.5
        if width < LANES:
            small[0:rows_here, :] = term
            pack_g[pl.ds(i, rows_here // 2, stride=2), :] = jnp.concatenate(
                [
                    small[pl.ds(0, rows_here // 2, stride=2), :],
                    small[pl.ds(1, rows_here // 2, stride=2), :],
                ],
                axis=1,
            )
        else:
            split = width // LANES
            for h in range(split):
                pack_g[pl.ds(2 * h + i, rows_here, stride=2 * split), :] = term[
                    :, h * LANES : (h + 1) * LANES
                ]

    @pl.when(phase == aid)
    def _():
        @others
        def _(to):
            copy_cols(to, me).wait_send()
            copy_front(to, me).wait_send()

    @pl.when(phase == helper)
    def _():
        mid_far(got_help, recv_help, 0).wait_send()

    @pl.when(phase == mid)
    def _():
        aim_copy.wait_send()

        for w in range(mid_owners):

            @pl.when(me != w)
            def _():
                mid_direct(w, me).wait_send()

        @pl.when(me < mid_owners)
        def _():
            got2[me] = part2[me]

            def received(sender):
                @pl.when(sender != me)
                def _():
                    mid_direct(0, sender).wait_recv()

                return got2[sender].astype(F32)

            total = received(0)
            if replicas <= 16:
                for sender in range(1, replicas):
                    total = total + received(sender)
            else:
                total = lax.fori_loop(1, replicas, lambda s, t: t + received(s), total)
            put_grad(mid, 0, total)
            for sender in range(mid_groups):
                mid_far(got_help, recv_help, sender).wait_recv()
            term = got_help[0].astype(F32)
            for sender in range(1, mid_groups):
                term = term + got_help[sender].astype(F32)
            put_grad(mid, 1, term)

    for layer in range(2):
        got = gots[layer]

        @pl.when(phase == layer)
        def _():
            owners, group, _ = group_of(layer)
            groups = replicas // owners

            @pl.when(group != 0)
            def _():
                far_copy(layer, group).wait_send()

            @pl.when(group == 0)
            def _():
                got[0] = sums_of[layer][0]
                for sender in range(1, groups):
                    far_copy(layer, sender).wait_recv()
                for i in range(2):
                    term = got[0, i].astype(F32)
                    for sender in range(1, groups):
                        term = term + got[sender, i].astype(F32)
                    put_grad(layer, i, term)

    @pl.when(phase == top)
    def _():
        span = micro * heights[top]

        def terms(sender):
            @pl.when(sender != me)
            def _():
                copy_cot(me, sender).wait_recv()
                copy_cols(me, sender).wait_recv()
                copy_front(me, sender).wait_recv()
                copy_back(me, sender).wait_recv()

            cols = cols_all[sender].astype(BF16)
            return (
                dot(cols[:, :span], slope_all[sender]),
                dot(cols[:, span:], cot_all[sender]),
            )

        total = terms(0)
        if replicas <= 16:
            for sender in range(1, replicas):
                total = jax.tree.map(jnp.add, total, terms(sender))
        else:
            total = lax.fori_loop(
                1, replicas, lambda s, t: jax.tree.map(jnp.add, t, terms(s)), total
            )
        for i in range(2):
            put_grad(top, i, total[i])

        @others
        def _(to):
            copy_cot(to, me).wait_send()
            copy_back(to, me).wait_send()

        top_aim.wait_send()


    for q in range(grad_out.shape[2] // LANES):
        grad_out[0, :, q * LANES : (q + 1) * LANES] = pack_g[2 * q : 2 * q + 2, :]


def deliver(dec_in, grad_in, dec_out, grad_out, sem):
    copies = [
        pltpu.make_async_copy(grad_in, grad_out, sem.at[0]),
        pltpu.make_async_copy(dec_in, dec_out, sem.at[1]),
    ]
    for copy in copies:
        copy.start()
    for copy in copies:
        copy.wait()


def on_device(*arrays):
    features, kms, dws = arrays[0], arrays[2:6], arrays[9:13]
    arrays = list(arrays)
    arrays[1] = arrays[1].T
    arrays[2:6] = [jnp.transpose(km, (1, 0, 2)) for km in kms]
    arrays[24] = arrays[24].T
    widths = [taps.shape[1] for taps in dws]
    heights = [km.shape[2] for km in kms]
    micro, elements = features.shape
    replicas = lax.axis_size("dp")
    owned = widths[3] * widths[3] // replicas

    def narrow(rows):
        return BF16 if rows % 16 == 0 else F32

    parts, gots, nears, sums_of = [], [], [], []
    for layer in range(3):
        rows_here = min(widths[layer], owned // widths[layer])
        owners = widths[layer] // rows_here
        kind = narrow(rows_here)
        if layer == 2:
            shape = (rows_here, widths[2])
            for held, first in ((parts, owners), (gots, replicas), (nears, owners), (sums_of, 1)):
                held.append(pltpu.VMEM((first, *shape), kind))
            break
        parts.append(pltpu.VMEM((owners, 2, rows_here, widths[layer]), kind))
        gots.append(pltpu.VMEM((replicas // owners, 2, rows_here, widths[layer]), kind))
        nears.append(pltpu.VMEM((owners, 2, rows_here, widths[layer]), kind))
        sums_of.append(pltpu.VMEM((1, 2, rows_here, widths[layer]), kind))
    top_rows = owned // widths[3]
    span = micro * heights[3]
    idx_lanes = -(-micro * sum(heights) // LANES) * LANES
    sem = pltpu.SemaphoreType.DMA((replicas,))
    scratch = [
        *[pltpu.VMEM(a.shape, a.dtype) for a in arrays],
        pltpu.SemaphoreType.DMA((len(arrays),)),
        pltpu.VMEM((2 * elements // LANES, LANES), F32),
        pltpu.VMEM((2 * elements // LANES, LANES), F32),
        pltpu.VMEM((2 * elements // LANES, LANES), F32),
        pltpu.VMEM((2 * owned // LANES, LANES), F32),
        pltpu.VMEM((heights[0], widths[0]), F32),
        pltpu.VMEM((-(-heights[0] // LANES), 2 * IDX_ROWS, LANES), F32),
        pltpu.VMEM((IDX_ROWS, idx_lanes), F32),
        pltpu.VMEM((idx_lanes, IDX_ROWS), F32),
        *parts,
        *gots,
        *nears,
        *sums_of,
        pltpu.VMEM((replicas, span, widths[3]), BF16),
        pltpu.VMEM((replicas, span, widths[3]), BF16),
        pltpu.VMEM((replicas, top_rows, 2 * span), narrow(top_rows)),
        pltpu.VMEM((replicas, top_rows, 2 * span), narrow(top_rows)),
        *[sem] * 10,
        pltpu.VMEM((2, micro * heights[2], widths[2]), BF16),
        gots[2],
        *[sem] * 6,
        pltpu.VMEM((1, span, widths[3]), BF16),
        *[sem] * 4,
    ]
    held = pl.pallas_call(
        functools.partial(kernel, replicas, heights, widths, micro, len(arrays)),
        out_shape=(
            pltpu.VMEM((1, micro, elements), BF16),
            pltpu.VMEM((1, 2, owned), F32),
        ),
        in_specs=[pl.BlockSpec(memory_space=pltpu.HBM)] * len(arrays),
        out_specs=[pl.BlockSpec(memory_space=pltpu.VMEM)] * 2,
        scratch_shapes=scratch,
        compiler_params=pltpu.CompilerParams(
            collective_id=0, has_side_effects=True, vmem_limit_bytes=64 * 1024 * 1024 - 512 * 1024
        ),
    )(*arrays)
    return pl.pallas_call(
        deliver,
        out_shape=(
            jax.ShapeDtypeStruct((1, micro, elements), BF16),
            jax.ShapeDtypeStruct((1, 2, owned), F32),
        ),
        in_specs=[pl.BlockSpec(memory_space=pltpu.VMEM)] * 2,
        out_specs=[pl.BlockSpec(memory_space=pltpu.HBM)] * 2,
        scratch_shapes=[pltpu.SemaphoreType.DMA((2,))],
        compiler_params=pltpu.CompilerParams(vmem_limit_bytes=1024 * 1024),
    )(*[pltpu.with_memory_space_constraint(a, pltpu.VMEM) for a in held])


def solution(mesh):
    placed = (
        (P(None, "dp"), P(None, "dp"))
        + (P(None, None, "dp"),) * 4
        + (P(None, "dp"),) * 3
        + (P(),) * 18
        + (P("phase", None, "dp"),)
    )
    return jax.shard_map(
        on_device,
        mesh=mesh,
        in_specs=placed,
        out_specs=(P("phase", None, "dp"), P("phase", None, "dp")),
        check_vma=False,
    )
```
